32 devices in a mesh: gz: 16 (over z, y, core), gy: 2 (over x).
Axes of the slice: x: 2, y: 2, z: 4, core: 2. Of those that a mesh axis runs over, the one named last changes fastest.
Arguments:
- measured: float32 [128, 512, 512], P('gz', 'gy'), may hold values from 0.2 to 5
- transfer_real: float32 [128, 512, 256], P('gz', 'gy'), may hold values from 0.6 to 1
- transfer_imag: float32 [128, 512, 256], P('gz', 'gy'), may hold values from -0.2 to 0.2
Outputs:
- estimate: float32 [128, 512, 512], P('gz', 'gy')
The draws below stay inside these ranges and needn't reach their ends.
All inputs are finite; a program needn't handle non-finite values.
Results may differ from the reference program's by a relative error of at most 0.0002.
Values sent between devices are 32-bit elements; how exact they have to be, the bound alone decides.
No kernel may reach another device: no remote copies, remote signals or barrier semaphores. Data moves between devices by JAX's collectives and lax.ppermute only.
A program may use at most 128 MiB of HBM per device.

```python
import math
import jax
import jax.numpy as jnp
from jax import lax

NZ = 128
NY = 512
NX = 512
ITERS = 2
RADIUS = 4
HALF = 256


def level_of(rng, dims, split, low, largest):
    loudness = 1.0
    for position, shards_of in split:
        steps = jax.random.uniform(jax.random.fold_in(jax.random.fold_in(rng, 6), position), (shards_of,), jnp.float32, low / len(split), largest / len(split))
        loudness = loudness * jnp.repeat(jnp.exp(steps), dims[position] // shards_of).reshape((-1,) + (1,) * (len(dims) - 1 - position))
    return loudness


def setup_inputs(seed: int = 0) -> dict:
    streams_of = jax.random.split(jax.random.key(seed), 4)
    measured = jnp.clip(jnp.exp(math.log(5.0) - 3.218876 * jax.random.uniform(streams_of[0], (NZ, NY, NX), jnp.float32) ** level_of(streams_of[0], (NZ, NY, NX), ((0, 16), (1, 2)), -0.2, 0.2)), 0.2, 5.0)
    transfer_real = jnp.clip(0.6 + 0.39999998 * jax.random.uniform(streams_of[1], (NZ, NY, HALF), jnp.float32) ** level_of(streams_of[1], (NZ, NY, HALF), ((0, 16), (1, 2)), -0.2, 0.2), 0.6, 1.0)
    transfer_imag = jnp.clip(jax.random.uniform(streams_of[2], (NZ, NY, HALF), jnp.float32, -0.2, 0.2) * level_of(streams_of[2], (NZ, NY, HALF), ((0, 16), (1, 2)), -0.4, 0.0), -0.2, 0.2)
    return dict(measured=measured, transfer_real=transfer_real, transfer_imag=transfer_imag)


SIGMA = 1.5
FLOOR = 0.1


def gauss_weights():
    offsets = jnp.arange(-RADIUS, RADIUS + 1).astype(jnp.float32)
    weights = jnp.exp(-offsets * offsets / (2.0 * SIGMA * SIGMA))
    return weights / jnp.sum(weights)


def taps_along(padded, axis, length):
    weights = gauss_weights()
    total = weights[0] * lax.slice_in_dim(padded, 0, length, axis=axis)
    for offset in range(1, 2 * RADIUS + 1):
        total = total + weights[offset] * lax.slice_in_dim(padded, offset, offset + length, axis=axis)
    return total


def blur_local(values, axis):
    length = values.shape[axis]
    widths = [(0, 0)] * values.ndim
    widths[axis] = (RADIUS, RADIUS)
    return taps_along(jnp.pad(values, widths), axis, length)


def reference(measured, transfer_real, transfer_imag):
    nyquist = jnp.zeros((NZ, NY, 1), transfer_real.dtype)
    transfer = lax.complex(jnp.concatenate([transfer_real, nyquist], axis=2), jnp.concatenate([transfer_imag, nyquist], axis=2))
    estimate = measured
    for iteration in range(ITERS):
        blurred = jnp.fft.irfftn(jnp.fft.rfftn(estimate) * transfer, s=(NZ, NY, NX))
        ratio = measured / jnp.maximum(blurred, FLOOR)
        correction = jnp.fft.irfftn(jnp.fft.rfftn(ratio) * jnp.conj(transfer), s=(NZ, NY, NX))
        correction = blur_local(blur_local(blur_local(correction, 2), 1), 0)
        estimate = estimate * correction
    return estimate
```

```python
import functools
import math

import jax
import jax.numpy as jnp
import numpy as np
from jax import lax
from jax.experimental import pallas as pl
from jax.experimental.pallas import tpu as pltpu
from jax.sharding import PartitionSpec as P

ITERS = 2
RADIUS = 4


SIGMA = 1.5
FLOOR = 0.1


def product(form, left, right):
    return jnp.einsum(
        form, left, right, precision=lax.Precision.HIGHEST, preferred_element_type=jnp.float32
    )


def gauss_weights():
    offsets = jnp.arange(-RADIUS, RADIUS + 1).astype(jnp.float32)
    weights = jnp.exp(-offsets * offsets / (2.0 * SIGMA * SIGMA))
    return weights / jnp.sum(weights)


def taps_along(padded, axis, length):
    weights = gauss_weights()
    total = weights[0] * lax.slice_in_dim(padded, 0, length, axis=axis)
    for offset in range(1, 2 * RADIUS + 1):
        total = total + weights[offset] * lax.slice_in_dim(
            padded, offset, offset + length, axis=axis
        )
    return total


def blur_local(values, axis):
    length = values.shape[axis]
    widths = [(0, 0)] * values.ndim
    widths[axis] = (RADIUS, RADIUS)
    return taps_along(jnp.pad(values, widths), axis, length)


def angles(length, count):
    position = jnp.arange(length, dtype=jnp.int32)
    frequency = jnp.arange(count, dtype=jnp.int32)
    phase = position[:, None] * frequency[None, :] % length
    return phase.astype(jnp.float32) * (2.0 * math.pi / length)


def square_tables(length):
    angle = angles(length, length)
    cosine = jnp.cos(angle)
    sine = jnp.sin(angle)
    return ((cosine, sine), (cosine / length, sine / length))


def half_tables(length):
    half = length // 2
    angle = angles(length, half)
    cosine = jnp.cos(angle)
    sine = jnp.sin(angle)
    ahead = jnp.stack((cosine, -sine), axis=1)
    weight = jnp.where(jnp.arange(half) == 0, 1.0, 2.0).astype(jnp.float32) / length
    behind = jnp.stack((weight[:, None] * cosine.T, -weight[:, None] * sine.T), axis=0)
    return (ahead, behind)


def shaped(table, shape):
    return (table[0].reshape(shape), table[1].reshape(shape))


def turn(form, values, table, forward):
    first = product(form, values, table[0])
    second = product(form, values, table[1])
    if forward:
        return jnp.stack(
            (first[..., 0, :] + second[..., 1, :], first[..., 1, :] - second[..., 0, :]), axis=-2
        )
    return jnp.stack(
        (first[..., 0, :] - second[..., 1, :], first[..., 1, :] + second[..., 0, :]), axis=-2
    )


def across_z(values):
    return lax.all_to_all(values, "gz", split_axis=0, concat_axis=0, tiled=True)


def across_y(values):
    return lax.all_to_all(values, "gy", split_axis=0, concat_axis=0, tiled=True)


def forward_zfirst(field, ahead, y_fwd, z_fwd):
    z_local, y_local, x_len = field.shape
    z_devs = lax.axis_size("gz")
    y_devs = lax.axis_size("gy")
    x_share = ahead.shape[2] // z_devs
    z_len = z_local * z_devs
    y_len = y_local * y_devs
    z_share = z_len // y_devs
    values = product("zyx,xrgq->gzyrq", field, ahead.reshape(x_len, 2, z_devs, x_share))
    values = across_z(values).reshape(z_len, y_local, 2, x_share)
    values = turn("zyrq,zgk->gykrq", values, shaped(z_fwd, (z_len, y_devs, z_share)), True)
    values = across_y(values).reshape(y_len, z_share, 2, x_share)
    return turn("yjrq,yk->kjrq", values, y_fwd, True)


def inverse_zfirst(spectrum, behind, y_back, z_back, z_local, y_local):
    z_devs = lax.axis_size("gz")
    y_devs = lax.axis_size("gy")
    y_len, z_share, pair, x_share = spectrum.shape
    x_len = behind.shape[2]
    values = turn("kjrq,kgy->gyjrq", spectrum, shaped(y_back, (y_len, y_devs, y_local)), False)
    values = across_y(values)
    values = turn(
        "syjrq,sjgz->gzyrq", values, shaped(z_back, (y_devs, z_share, z_devs, z_local)), False
    )
    values = across_z(values)
    return product("szyrq,rsqx->zyx", values, behind.reshape(2, z_devs, x_share, x_len))


def gains_zfirst(transfer_real, transfer_imag):
    z_local, y_local, half = transfer_real.shape
    z_devs = lax.axis_size("gz")
    y_devs = lax.axis_size("gy")
    x_share = half // z_devs
    z_len = z_local * z_devs
    z_share = z_len // y_devs
    stacked = (
        jnp.stack((transfer_real, transfer_imag), axis=2)
        .reshape(z_local, y_local, 2, z_devs, x_share)
        .transpose(3, 0, 1, 2, 4)
    )
    stacked = (
        across_z(stacked).reshape(y_devs, z_share, y_local, 2, x_share).transpose(0, 2, 1, 3, 4)
    )
    return across_y(stacked).reshape(y_local * y_devs, z_share, 2, x_share)


def apply_gains(spectrum, gains, conjugate):
    spec_real = spectrum[..., 0, :]
    spec_imag = spectrum[..., 1, :]
    gain_real = gains[..., 0, :]
    gain_imag = gains[..., 1, :]
    if conjugate:
        return jnp.stack(
            (
                spec_real * gain_real + spec_imag * gain_imag,
                spec_imag * gain_real - spec_real * gain_imag,
            ),
            axis=-2,
        )
    return jnp.stack(
        (
            spec_real * gain_real - spec_imag * gain_imag,
            spec_real * gain_imag + spec_imag * gain_real,
        ),
        axis=-2,
    )


def on_device_rows(measured, transfer_real, transfer_imag):
    z_local, y_local, x_len = measured.shape
    z_len = z_local * lax.axis_size("gz")
    y_len = y_local * lax.axis_size("gy")
    ahead, behind = half_tables(x_len)
    y_fwd, y_back = square_tables(y_len)
    z_fwd, z_back = square_tables(z_len)
    soft_x = blur_local(behind, 2)
    soft_y = (blur_local(y_back[0], 1), blur_local(y_back[1], 1))
    soft_z = (blur_local(z_back[0], 1), blur_local(z_back[1], 1))
    gains = gains_zfirst(transfer_real, transfer_imag)
    estimate = measured
    for iteration in range(ITERS):
        spectrum = forward_zfirst(estimate, ahead, y_fwd, z_fwd)
        blurred = inverse_zfirst(
            apply_gains(spectrum, gains, False), behind, y_back, z_back, z_local, y_local
        )
        ratio = measured / jnp.maximum(blurred, FLOOR)
        spectrum = forward_zfirst(ratio, ahead, y_fwd, z_fwd)
        correction = inverse_zfirst(
            apply_gains(spectrum, gains, True), soft_x, soft_y, soft_z, z_local, y_local
        )
        estimate = estimate * correction
    return estimate


LANES = 128
SUBLANES = 8


def gauss_weights_np():
    offsets = np.arange(-RADIUS, RADIUS + 1).astype(np.float64)
    weights = np.exp(-offsets * offsets / (2.0 * SIGMA * SIGMA))
    return weights / weights.sum()


def smooth_np(table, axis):
    weights = gauss_weights_np()
    widths = [(0, 0)] * table.ndim
    widths[axis] = (RADIUS, RADIUS)
    padded = np.pad(table, widths)
    length = table.shape[axis]
    return sum(
        weights[j] * np.take(padded, np.arange(j, j + length), axis=axis)
        for j in range(2 * RADIUS + 1)
    )


def two_terms(table):
    high = table.astype(np.float32).astype(jnp.bfloat16)
    low = (table - high.astype(np.float64)).astype(np.float32).astype(jnp.bfloat16)
    return np.stack((high, low))


def phase_np(first, second, length):
    return 2.0 * np.pi * ((first[:, None] * second[None, :]) % length) / length


def x_tables(length):
    half = length // 2
    where = np.arange(length)
    ahead, behind = [], []
    for odd in range(2):
        k = 2 * np.arange(half // 2) + odd
        angle = phase_np(where, k, length)
        ahead.append(np.concatenate((np.cos(angle), -np.sin(angle)), axis=1)[:half])
        weight = (np.where(k == 0, 1.0, 2.0) / length)[:, None]
        behind.append(np.concatenate((weight * np.cos(angle).T, -weight * np.sin(angle).T), axis=0))
    sharp = np.stack([table[:, :half] for table in behind])
    soft = smooth_np(np.concatenate(behind, axis=0), 1)
    return two_terms(np.stack(ahead)), two_terms(sharp), two_terms(soft)


def y_tables(length):
    half = length // 2
    where = np.arange(length)
    ahead, sharp, soft = [], [], []
    for odd in range(2):
        k = 2 * np.arange(half) + odd
        angle = phase_np(k, where, length)
        cosine, sine = np.cos(angle), np.sin(angle)
        ahead.append(np.concatenate((cosine[:, :half], sine[:, :half]), axis=0))
        cosine, sine = cosine.T / length, sine.T / length
        sharp.append(np.concatenate((cosine[:half], sine[:half]), axis=0))
        soft.append(np.concatenate((smooth_np(cosine, 0), smooth_np(sine, 0)), axis=0))
    return two_terms(np.stack(ahead)), two_terms(np.stack(sharp)), two_terms(np.stack(soft))


def z_tables(length):
    where = np.arange(length)
    angle = phase_np(where, where, length)
    cosine, sine = np.cos(angle), np.sin(angle)
    ahead = np.block([[cosine, sine], [-sine, cosine]])
    cosine, sine = cosine / length, sine / length
    sharp = np.block([[cosine, -sine], [sine, cosine]])
    cosine, sine = smooth_np(cosine, 0), smooth_np(sine, 0)
    soft = np.block([[cosine, -sine], [sine, cosine]])
    return two_terms(ahead), two_terms(sharp), two_terms(soft)


def dot(left, right):
    return jnp.dot(left, right, preferred_element_type=jnp.float32)


def split_terms(values):
    high = values.astype(jnp.bfloat16)
    return high, (values - high.astype(jnp.float32)).astype(jnp.bfloat16)


def table_times(high, low, values):
    first, second = split_terms(values)
    return dot(high, first) + dot(high, second) + dot(low, first)


def times_table(values, high, low):
    first, second = split_terms(values)
    return dot(first, high) + dot(second, high) + dot(first, low)


def quarters(values):
    return [values[:, LANES * i : LANES * (i + 1)] for i in range(4)]


def load_spectrum(got_ref, odd):
    y_devs = got_ref.shape[1]
    rows = got_ref.shape[4] // 2
    part = []
    for lane in range(4):
        pieces = [
            got_ref[:, g, 0, lane, odd * rows : (odd + 1) * rows, :].reshape(-1, LANES)
            for g in range(y_devs)
        ]
        part.append(jnp.concatenate(pieces, axis=0))
    return jnp.concatenate(part, axis=1)


def store_spectrum(send_ref, odd, parts):
    z_devs, y_devs = send_ref.shape[0], send_ref.shape[1]
    rows = send_ref.shape[4] // 2
    for lane in range(4):
        for g in range(y_devs):
            piece = parts[lane][g * z_devs * rows : (g + 1) * z_devs * rows]
            send_ref[:, g, 0, lane, odd * rows : (odd + 1) * rows, :] = piece.reshape(
                z_devs, rows, LANES
            )


def turned_back(both):
    rows = both.shape[0] // 2
    cosine, sine = quarters(both[:rows]), quarters(both[rows:])
    return [
        cosine[0] - sine[1],
        cosine[1] + sine[0],
        cosine[2] - sine[3],
        cosine[3] + sine[2],
    ]


def turned_ahead(both):
    rows = both.shape[0] // 2
    cosine, sine = quarters(both[:rows]), quarters(both[rows:])
    return [
        cosine[0] + sine[1],
        cosine[1] - sine[0],
        cosine[2] + sine[3],
        cosine[3] - sine[2],
    ]


def plane_back_sharp(got_ref, y_ref, x_ref):
    even = turned_back(table_times(y_ref[0, 0], y_ref[1, 0], load_spectrum(got_ref, 0)))
    odd = turned_back(table_times(y_ref[0, 1], y_ref[1, 1], load_spectrum(got_ref, 1)))
    upper = [a + b for a, b in zip(even, odd)]
    lower = [a - b for a, b in zip(even, odd)]
    spans = []
    for parity in range(2):
        values = jnp.concatenate(
            (
                jnp.concatenate(upper[2 * parity : 2 * parity + 2], axis=1),
                jnp.concatenate(lower[2 * parity : 2 * parity + 2], axis=1),
            ),
            axis=0,
        )
        spans.append(times_table(values, x_ref[0, parity], x_ref[1, parity]))
    return spans[0] + spans[1], spans[0] - spans[1]


def plane_back_soft(got_ref, y_ref, x_ref):
    both = table_times(y_ref[0, 0], y_ref[1, 0], load_spectrum(got_ref, 0)) + table_times(
        y_ref[0, 1], y_ref[1, 1], load_spectrum(got_ref, 1)
    )
    values = jnp.concatenate(turned_back(both), axis=1)
    plane = times_table(values, x_ref[0], x_ref[1])
    half = plane.shape[1] // 2
    return plane[:, :half], plane[:, half:]


def plane_ahead(left, right, send_ref, y_ref, x_ref):
    even = times_table(left + right, x_ref[0, 0], x_ref[1, 0])
    odd = times_table(left - right, x_ref[0, 1], x_ref[1, 1])
    values = jnp.concatenate((even, odd), axis=1)
    half = values.shape[0] // 2
    upper, lower = values[:half], values[half:]
    for parity, part in enumerate((upper + lower, upper - lower)):
        both = table_times(y_ref[0, parity], y_ref[1, parity], part)
        store_spectrum(send_ref, parity, turned_ahead(both))


def first_kernel(volume_ref, ya_ref, xa_ref, send_ref):
    half = volume_ref.shape[2] // 2
    plane_ahead(volume_ref[0, :, :half], volume_ref[0, :, half:], send_ref, ya_ref, xa_ref)


def ratio_kernel(got_ref, measured_ref, yb_ref, xb_ref, ya_ref, xa_ref, send_ref):
    half = measured_ref.shape[2] // 2
    left, right = plane_back_sharp(got_ref, yb_ref, xb_ref)
    left = measured_ref[0, :, :half] / jnp.maximum(left, FLOOR)
    right = measured_ref[0, :, half:] / jnp.maximum(right, FLOOR)
    plane_ahead(left, right, send_ref, ya_ref, xa_ref)


def correct_kernel(got_ref, estimate_ref, yb_ref, xb_ref, ya_ref, xa_ref, send_ref, out_ref):
    half = estimate_ref.shape[2] // 2
    left, right = plane_back_soft(got_ref, yb_ref, xb_ref)
    left = estimate_ref[0, :, :half] * left
    right = estimate_ref[0, :, half:] * right
    out_ref[0, :, :half] = left
    out_ref[0, :, half:] = right
    plane_ahead(left, right, send_ref, ya_ref, xa_ref)


def last_kernel(got_ref, estimate_ref, yb_ref, xb_ref, out_ref):
    half = estimate_ref.shape[2] // 2
    left, right = plane_back_soft(got_ref, yb_ref, xb_ref)
    out_ref[0, :, :half] = estimate_ref[0, :, :half] * left
    out_ref[0, :, half:] = estimate_ref[0, :, half:] * right


def gain_kernel(conjugate, got_ref, gain_ref, za_ref, zb_ref, send_ref):
    z_len, _, rows, _ = got_ref.shape
    flat = got_ref.reshape(z_len * 2 * rows, LANES)
    sent = send_ref.reshape(z_len * 2 * rows, LANES)

    def column(part):
        pieces = [flat[pl.ds(part * rows + i, z_len, 2 * rows), :] for i in range(rows)]
        return jnp.concatenate(pieces, axis=1)

    values = jnp.concatenate((column(0), column(1)), axis=0)
    spectrum = table_times(za_ref[0], za_ref[1], values)
    real, imag = spectrum[:z_len], spectrum[z_len:]
    gain_real, gain_imag = gain_ref[0, 0], gain_ref[0, 1]
    if conjugate:
        turned = (real * gain_real + imag * gain_imag, imag * gain_real - real * gain_imag)
    else:
        turned = (real * gain_real - imag * gain_imag, real * gain_imag + imag * gain_real)
    values = table_times(zb_ref[0], zb_ref[1], jnp.concatenate(turned, axis=0))
    for part in range(2):
        for i in range(rows):
            sent[pl.ds(part * rows + i, z_len, 2 * rows), :] = values[
                part * z_len : (part + 1) * z_len, i * LANES : (i + 1) * LANES
            ]


VMEM_BYTES = 58 * 2**20


def whole(table):
    return pl.BlockSpec(table.shape, lambda *_: (0,) * table.ndim)


def call(kernel, grid, arrays, specs, tables, outs, out_specs, flops, name):
    moved = sum(math.prod(a.shape) * a.dtype.itemsize for a in (*arrays, *tables, *jax.tree.leaves(outs)))
    return pl.pallas_call(
        kernel,
        grid=grid,
        in_specs=list(specs) + [whole(t) for t in tables],
        out_specs=out_specs,
        out_shape=outs,
        compiler_params=pltpu.CompilerParams(vmem_limit_bytes=VMEM_BYTES),
        cost_estimate=pl.CostEstimate(flops=flops, bytes_accessed=moved, transcendentals=0),
        name=name,
    )(*arrays, *tables)


def exchange(values):
    z_devs, y_devs = values.shape[:2]
    flat = values.reshape(z_devs * y_devs, *values.shape[2:])
    flat = lax.all_to_all(flat, ("gz", "gy"), split_axis=0, concat_axis=0, tiled=True)
    return flat.reshape(values.shape)


def to_planes(volume):
    return lax.all_to_all(volume, "gy", split_axis=0, concat_axis=1, tiled=True)


def from_planes(volume):
    return lax.all_to_all(volume, "gy", split_axis=1, concat_axis=0, tiled=True)


def gains_planes(transfer_real, transfer_imag):
    half = transfer_real.shape[2]
    both = jnp.stack((transfer_real, transfer_imag))
    both = lax.all_to_all(both, "gz", split_axis=2, concat_axis=1, tiled=True)
    _, z_len, rows, _ = both.shape
    both = both.reshape(2, z_len, rows // 2, 2, half // 2, 2).transpose(3, 5, 0, 1, 2, 4)
    return both.reshape(4, 2, z_len, rows // 2 * (half // 2))


def on_device_planes(measured, transfer_real, transfer_imag):
    z_devs, y_devs = lax.axis_size("gz"), lax.axis_size("gy")
    devs = z_devs * y_devs
    z_local, y_local, x_len = measured.shape
    z_len, y_len = z_local * z_devs, y_local * y_devs
    planes, rows = z_len // devs, y_len // devs
    xa, xb, xs = (jnp.asarray(t) for t in x_tables(x_len))
    ya, yb, ys = (jnp.asarray(t) for t in y_tables(y_len))
    za, zb, zs = (jnp.asarray(t) for t in z_tables(z_len))

    spectrum = jax.ShapeDtypeStruct((z_devs, y_devs, planes, 4, rows, LANES), jnp.float32)
    volume = jax.ShapeDtypeStruct((planes, y_len, x_len), jnp.float32)
    spectrum_spec = pl.BlockSpec(
        (z_devs, y_devs, 1, 4, rows, LANES), lambda p: (0, 0, p, 0, 0, 0)
    )
    volume_spec = pl.BlockSpec((1, y_len, x_len), lambda p: (p, 0, 0))
    ahead_flops = 3 * planes * y_len * x_len * (x_len + 2 * y_len)
    sharp_flops = ahead_flops
    soft_flops = 2 * ahead_flops

    def first(values):
        return call(
            first_kernel, (planes,), (values,), (volume_spec,), (ya, xa),
            spectrum, spectrum_spec, ahead_flops, "first",
        )

    def ratio(got, values):
        return call(
            ratio_kernel, (planes,), (got, values), (spectrum_spec, volume_spec), (yb, xb, ya, xa),
            spectrum, spectrum_spec, ahead_flops + sharp_flops, "ratio",
        )

    def correct(got, values):
        return call(
            correct_kernel, (planes,), (got, values), (spectrum_spec, volume_spec),
            (ys, xs, ya, xa), (spectrum, volume), (spectrum_spec, volume_spec),
            ahead_flops + soft_flops, "correct",
        )

    def last(got, values):
        return call(
            last_kernel, (planes,), (got, values), (spectrum_spec, volume_spec), (ys, xs),
            volume, volume_spec, soft_flops, "last",
        )

    columns = jax.ShapeDtypeStruct((z_len, 4, rows, LANES), jnp.float32)
    columns_spec = pl.BlockSpec((z_len, 2, rows // 2, LANES), lambda s: (0, s % 2, s // 2, 0))

    def filtered(got, gains, conjugate):
        gains_spec = pl.BlockSpec((1, *gains.shape[1:]), lambda s: (s, 0, 0, 0))
        return call(
            functools.partial(gain_kernel, conjugate), (4,),
            (got.reshape(columns.shape), gains), (columns_spec, gains_spec),
            (za, zs if conjugate else zb), columns, columns_spec,
            3 * 2 * 2 * 4 * z_len * z_len * rows * x_len, "adjoint" if conjugate else "blur",
        ).reshape(spectrum.shape)

    measured = to_planes(measured)
    gains = gains_planes(transfer_real, transfer_imag)
    estimate = measured
    send = first(measured)
    for iteration in range(ITERS):
        send = filtered(exchange(send), gains, False)
        send = ratio(exchange(send), measured)
        send = filtered(exchange(send), gains, True)
        got = exchange(send)
        if iteration < ITERS - 1:
            send, estimate = correct(got, estimate)
        else:
            estimate = last(got, estimate)
    return from_planes(estimate)


def planes_fit(mesh, shape):
    devs = mesh.shape["gz"] * mesh.shape["gy"]
    z_len, y_len, x_len = shape
    return (
        z_len % devs == 0
        and z_len % LANES == 0
        and y_len % (2 * SUBLANES * devs) == 0
        and x_len == 4 * LANES
    )


def solution(mesh):
    def run(measured, transfer_real, transfer_imag):
        spec = P("gz", "gy", None)
        fits = planes_fit(mesh, measured.shape)
        return jax.shard_map(
            on_device_planes if fits else on_device_rows,
            mesh=mesh,
            in_specs=(spec, spec, spec),
            out_specs=spec,
            check_vma=False,
        )(measured, transfer_real, transfer_imag)

    return run
```

```python
import functools
import math

import jax
import jax.numpy as jnp
import numpy as np
from jax import lax
from jax.experimental import pallas as pl
from jax.experimental.pallas import tpu as pltpu
from jax.sharding import PartitionSpec as P

ITERS = 2
RADIUS = 4


SIGMA = 1.5
FLOOR = 0.1


def product(form, left, right):
    return jnp.einsum(
        form, left, right, precision=lax.Precision.HIGHEST, preferred_element_type=jnp.float32
    )


def gauss_weights():
    offsets = jnp.arange(-RADIUS, RADIUS + 1).astype(jnp.float32)
    weights = jnp.exp(-offsets * offsets / (2.0 * SIGMA * SIGMA))
    return weights / jnp.sum(weights)


def taps_along(padded, axis, length):
    weights = gauss_weights()
    total = weights[0] * lax.slice_in_dim(padded, 0, length, axis=axis)
    for offset in range(1, 2 * RADIUS + 1):
        total = total + weights[offset] * lax.slice_in_dim(
            padded, offset, offset + length, axis=axis
        )
    return total


def blur_local(values, axis):
    length = values.shape[axis]
    widths = [(0, 0)] * values.ndim
    widths[axis] = (RADIUS, RADIUS)
    return taps_along(jnp.pad(values, widths), axis, length)


def angles(length, count):
    position = jnp.arange(length, dtype=jnp.int32)
    frequency = jnp.arange(count, dtype=jnp.int32)
    phase = position[:, None] * frequency[None, :] % length
    return phase.astype(jnp.float32) * (2.0 * math.pi / length)


def square_tables(length):
    angle = angles(length, length)
    cosine = jnp.cos(angle)
    sine = jnp.sin(angle)
    return ((cosine, sine), (cosine / length, sine / length))


def half_tables(length):
    half = length // 2
    angle = angles(length, half)
    cosine = jnp.cos(angle)
    sine = jnp.sin(angle)
    ahead = jnp.stack((cosine, -sine), axis=1)
    weight = jnp.where(jnp.arange(half) == 0, 1.0, 2.0).astype(jnp.float32) / length
    behind = jnp.stack((weight[:, None] * cosine.T, -weight[:, None] * sine.T), axis=0)
    return (ahead, behind)


def shaped(table, shape):
    return (table[0].reshape(shape), table[1].reshape(shape))


def turn(form, values, table, forward):
    first = product(form, values, table[0])
    second = product(form, values, table[1])
    if forward:
        return jnp.stack(
            (first[..., 0, :] + second[..., 1, :], first[..., 1, :] - second[..., 0, :]), axis=-2
        )
    return jnp.stack(
        (first[..., 0, :] - second[..., 1, :], first[..., 1, :] + second[..., 0, :]), axis=-2
    )


def across_z(values):
    return lax.all_to_all(values, "gz", split_axis=0, concat_axis=0, tiled=True)


def across_y(values):
    return lax.all_to_all(values, "gy", split_axis=0, concat_axis=0, tiled=True)


def forward_zfirst(field, ahead, y_fwd, z_fwd):
    z_local, y_local, x_len = field.shape
    z_devs = lax.axis_size("gz")
    y_devs = lax.axis_size("gy")
    x_share = ahead.shape[2] // z_devs
    z_len = z_local * z_devs
    y_len = y_local * y_devs
    z_share = z_len // y_devs
    values = product("zyx,xrgq->gzyrq", field, ahead.reshape(x_len, 2, z_devs, x_share))
    values = across_z(values).reshape(z_len, y_local, 2, x_share)
    values = turn("zyrq,zgk->gykrq", values, shaped(z_fwd, (z_len, y_devs, z_share)), True)
    values = across_y(values).reshape(y_len, z_share, 2, x_share)
    return turn("yjrq,yk->kjrq", values, y_fwd, True)


def inverse_zfirst(spectrum, behind, y_back, z_back, z_local, y_local):
    z_devs = lax.axis_size("gz")
    y_devs = lax.axis_size("gy")
    y_len, z_share, pair, x_share = spectrum.shape
    x_len = behind.shape[2]
    values = turn("kjrq,kgy->gyjrq", spectrum, shaped(y_back, (y_len, y_devs, y_local)), False)
    values = across_y(values)
    values = turn(
        "syjrq,sjgz->gzyrq", values, shaped(z_back, (y_devs, z_share, z_devs, z_local)), False
    )
    values = across_z(values)
    return product("szyrq,rsqx->zyx", values, behind.reshape(2, z_devs, x_share, x_len))


def gains_zfirst(transfer_real, transfer_imag):
    z_local, y_local, half = transfer_real.shape
    z_devs = lax.axis_size("gz")
    y_devs = lax.axis_size("gy")
    x_share = half // z_devs
    z_len = z_local * z_devs
    z_share = z_len // y_devs
    stacked = (
        jnp.stack((transfer_real, transfer_imag), axis=2)
        .reshape(z_local, y_local, 2, z_devs, x_share)
        .transpose(3, 0, 1, 2, 4)
    )
    stacked = (
        across_z(stacked).reshape(y_devs, z_share, y_local, 2, x_share).transpose(0, 2, 1, 3, 4)
    )
    return across_y(stacked).reshape(y_local * y_devs, z_share, 2, x_share)


def apply_gains(spectrum, gains, conjugate):
    spec_real = spectrum[..., 0, :]
    spec_imag = spectrum[..., 1, :]
    gain_real = gains[..., 0, :]
    gain_imag = gains[..., 1, :]
    if conjugate:
        return jnp.stack(
            (
                spec_real * gain_real + spec_imag * gain_imag,
                spec_imag * gain_real - spec_real * gain_imag,
            ),
            axis=-2,
        )
    return jnp.stack(
        (
            spec_real * gain_real - spec_imag * gain_imag,
            spec_real * gain_imag + spec_imag * gain_real,
        ),
        axis=-2,
    )


def on_device_rows(measured, transfer_real, transfer_imag):
    z_local, y_local, x_len = measured.shape
    z_len = z_local * lax.axis_size("gz")
    y_len = y_local * lax.axis_size("gy")
    ahead, behind = half_tables(x_len)
    y_fwd, y_back = square_tables(y_len)
    z_fwd, z_back = square_tables(z_len)
    soft_x = blur_local(behind, 2)
    soft_y = (blur_local(y_back[0], 1), blur_local(y_back[1], 1))
    soft_z = (blur_local(z_back[0], 1), blur_local(z_back[1], 1))
    gains = gains_zfirst(transfer_real, transfer_imag)
    estimate = measured
    for iteration in range(ITERS):
        spectrum = forward_zfirst(estimate, ahead, y_fwd, z_fwd)
        blurred = inverse_zfirst(
            apply_gains(spectrum, gains, False), behind, y_back, z_back, z_local, y_local
        )
        ratio = measured / jnp.maximum(blurred, FLOOR)
        spectrum = forward_zfirst(ratio, ahead, y_fwd, z_fwd)
        correction = inverse_zfirst(
            apply_gains(spectrum, gains, True), soft_x, soft_y, soft_z, z_local, y_local
        )
        estimate = estimate * correction
    return estimate


LANES = 128
SUBLANES = 8


def gauss_weights_np():
    offsets = np.arange(-RADIUS, RADIUS + 1).astype(np.float64)
    weights = np.exp(-offsets * offsets / (2.0 * SIGMA * SIGMA))
    return weights / weights.sum()


def smooth_np(table, axis):
    weights = gauss_weights_np()
    widths = [(0, 0)] * table.ndim
    widths[axis] = (RADIUS, RADIUS)
    padded = np.pad(table, widths)
    length = table.shape[axis]
    return sum(
        weights[j] * np.take(padded, np.arange(j, j + length), axis=axis)
        for j in range(2 * RADIUS + 1)
    )


def two_terms(table):
    high = table.astype(np.float32).astype(jnp.bfloat16)
    low = (table - high.astype(np.float64)).astype(np.float32).astype(jnp.bfloat16)
    return np.stack((high, low))


def phase_np(first, second, length):
    return 2.0 * np.pi * ((first[:, None] * second[None, :]) % length) / length


def x_tables(length):
    half = length // 2
    where = np.arange(length)
    ahead, behind = [], []
    for odd in range(2):
        k = 2 * np.arange(half // 2) + odd
        angle = phase_np(where, k, length)
        ahead.append(np.concatenate((np.cos(angle), -np.sin(angle)), axis=1)[:half])
        weight = (np.where(k == 0, 1.0, 2.0) / length)[:, None]
        behind.append(np.concatenate((weight * np.cos(angle).T, -weight * np.sin(angle).T), axis=0))
    sharp = np.stack([table[:, :half] for table in behind])
    soft = smooth_np(np.concatenate(behind, axis=0), 1)
    return two_terms(np.stack(ahead)), two_terms(sharp), two_terms(soft)


def y_tables(length):
    half = length // 2
    where = np.arange(length)
    ahead, sharp, soft = [], [], []
    for odd in range(2):
        k = 2 * np.arange(half) + odd
        angle = phase_np(k, where, length)
        cosine, sine = np.cos(angle), np.sin(angle)
        ahead.append(np.concatenate((cosine[:, :half], sine[:, :half]), axis=0))
        cosine, sine = cosine.T / length, sine.T / length
        sharp.append(np.concatenate((cosine[:half], sine[:half]), axis=0))
        soft.append(np.concatenate((smooth_np(cosine, 0), smooth_np(sine, 0)), axis=0))
    return two_terms(np.stack(ahead)), two_terms(np.stack(sharp)), two_terms(np.stack(soft))


def z_tables(length, order):
    where = np.arange(length)
    angle = phase_np(where, where, length)
    cosine, sine = np.cos(angle), np.sin(angle)
    ahead = np.block([[cosine, sine], [-sine, cosine]])
    cosine, sine = cosine / length, sine / length
    sharp = np.block([[cosine, -sine], [sine, cosine]])
    cosine, sine = smooth_np(cosine, 0), smooth_np(sine, 0)
    soft = np.block([[cosine, -sine], [sine, cosine]])
    cosine, sine = cosine[order], sine[order]
    parted = np.block([[cosine, -sine], [sine, cosine]])
    return two_terms(ahead), two_terms(sharp), two_terms(soft), two_terms(parted)


def dot(left, right):
    return jnp.dot(left, right, preferred_element_type=jnp.float32)


def split_terms(values):
    high = values.astype(jnp.bfloat16)
    return high, (values - high.astype(jnp.float32)).astype(jnp.bfloat16)


def table_times(high, low, values):
    first, second = split_terms(values)
    return dot(high, first) + dot(high, second) + dot(low, first)


def times_table(values, high, low):
    first, second = split_terms(values)
    return dot(first, high) + dot(second, high) + dot(first, low)


def quarters(values):
    return [values[:, LANES * i : LANES * (i + 1)] for i in range(4)]


def load_spectrum(got_ref, odd):
    y_devs = got_ref.shape[1]
    rows = got_ref.shape[4] // 2
    part = []
    for lane in range(4):
        pieces = [
            got_ref[:, g, 0, lane, odd * rows : (odd + 1) * rows, :].reshape(-1, LANES)
            for g in range(y_devs)
        ]
        part.append(jnp.concatenate(pieces, axis=0))
    return jnp.concatenate(part, axis=1)


def store_spectrum(send_ref, odd, parts):
    z_devs, y_devs = send_ref.shape[0], send_ref.shape[1]
    rows = send_ref.shape[4] // 2
    for lane in range(4):
        for g in range(y_devs):
            piece = parts[lane][g * z_devs * rows : (g + 1) * z_devs * rows]
            send_ref[:, g, 0, lane, odd * rows : (odd + 1) * rows, :] = piece.reshape(
                z_devs, rows, LANES
            )


def turned_back(both):
    rows = both.shape[0] // 2
    cosine, sine = quarters(both[:rows]), quarters(both[rows:])
    return [
        cosine[0] - sine[1],
        cosine[1] + sine[0],
        cosine[2] - sine[3],
        cosine[3] + sine[2],
    ]


def turned_ahead(both):
    rows = both.shape[0] // 2
    cosine, sine = quarters(both[:rows]), quarters(both[rows:])
    return [
        cosine[0] + sine[1],
        cosine[1] - sine[0],
        cosine[2] + sine[3],
        cosine[3] - sine[2],
    ]


def plane_back_sharp(got_ref, y_ref, x_ref):
    even = turned_back(table_times(y_ref[0, 0], y_ref[1, 0], load_spectrum(got_ref, 0)))
    odd = turned_back(table_times(y_ref[0, 1], y_ref[1, 1], load_spectrum(got_ref, 1)))
    upper = [a + b for a, b in zip(even, odd)]
    lower = [a - b for a, b in zip(even, odd)]
    spans = []
    for parity in range(2):
        values = jnp.concatenate(
            (
                jnp.concatenate(upper[2 * parity : 2 * parity + 2], axis=1),
                jnp.concatenate(lower[2 * parity : 2 * parity + 2], axis=1),
            ),
            axis=0,
        )
        spans.append(times_table(values, x_ref[0, parity], x_ref[1, parity]))
    return spans[0] + spans[1], spans[0] - spans[1]


def plane_back_soft(got_ref, y_ref, x_ref):
    both = table_times(y_ref[0, 0], y_ref[1, 0], load_spectrum(got_ref, 0)) + table_times(
        y_ref[0, 1], y_ref[1, 1], load_spectrum(got_ref, 1)
    )
    values = jnp.concatenate(turned_back(both), axis=1)
    plane = times_table(values, x_ref[0], x_ref[1])
    half = plane.shape[1] // 2
    return plane[:, :half], plane[:, half:]


def plane_ahead(left, right, send_ref, y_ref, x_ref):
    even = times_table(left + right, x_ref[0, 0], x_ref[1, 0])
    odd = times_table(left - right, x_ref[0, 1], x_ref[1, 1])
    values = jnp.concatenate((even, odd), axis=1)
    half = values.shape[0] // 2
    upper, lower = values[:half], values[half:]
    for parity, part in enumerate((upper + lower, upper - lower)):
        both = table_times(y_ref[0, parity], y_ref[1, parity], part)
        store_spectrum(send_ref, parity, turned_ahead(both))


def first_kernel(volume_ref, ya_ref, xa_ref, send_ref):
    half = volume_ref.shape[2] // 2
    plane_ahead(volume_ref[0, :, :half], volume_ref[0, :, half:], send_ref, ya_ref, xa_ref)


def ratio_kernel(got_ref, measured_ref, yb_ref, xb_ref, ya_ref, xa_ref, send_ref):
    half = measured_ref.shape[2] // 2
    left, right = plane_back_sharp(got_ref, yb_ref, xb_ref)
    left = measured_ref[0, :, :half] / jnp.maximum(left, FLOOR)
    right = measured_ref[0, :, half:] / jnp.maximum(right, FLOOR)
    plane_ahead(left, right, send_ref, ya_ref, xa_ref)


def correct_kernel(got_ref, estimate_ref, yb_ref, xb_ref, ya_ref, xa_ref, send_ref, out_ref):
    half = estimate_ref.shape[2] // 2
    left, right = plane_back_soft(got_ref, yb_ref, xb_ref)
    left = estimate_ref[0, :, :half] * left
    right = estimate_ref[0, :, half:] * right
    out_ref[0, :, :half] = left
    out_ref[0, :, half:] = right
    plane_ahead(left, right, send_ref, ya_ref, xa_ref)


def last_kernel(got_ref, estimate_ref, yb_ref, xb_ref, out_ref):
    half = estimate_ref.shape[2] // 2
    left, right = plane_back_soft(got_ref, yb_ref, xb_ref)
    out_ref[0, :, :half] = estimate_ref[0, :, :half] * left
    out_ref[0, :, half:] = estimate_ref[0, :, half:] * right


def gain_kernel(conjugate, got_ref, gain_ref, za_ref, zb_ref, *send_refs):
    z_len, _, rows, _ = got_ref.shape
    flat = got_ref.reshape(z_len * 2 * rows, LANES)

    def column(part):
        pieces = [flat[pl.ds(part * rows + i, z_len, 2 * rows), :] for i in range(rows)]
        return jnp.concatenate(pieces, axis=1)

    values = jnp.concatenate((column(0), column(1)), axis=0)
    spectrum = table_times(za_ref[0], za_ref[1], values)
    real, imag = spectrum[:z_len], spectrum[z_len:]
    gain_real, gain_imag = gain_ref[0, 0], gain_ref[0, 1]
    if conjugate:
        turned = (real * gain_real + imag * gain_imag, imag * gain_real - real * gain_imag)
    else:
        turned = (real * gain_real - imag * gain_imag, real * gain_imag + imag * gain_real)
    values = table_times(zb_ref[0], zb_ref[1], jnp.concatenate(turned, axis=0))
    start = 0
    for send_ref in send_refs:
        count = send_ref.shape[0]
        sent = send_ref.reshape(count * 2 * rows, LANES)
        for part in range(2):
            low = part * z_len + start
            for i in range(rows):
                sent[pl.ds(part * rows + i, count, 2 * rows), :] = values[
                    low : low + count, i * LANES : (i + 1) * LANES
                ]
        start += count


VMEM_BYTES = 58 * 2**20


def whole(table):
    return pl.BlockSpec(table.shape, lambda *_: (0,) * table.ndim)


def call(kernel, grid, arrays, specs, tables, outs, out_specs, flops, name):
    moved = sum(math.prod(a.shape) * a.dtype.itemsize for a in (*arrays, *tables, *jax.tree.leaves(outs)))
    return pl.pallas_call(
        kernel,
        grid=grid,
        in_specs=list(specs) + [whole(t) for t in tables],
        out_specs=out_specs,
        out_shape=outs,
        compiler_params=pltpu.CompilerParams(vmem_limit_bytes=VMEM_BYTES),
        cost_estimate=pl.CostEstimate(flops=flops, bytes_accessed=moved, transcendentals=0),
        name=name,
    )(*arrays, *tables)


def exchange(values):
    z_devs, y_devs = values.shape[:2]
    flat = values.reshape(z_devs * y_devs, *values.shape[2:])
    flat = lax.all_to_all(flat, ("gz", "gy"), split_axis=0, concat_axis=0, tiled=True)
    return flat.reshape(values.shape)


def swap(pieces):
    devs = pieces.shape[0]
    me = lax.axis_index("gy")
    got = lax.dynamic_update_index_in_dim(
        jnp.zeros_like(pieces), lax.dynamic_index_in_dim(pieces, me, 0), me, 0
    )
    for step in range(1, devs):
        to, source = lax.rem(me + step, devs), lax.rem(me + devs - step, devs)
        piece = lax.dynamic_index_in_dim(pieces, to, 0)
        piece = lax.ppermute(piece, "gy", [(i, (i + step) % devs) for i in range(devs)])
        got = lax.dynamic_update_index_in_dim(got, piece, source, 0)
    return got


def to_planes(volume):
    devs = lax.axis_size("gy")
    z_local, y_local, x_len = volume.shape
    got = swap(volume.reshape(devs, z_local // devs, y_local, x_len))
    return got.transpose(1, 0, 2, 3).reshape(z_local // devs, devs * y_local, x_len)


def from_planes(groups):
    devs = lax.axis_size("gy")
    parts = []
    for group in groups:
        count, y_len, x_len = group.shape
        parts.append(swap(group.reshape(count, devs, y_len // devs, x_len).transpose(1, 0, 2, 3)))
    whole_part = jnp.concatenate(parts, axis=1)
    return whole_part.reshape(-1, *whole_part.shape[2:])


def gains_planes(transfer_real, transfer_imag):
    half = transfer_real.shape[2]
    both = jnp.stack((transfer_real, transfer_imag))
    both = lax.all_to_all(both, "gz", split_axis=2, concat_axis=1, tiled=True)
    _, z_len, rows, _ = both.shape
    both = both.reshape(2, z_len, rows // 2, 2, half // 2, 2).transpose(3, 5, 0, 1, 2, 4)
    return both.reshape(4, 2, z_len, rows // 2 * (half // 2))


def on_device_planes(measured, transfer_real, transfer_imag):
    z_devs, y_devs = lax.axis_size("gz"), lax.axis_size("gy")
    devs = z_devs * y_devs
    z_local, y_local, x_len = measured.shape
    z_len, y_len = z_local * z_devs, y_local * y_devs
    planes, rows = z_len // devs, y_len // devs
    xa, xb, xs = (jnp.asarray(t) for t in x_tables(x_len))
    ya, yb, ys = (jnp.asarray(t) for t in y_tables(y_len))
    groups = (planes - 1, 1) if planes > 1 else (planes,)
    starts = [sum(groups[:i]) for i in range(len(groups))]
    by_plane = np.arange(z_len).reshape(devs, planes)
    order = np.concatenate(
        [by_plane[:, s : s + n].reshape(-1) for s, n in zip(starts, groups)]
    )
    za, zb, zs, zp = (jnp.asarray(t) for t in z_tables(z_len, order))

    spectrum = jax.ShapeDtypeStruct((z_devs, y_devs, planes, 4, rows, LANES), jnp.float32)
    volume = jax.ShapeDtypeStruct((planes, y_len, x_len), jnp.float32)
    spectrum_spec = pl.BlockSpec(
        (z_devs, y_devs, 1, 4, rows, LANES), lambda p: (0, 0, p, 0, 0, 0)
    )
    volume_spec = pl.BlockSpec((1, y_len, x_len), lambda p: (p, 0, 0))
    ahead_flops = 3 * planes * y_len * x_len * (x_len + 2 * y_len)
    sharp_flops = ahead_flops
    soft_flops = 2 * ahead_flops

    def first(values):
        return call(
            first_kernel, (planes,), (values,), (volume_spec,), (ya, xa),
            spectrum, spectrum_spec, ahead_flops, "first",
        )

    def ratio(got, values):
        return call(
            ratio_kernel, (planes,), (got, values), (spectrum_spec, volume_spec), (yb, xb, ya, xa),
            spectrum, spectrum_spec, ahead_flops + sharp_flops, "ratio",
        )

    def correct(got, values):
        return call(
            correct_kernel, (planes,), (got, values), (spectrum_spec, volume_spec),
            (ys, xs, ya, xa), (spectrum, volume), (spectrum_spec, volume_spec),
            ahead_flops + soft_flops, "correct",
        )

    def last(got, values, start):
        count = got.shape[2]
        return call(
            last_kernel, (count,), (got, values),
            (spectrum_spec, pl.BlockSpec((1, y_len, x_len), lambda p: (p + start, 0, 0))),
            (ys, xs), jax.ShapeDtypeStruct((count, y_len, x_len), jnp.float32), volume_spec,
            soft_flops * count // planes, "last",
        )

    columns = (z_len, 4, rows, LANES)

    def columns_spec(count):
        return pl.BlockSpec((count, 2, rows // 2, LANES), lambda s: (0, s % 2, s // 2, 0))

    def filtered(got, gains, conjugate, back, parts):
        gains_spec = pl.BlockSpec((1, *gains.shape[1:]), lambda s: (s, 0, 0, 0))
        sent = call(
            functools.partial(gain_kernel, conjugate), (4,),
            (got.reshape(columns), gains), (columns_spec(z_len), gains_spec),
            (za, back),
            [jax.ShapeDtypeStruct((devs * n, *columns[1:]), jnp.float32) for n in parts],
            [columns_spec(devs * n) for n in parts],
            3 * 2 * 2 * 4 * z_len * z_len * rows * x_len, "adjoint" if conjugate else "blur",
        )
        return [v.reshape(z_devs, y_devs, n, *columns[1:]) for v, n in zip(sent, parts)]

    gains = gains_planes(transfer_real, transfer_imag)
    measured = to_planes(measured)
    estimate = measured
    send = first(measured)
    for iteration in range(ITERS):
        (send,) = filtered(exchange(send), gains, False, zb, (planes,))
        send = ratio(exchange(send), measured)
        if iteration < ITERS - 1:
            (send,) = filtered(exchange(send), gains, True, zs, (planes,))
            send, estimate = correct(exchange(send), estimate)
    sends = filtered(exchange(send), gains, True, zp, groups)
    return from_planes([last(exchange(v), estimate, s) for v, s in zip(sends, starts)])


def planes_fit(mesh, shape):
    devs = mesh.shape["gz"] * mesh.shape["gy"]
    z_len, y_len, x_len = shape
    return (
        z_len % devs == 0
        and z_len % LANES == 0
        and y_len % (2 * SUBLANES * devs) == 0
        and x_len == 4 * LANES
    )


def solution(mesh):
    def run(measured, transfer_real, transfer_imag):
        spec = P("gz", "gy", None)
        fits = planes_fit(mesh, measured.shape)
        return jax.shard_map(
            on_device_planes if fits else on_device_rows,
            mesh=mesh,
            in_specs=(spec, spec, spec),
            out_specs=spec,
            check_vma=False,
        )(measured, transfer_real, transfer_imag)

    return run
```

```python
import functools
import math

import jax
import jax.numpy as jnp
import numpy as np
from jax import lax
from jax.experimental import pallas as pl
from jax.experimental.pallas import tpu as pltpu
from jax.sharding import PartitionSpec as P

ITERS = 2
RADIUS = 4


SIGMA = 1.5
FLOOR = 0.1


def product(form, left, right):
    return jnp.einsum(
        form, left, right, precision=lax.Precision.HIGHEST, preferred_element_type=jnp.float32
    )


def gauss_weights():
    offsets = jnp.arange(-RADIUS, RADIUS + 1).astype(jnp.float32)
    weights = jnp.exp(-offsets * offsets / (2.0 * SIGMA * SIGMA))
    return weights / jnp.sum(weights)


def taps_along(padded, axis, length):
    weights = gauss_weights()
    total = weights[0] * lax.slice_in_dim(padded, 0, length, axis=axis)
    for offset in range(1, 2 * RADIUS + 1):
        total = total + weights[offset] * lax.slice_in_dim(
            padded, offset, offset + length, axis=axis
        )
    return total


def blur_local(values, axis):
    length = values.shape[axis]
    widths = [(0, 0)] * values.ndim
    widths[axis] = (RADIUS, RADIUS)
    return taps_along(jnp.pad(values, widths), axis, length)


def angles(length, count):
    position = jnp.arange(length, dtype=jnp.int32)
    frequency = jnp.arange(count, dtype=jnp.int32)
    phase = position[:, None] * frequency[None, :] % length
    return phase.astype(jnp.float32) * (2.0 * math.pi / length)


def square_tables(length):
    angle = angles(length, length)
    cosine = jnp.cos(angle)
    sine = jnp.sin(angle)
    return ((cosine, sine), (cosine / length, sine / length))


def half_tables(length):
    half = length // 2
    angle = angles(length, half)
    cosine = jnp.cos(angle)
    sine = jnp.sin(angle)
    ahead = jnp.stack((cosine, -sine), axis=1)
    weight = jnp.where(jnp.arange(half) == 0, 1.0, 2.0).astype(jnp.float32) / length
    behind = jnp.stack((weight[:, None] * cosine.T, -weight[:, None] * sine.T), axis=0)
    return (ahead, behind)


def shaped(table, shape):
    return (table[0].reshape(shape), table[1].reshape(shape))


def turn(form, values, table, forward):
    first = product(form, values, table[0])
    second = product(form, values, table[1])
    if forward:
        return jnp.stack(
            (first[..., 0, :] + second[..., 1, :], first[..., 1, :] - second[..., 0, :]), axis=-2
        )
    return jnp.stack(
        (first[..., 0, :] - second[..., 1, :], first[..., 1, :] + second[..., 0, :]), axis=-2
    )


def across_z(values):
    return lax.all_to_all(values, "gz", split_axis=0, concat_axis=0, tiled=True)


def across_y(values):
    return lax.all_to_all(values, "gy", split_axis=0, concat_axis=0, tiled=True)


def forward_zfirst(field, ahead, y_fwd, z_fwd):
    z_local, y_local, x_len = field.shape
    z_devs = lax.axis_size("gz")
    y_devs = lax.axis_size("gy")
    x_share = ahead.shape[2] // z_devs
    z_len = z_local * z_devs
    y_len = y_local * y_devs
    z_share = z_len // y_devs
    values = product("zyx,xrgq->gzyrq", field, ahead.reshape(x_len, 2, z_devs, x_share))
    values = across_z(values).reshape(z_len, y_local, 2, x_share)
    values = turn("zyrq,zgk->gykrq", values, shaped(z_fwd, (z_len, y_devs, z_share)), True)
    values = across_y(values).reshape(y_len, z_share, 2, x_share)
    return turn("yjrq,yk->kjrq", values, y_fwd, True)


def inverse_zfirst(spectrum, behind, y_back, z_back, z_local, y_local):
    z_devs = lax.axis_size("gz")
    y_devs = lax.axis_size("gy")
    y_len, z_share, pair, x_share = spectrum.shape
    x_len = behind.shape[2]
    values = turn("kjrq,kgy->gyjrq", spectrum, shaped(y_back, (y_len, y_devs, y_local)), False)
    values = across_y(values)
    values = turn(
        "syjrq,sjgz->gzyrq", values, shaped(z_back, (y_devs, z_share, z_devs, z_local)), False
    )
    values = across_z(values)
    return product("szyrq,rsqx->zyx", values, behind.reshape(2, z_devs, x_share, x_len))


def gains_zfirst(transfer_real, transfer_imag):
    z_local, y_local, half = transfer_real.shape
    z_devs = lax.axis_size("gz")
    y_devs = lax.axis_size("gy")
    x_share = half // z_devs
    z_len = z_local * z_devs
    z_share = z_len // y_devs
    stacked = (
        jnp.stack((transfer_real, transfer_imag), axis=2)
        .reshape(z_local, y_local, 2, z_devs, x_share)
        .transpose(3, 0, 1, 2, 4)
    )
    stacked = (
        across_z(stacked).reshape(y_devs, z_share, y_local, 2, x_share).transpose(0, 2, 1, 3, 4)
    )
    return across_y(stacked).reshape(y_local * y_devs, z_share, 2, x_share)


def apply_gains(spectrum, gains, conjugate):
    spec_real = spectrum[..., 0, :]
    spec_imag = spectrum[..., 1, :]
    gain_real = gains[..., 0, :]
    gain_imag = gains[..., 1, :]
    if conjugate:
        return jnp.stack(
            (
                spec_real * gain_real + spec_imag * gain_imag,
                spec_imag * gain_real - spec_real * gain_imag,
            ),
            axis=-2,
        )
    return jnp.stack(
        (
            spec_real * gain_real - spec_imag * gain_imag,
            spec_real * gain_imag + spec_imag * gain_real,
        ),
        axis=-2,
    )


def on_device_rows(measured, transfer_real, transfer_imag):
    z_local, y_local, x_len = measured.shape
    z_len = z_local * lax.axis_size("gz")
    y_len = y_local * lax.axis_size("gy")
    ahead, behind = half_tables(x_len)
    y_fwd, y_back = square_tables(y_len)
    z_fwd, z_back = square_tables(z_len)
    soft_x = blur_local(behind, 2)
    soft_y = (blur_local(y_back[0], 1), blur_local(y_back[1], 1))
    soft_z = (blur_local(z_back[0], 1), blur_local(z_back[1], 1))
    gains = gains_zfirst(transfer_real, transfer_imag)
    estimate = measured
    for iteration in range(ITERS):
        spectrum = forward_zfirst(estimate, ahead, y_fwd, z_fwd)
        blurred = inverse_zfirst(
            apply_gains(spectrum, gains, False), behind, y_back, z_back, z_local, y_local
        )
        ratio = measured / jnp.maximum(blurred, FLOOR)
        spectrum = forward_zfirst(ratio, ahead, y_fwd, z_fwd)
        correction = inverse_zfirst(
            apply_gains(spectrum, gains, True), soft_x, soft_y, soft_z, z_local, y_local
        )
        estimate = estimate * correction
    return estimate


LANES = 128
SUBLANES = 8


def gauss_weights_np():
    offsets = np.arange(-RADIUS, RADIUS + 1).astype(np.float64)
    weights = np.exp(-offsets * offsets / (2.0 * SIGMA * SIGMA))
    return weights / weights.sum()


def smooth_np(table, axis):
    weights = gauss_weights_np()
    widths = [(0, 0)] * table.ndim
    widths[axis] = (RADIUS, RADIUS)
    padded = np.pad(table, widths)
    length = table.shape[axis]
    return sum(
        weights[j] * np.take(padded, np.arange(j, j + length), axis=axis)
        for j in range(2 * RADIUS + 1)
    )


def two_terms(table):
    high = table.astype(np.float32).astype(jnp.bfloat16)
    low = (table - high.astype(np.float64)).astype(np.float32).astype(jnp.bfloat16)
    return np.stack((high, low))


def phase_np(first, second, length):
    return 2.0 * np.pi * ((first[:, None] * second[None, :]) % length) / length


def x_tables(length):
    half = length // 2
    where = np.arange(length)
    ahead, behind = [], []
    for odd in range(2):
        k = 2 * np.arange(half // 2) + odd
        angle = phase_np(k, where, length)
        ahead.append(np.concatenate((np.cos(angle), -np.sin(angle)), axis=0)[:, :half])
        weight = (np.where(k == 0, 1.0, 2.0) / length)[:, None]
        behind.append(np.concatenate((weight * np.cos(angle), -weight * np.sin(angle)), axis=0))
    sharp = np.stack([table[:, :half] for table in behind])
    soft = smooth_np(np.concatenate(behind, axis=0), 1)
    return two_terms(np.stack(ahead)), two_terms(sharp), two_terms(soft)


def y_tables(length):
    half = length // 2
    where = np.arange(length)
    ahead, sharp, soft = [], [], []
    for odd in range(2):
        k = 2 * np.arange(half) + odd
        angle = phase_np(where, k, length)
        cosine, sine = np.cos(angle), np.sin(angle)
        ahead.append(np.concatenate((cosine[:half], sine[:half]), axis=1))
        cosine, sine = cosine.T / length, sine.T / length
        sharp.append(np.concatenate((cosine[:, :half], sine[:, :half]), axis=1))
        soft.append(np.concatenate((smooth_np(cosine, 1), smooth_np(sine, 1)), axis=1))
    return two_terms(np.stack(ahead)), two_terms(np.stack(sharp)), two_terms(np.concatenate(soft))


def z_tables(length):
    where = np.arange(length)
    angle = phase_np(where, where, length)
    cosine, sine = np.cos(angle), np.sin(angle)
    ahead = np.block([[cosine, sine], [-sine, cosine]])
    cosine, sine = cosine / length, sine / length
    sharp = np.block([[cosine, -sine], [sine, cosine]])
    cosine, sine = smooth_np(cosine, 0), smooth_np(sine, 0)
    soft = np.block([[cosine, -sine], [sine, cosine]])
    return two_terms(ahead), two_terms(sharp), two_terms(soft)


def dot(left, right):
    return jnp.dot(left, right, preferred_element_type=jnp.float32)


def split_terms(values):
    high = values.astype(jnp.bfloat16)
    return high, (values - high.astype(jnp.float32)).astype(jnp.bfloat16)


def table_times(high, low, values):
    first, second = split_terms(values)
    return dot(
        jnp.concatenate((high, high, low), axis=1), jnp.concatenate((first, second, first), axis=0)
    )


def times_table(values, high, low):
    first, second = split_terms(values)
    return dot(
        jnp.concatenate((first, second, first), axis=1), jnp.concatenate((high, high, low), axis=0)
    )


def table_times_lines(high, low, values):
    first, second = split_terms(values)
    return lax.dot_general(
        jnp.concatenate((high, high, low), axis=1),
        jnp.concatenate((first, second, first), axis=1),
        (((1,), (1,)), ((), ())),
        preferred_element_type=jnp.float32,
    )


def lines_of(values, high, low):
    return times_table(values.T, high, low)


def load_lines(got_ref):
    kx_len = got_ref.shape[0] * got_ref.shape[1]
    z_len = got_ref.shape[4]
    flat = got_ref.reshape(kx_len * 2 * z_len, LANES)
    parities = []
    for odd in range(2):
        parts = []
        for part in range(2):
            pieces = [
                flat[pl.ds((odd * 2 + part) * z_len + z, kx_len // 2, 4 * z_len), :]
                for z in range(z_len)
            ]
            parts.append(jnp.concatenate(pieces, axis=1))
        parities.append(jnp.concatenate(parts, axis=0))
    return parities


def store_lines(send_ref, odd, values):
    kx_len = send_ref.shape[0] * send_ref.shape[1]
    z_len = send_ref.shape[4]
    flat = send_ref.reshape(kx_len * 2 * z_len, LANES)
    half = kx_len // 2
    for part in range(2):
        for z in range(z_len):
            flat[pl.ds((odd * 2 + part) * z_len + z, half, 4 * z_len), :] = values[
                part * half : (part + 1) * half, z * LANES : (z + 1) * LANES
            ]


def lines_back_sharp(got_ref, x_ref):
    even, odd = load_lines(got_ref)
    even = lines_of(even, x_ref[0, 0], x_ref[1, 0])
    odd = lines_of(odd, x_ref[0, 1], x_ref[1, 1])
    return even + odd, even - odd


def lines_back_soft(got_ref, x_ref):
    both = lines_of(jnp.concatenate(load_lines(got_ref), axis=0), x_ref[0], x_ref[1])
    half = both.shape[1] // 2
    return both[:, :half], both[:, half:]


def lines_ahead(left, right, send_ref, x_ref):
    store_lines(send_ref, 0, table_times_lines(x_ref[0, 0], x_ref[1, 0], left + right))
    store_lines(send_ref, 1, table_times_lines(x_ref[0, 1], x_ref[1, 1], left - right))


def halves(volume_ref):
    half = volume_ref.shape[2] // 2
    return (
        volume_ref[:, :, :half].reshape(-1, half),
        volume_ref[:, :, half:].reshape(-1, half),
    )


def store_halves(volume_ref, left, right):
    half = volume_ref.shape[2] // 2
    shape = (*volume_ref.shape[:2], half)
    volume_ref[:, :, :half] = left.reshape(shape)
    volume_ref[:, :, half:] = right.reshape(shape)


def first_kernel(volume_ref, xa_ref, send_ref):
    left, right = halves(volume_ref)
    lines_ahead(left, right, send_ref, xa_ref)


def ratio_kernel(got_ref, measured_ref, xb_ref, xa_ref, send_ref):
    left, right = lines_back_sharp(got_ref, xb_ref)
    over_left, over_right = halves(measured_ref)
    left = over_left / jnp.maximum(left, FLOOR)
    right = over_right / jnp.maximum(right, FLOOR)
    lines_ahead(left, right, send_ref, xa_ref)


def correct_kernel(got_ref, estimate_ref, xb_ref, xa_ref, send_ref, out_ref):
    left, right = lines_back_soft(got_ref, xb_ref)
    old_left, old_right = halves(estimate_ref)
    left, right = old_left * left, old_right * right
    store_halves(out_ref, left, right)
    lines_ahead(left, right, send_ref, xa_ref)


def last_kernel(got_ref, estimate_ref, xb_ref, out_ref):
    left, right = lines_back_soft(got_ref, xb_ref)
    old_left, old_right = halves(estimate_ref)
    store_halves(out_ref, old_left * left, old_right * right)


def arrange_kernel(real_ref, imag_ref, pick_ref, send_ref):
    z_len, _, kx_len = real_ref.shape
    tiles = send_ref.shape[2]
    flat = send_ref.reshape(kx_len * 2 * tiles * z_len, LANES)
    for part, ref in enumerate((real_ref, imag_ref)):
        for z in range(z_len):
            values = ref[z].T
            first, second = split_terms(values)
            rest = values - first.astype(jnp.float32) - second.astype(jnp.float32)
            pick = pick_ref[...]
            values = dot(first, pick) + dot(second, pick) + dot(rest.astype(jnp.bfloat16), pick)
            for tile in range(tiles):
                start = (part * tiles + tile) * z_len + z
                flat[pl.ds(start, kx_len, 2 * tiles * z_len), :] = values[
                    :, tile * LANES : (tile + 1) * LANES
                ]


def plane_of(ref, k, part, tiles):
    pieces = [
        ref[:, g, k, part, tile].reshape(-1, LANES) for g in range(ref.shape[1]) for tile in tiles
    ]
    return jnp.concatenate(pieces, axis=1)


def turned_ahead(both):
    rows, half = both.shape[0] // 2, both.shape[1] // 2
    return (
        both[:rows, :half] + both[rows:, half:],
        both[rows:, :half] - both[:rows, half:],
    )


def turned_back(both):
    rows, half = both.shape[0] // 2, both.shape[1] // 2
    return (
        both[:rows, :half] - both[rows:, half:],
        both[rows:, :half] + both[:rows, half:],
    )


def gain_kernel(adjoint, got_ref, gain_ref, ya_ref, za_ref, zb_ref, yb_ref, send_ref):
    z_devs, y_devs, share, _, tiles, z_local, _ = got_ref.shape
    rows = 2 * z_devs * z_local
    half = y_devs * tiles * LANES // 2

    def by_kx(values):
        return [values[k * rows : (k + 1) * rows] for k in range(share)]

    values = jnp.concatenate(
        [plane_of(got_ref, k, part, range(tiles)) for k in range(share) for part in range(2)],
        axis=0,
    )
    left, right = values[:, :half], values[:, half:]
    evens = by_kx(times_table(left + right, ya_ref[0, 0], ya_ref[1, 0]))
    odds = by_kx(times_table(left - right, ya_ref[0, 1], ya_ref[1, 1]))
    planes = []
    for k in range(share):
        even, odd = turned_ahead(evens[k]), turned_ahead(odds[k])
        values = jnp.concatenate(
            [jnp.concatenate((even[part], odd[part]), axis=1) for part in range(2)], axis=0
        )
        values = table_times(za_ref[0], za_ref[1], values)
        real, imag = values[: rows // 2], values[rows // 2 :]
        gain_real, gain_imag = [
            jnp.concatenate(
                (
                    plane_of(gain_ref, k, part, range(tiles // 2)),
                    plane_of(gain_ref, k, part, range(tiles // 2, tiles)),
                ),
                axis=1,
            )
            for part in range(2)
        ]
        if adjoint:
            turned = (real * gain_real + imag * gain_imag, imag * gain_real - real * gain_imag)
        else:
            turned = (real * gain_real - imag * gain_imag, real * gain_imag + imag * gain_real)
        planes.append(table_times(zb_ref[0], zb_ref[1], jnp.concatenate(turned, axis=0)))
    values = jnp.concatenate(planes, axis=0)
    if adjoint:
        boths = by_kx(times_table(values, yb_ref[0], yb_ref[1]))
    else:
        evens = by_kx(times_table(values[:, :half], yb_ref[0, 0], yb_ref[1, 0]))
        odds = by_kx(times_table(values[:, half:], yb_ref[0, 1], yb_ref[1, 1]))
    for k in range(share):
        if adjoint:
            parts = turned_back(boths[k])
        else:
            even, odd = turned_back(evens[k]), turned_back(odds[k])
            parts = [jnp.concatenate((a + b, a - b), axis=1) for a, b in zip(even, odd)]
        for part in range(2):
            for g in range(y_devs):
                for tile in range(tiles):
                    low = (g * tiles + tile) * LANES
                    send_ref[:, g, k, part, tile] = parts[part][:, low : low + LANES].reshape(
                        z_devs, z_local, LANES
                    )


KX_AT_ONCE = 2
VMEM_BYTES = 32 * 2**20


def whole(table):
    return pl.BlockSpec(table.shape, lambda *_: (0,) * table.ndim)


def call(kernel, grid, arrays, specs, tables, outs, out_specs, flops, name):
    leaves = (*arrays, *tables, *jax.tree.leaves(outs))
    moved = sum(math.prod(a.shape) * a.dtype.itemsize for a in leaves)
    return pl.pallas_call(
        kernel,
        grid=grid,
        in_specs=list(specs) + [whole(t) for t in tables],
        out_specs=out_specs,
        out_shape=outs,
        compiler_params=pltpu.CompilerParams(vmem_limit_bytes=VMEM_BYTES),
        cost_estimate=pl.CostEstimate(flops=flops, bytes_accessed=moved, transcendentals=0),
        name=name,
    )(*arrays, *tables)


def exchange(values):
    return lax.all_to_all(values, ("gz", "gy"), split_axis=0, concat_axis=0, tiled=True)


def on_device_lines(measured, transfer_real, transfer_imag):
    z_devs, y_devs = lax.axis_size("gz"), lax.axis_size("gy")
    devs = z_devs * y_devs
    z_local, y_local, x_len = measured.shape
    z_len, y_len, kx_len = z_local * z_devs, y_local * y_devs, x_len // 2
    tiles, share = y_local // LANES, kx_len // devs
    xa, xb, xs = (jnp.asarray(t) for t in x_tables(x_len))
    ya, yb, ys = (jnp.asarray(t) for t in y_tables(y_len))
    za, zb, zs = (jnp.asarray(t) for t in z_tables(z_len))
    picked = np.concatenate((np.arange(0, y_local, 2), np.arange(1, y_local, 2)))
    pick = jnp.asarray(np.eye(y_local, dtype=np.float32)[:, picked].astype(jnp.bfloat16))

    spectrum = jax.ShapeDtypeStruct((devs, share, 2, tiles, z_local, LANES), jnp.float32)
    volume = jax.ShapeDtypeStruct(measured.shape, jnp.float32)
    lines_spec = pl.BlockSpec(
        (devs, share, 2, 1, z_local, LANES), lambda t: (0, 0, 0, t, 0, 0)
    )
    volume_spec = pl.BlockSpec((z_local, LANES, x_len), lambda t: (0, t, 0))
    line_flops = 3 * z_local * y_local * x_len * x_len

    def first(values):
        return call(
            first_kernel, (tiles,), (values,), (volume_spec,), (xa,),
            spectrum, lines_spec, line_flops, "first",
        )

    def ratio(got, values):
        return call(
            ratio_kernel, (tiles,), (got, values), (lines_spec, volume_spec), (xb, xa),
            spectrum, lines_spec, 2 * line_flops, "ratio",
        )

    def correct(got, values):
        return call(
            correct_kernel, (tiles,), (got, values), (lines_spec, volume_spec), (xs, xa),
            (spectrum, volume), (lines_spec, volume_spec), 3 * line_flops, "correct",
        )

    def last(got, values):
        return call(
            last_kernel, (tiles,), (got, values), (lines_spec, volume_spec), (xs,),
            volume, volume_spec, 2 * line_flops, "last",
        )

    planes = (z_devs, y_devs, *spectrum.shape[1:])
    at_once = KX_AT_ONCE if share % KX_AT_ONCE == 0 else 1
    plane_spec = pl.BlockSpec(
        (z_devs, y_devs, at_once, 2, tiles, z_local, LANES), lambda k: (0, 0, k, 0, 0, 0, 0)
    )

    def filtered(got, gains, adjoint):
        return call(
            functools.partial(gain_kernel, adjoint), (share // at_once,),
            (got.reshape(planes), gains.reshape(planes)), (plane_spec, plane_spec),
            (ya, za, zs, ys) if adjoint else (ya, za, zb, yb),
            jax.ShapeDtypeStruct(planes, jnp.float32), plane_spec,
            3 * 8 * share * z_len * y_len * (2 * z_len + y_len), "adjoint" if adjoint else "blur",
        ).reshape(spectrum.shape)

    def arranged(transfer_real, transfer_imag):
        in_spec = pl.BlockSpec((z_local, y_local, LANES), lambda k: (0, 0, k))
        out_spec = pl.BlockSpec((LANES, 2, tiles, z_local, LANES), lambda k: (k, 0, 0, 0, 0))
        return call(
            arrange_kernel, (kx_len // LANES,), (transfer_real, transfer_imag), (in_spec, in_spec),
            (pick,), jax.ShapeDtypeStruct((kx_len, *spectrum.shape[2:]), jnp.float32), out_spec,
            3 * 4 * z_local * y_local * y_local * kx_len, "arrange",
        ).reshape(spectrum.shape)

    send = first(measured)
    send, transfer_real, transfer_imag = lax.optimization_barrier(
        (send, transfer_real, transfer_imag)
    )
    send = exchange(send)
    gains = exchange(arranged(transfer_real, transfer_imag))
    estimate = measured
    for iteration in range(ITERS):
        send = ratio(exchange(filtered(send, gains, False)), measured)
        send = exchange(filtered(exchange(send), gains, True))
        if iteration < ITERS - 1:
            send, estimate = correct(send, estimate)
            send = exchange(send)
    return last(send, estimate)


def lines_fit(mesh, shape):
    z_devs, y_devs = mesh.shape["gz"], mesh.shape["gy"]
    z_len, y_len, x_len = shape
    return (
        z_len % LANES == 0
        and z_len // z_devs == SUBLANES
        and y_len % (2 * LANES * y_devs) == 0
        and x_len % (4 * LANES) == 0
        and x_len // 2 % (z_devs * y_devs) == 0
    )


def solution(mesh):
    def run(measured, transfer_real, transfer_imag):
        spec = P("gz", "gy", None)
        fits = lines_fit(mesh, measured.shape)
        return jax.shard_map(
            on_device_lines if fits else on_device_rows,
            mesh=mesh,
            in_specs=(spec, spec, spec),
            out_specs=spec,
            check_vma=False,
        )(measured, transfer_real, transfer_imag)

    return run
```

```python
import functools
import math

import jax
import jax.numpy as jnp
import numpy as np
from jax import lax
from jax.experimental import pallas as pl
from jax.experimental.pallas import tpu as pltpu
from jax.sharding import PartitionSpec as P

ITERS = 2
RADIUS = 4


SIGMA = 1.5
FLOOR = 0.1


def product(form, left, right):
    return jnp.einsum(
        form, left, right, precision=lax.Precision.HIGHEST, preferred_element_type=jnp.float32
    )


def gauss_weights():
    offsets = jnp.arange(-RADIUS, RADIUS + 1).astype(jnp.float32)
    weights = jnp.exp(-offsets * offsets / (2.0 * SIGMA * SIGMA))
    return weights / jnp.sum(weights)


def taps_along(padded, axis, length):
    weights = gauss_weights()
    total = weights[0] * lax.slice_in_dim(padded, 0, length, axis=axis)
    for offset in range(1, 2 * RADIUS + 1):
        total = total + weights[offset] * lax.slice_in_dim(
            padded, offset, offset + length, axis=axis
        )
    return total


def blur_local(values, axis):
    length = values.shape[axis]
    widths = [(0, 0)] * values.ndim
    widths[axis] = (RADIUS, RADIUS)
    return taps_along(jnp.pad(values, widths), axis, length)


def angles(length, count):
    position = jnp.arange(length, dtype=jnp.int32)
    frequency = jnp.arange(count, dtype=jnp.int32)
    phase = position[:, None] * frequency[None, :] % length
    return phase.astype(jnp.float32) * (2.0 * math.pi / length)


def square_tables(length):
    angle = angles(length, length)
    cosine = jnp.cos(angle)
    sine = jnp.sin(angle)
    return ((cosine, sine), (cosine / length, sine / length))


def half_tables(length):
    half = length // 2
    angle = angles(length, half)
    cosine = jnp.cos(angle)
    sine = jnp.sin(angle)
    ahead = jnp.stack((cosine, -sine), axis=1)
    weight = jnp.where(jnp.arange(half) == 0, 1.0, 2.0).astype(jnp.float32) / length
    behind = jnp.stack((weight[:, None] * cosine.T, -weight[:, None] * sine.T), axis=0)
    return (ahead, behind)


def shaped(table, shape):
    return (table[0].reshape(shape), table[1].reshape(shape))


def turn(form, values, table, forward):
    first = product(form, values, table[0])
    second = product(form, values, table[1])
    if forward:
        return jnp.stack(
            (first[..., 0, :] + second[..., 1, :], first[..., 1, :] - second[..., 0, :]), axis=-2
        )
    return jnp.stack(
        (first[..., 0, :] - second[..., 1, :], first[..., 1, :] + second[..., 0, :]), axis=-2
    )


def across_z(values):
    return lax.all_to_all(values, "gz", split_axis=0, concat_axis=0, tiled=True)


def across_y(values):
    return lax.all_to_all(values, "gy", split_axis=0, concat_axis=0, tiled=True)


def forward_zfirst(field, ahead, y_fwd, z_fwd):
    z_local, y_local, x_len = field.shape
    z_devs = lax.axis_size("gz")
    y_devs = lax.axis_size("gy")
    x_share = ahead.shape[2] // z_devs
    z_len = z_local * z_devs
    y_len = y_local * y_devs
    z_share = z_len // y_devs
    values = product("zyx,xrgq->gzyrq", field, ahead.reshape(x_len, 2, z_devs, x_share))
    values = across_z(values).reshape(z_len, y_local, 2, x_share)
    values = turn("zyrq,zgk->gykrq", values, shaped(z_fwd, (z_len, y_devs, z_share)), True)
    values = across_y(values).reshape(y_len, z_share, 2, x_share)
    return turn("yjrq,yk->kjrq", values, y_fwd, True)


def inverse_zfirst(spectrum, behind, y_back, z_back, z_local, y_local):
    z_devs = lax.axis_size("gz")
    y_devs = lax.axis_size("gy")
    y_len, z_share, pair, x_share = spectrum.shape
    x_len = behind.shape[2]
    values = turn("kjrq,kgy->gyjrq", spectrum, shaped(y_back, (y_len, y_devs, y_local)), False)
    values = across_y(values)
    values = turn(
        "syjrq,sjgz->gzyrq", values, shaped(z_back, (y_devs, z_share, z_devs, z_local)), False
    )
    values = across_z(values)
    return product("szyrq,rsqx->zyx", values, behind.reshape(2, z_devs, x_share, x_len))


def gains_zfirst(transfer_real, transfer_imag):
    z_local, y_local, half = transfer_real.shape
    z_devs = lax.axis_size("gz")
    y_devs = lax.axis_size("gy")
    x_share = half // z_devs
    z_len = z_local * z_devs
    z_share = z_len // y_devs
    stacked = (
        jnp.stack((transfer_real, transfer_imag), axis=2)
        .reshape(z_local, y_local, 2, z_devs, x_share)
        .transpose(3, 0, 1, 2, 4)
    )
    stacked = (
        across_z(stacked).reshape(y_devs, z_share, y_local, 2, x_share).transpose(0, 2, 1, 3, 4)
    )
    return across_y(stacked).reshape(y_local * y_devs, z_share, 2, x_share)


def apply_gains(spectrum, gains, conjugate):
    spec_real = spectrum[..., 0, :]
    spec_imag = spectrum[..., 1, :]
    gain_real = gains[..., 0, :]
    gain_imag = gains[..., 1, :]
    if conjugate:
        return jnp.stack(
            (
                spec_real * gain_real + spec_imag * gain_imag,
                spec_imag * gain_real - spec_real * gain_imag,
            ),
            axis=-2,
        )
    return jnp.stack(
        (
            spec_real * gain_real - spec_imag * gain_imag,
            spec_real * gain_imag + spec_imag * gain_real,
        ),
        axis=-2,
    )


def on_device_rows(measured, transfer_real, transfer_imag):
    z_local, y_local, x_len = measured.shape
    z_len = z_local * lax.axis_size("gz")
    y_len = y_local * lax.axis_size("gy")
    ahead, behind = half_tables(x_len)
    y_fwd, y_back = square_tables(y_len)
    z_fwd, z_back = square_tables(z_len)
    soft_x = blur_local(behind, 2)
    soft_y = (blur_local(y_back[0], 1), blur_local(y_back[1], 1))
    soft_z = (blur_local(z_back[0], 1), blur_local(z_back[1], 1))
    gains = gains_zfirst(transfer_real, transfer_imag)
    estimate = measured
    for iteration in range(ITERS):
        spectrum = forward_zfirst(estimate, ahead, y_fwd, z_fwd)
        blurred = inverse_zfirst(
            apply_gains(spectrum, gains, False), behind, y_back, z_back, z_local, y_local
        )
        ratio = measured / jnp.maximum(blurred, FLOOR)
        spectrum = forward_zfirst(ratio, ahead, y_fwd, z_fwd)
        correction = inverse_zfirst(
            apply_gains(spectrum, gains, True), soft_x, soft_y, soft_z, z_local, y_local
        )
        estimate = estimate * correction
    return estimate


LANES = 128
SUBLANES = 8


def gauss_weights_np():
    offsets = np.arange(-RADIUS, RADIUS + 1).astype(np.float64)
    weights = np.exp(-offsets * offsets / (2.0 * SIGMA * SIGMA))
    return weights / weights.sum()


def smooth_np(table, axis):
    weights = gauss_weights_np()
    widths = [(0, 0)] * table.ndim
    widths[axis] = (RADIUS, RADIUS)
    padded = np.pad(table, widths)
    length = table.shape[axis]
    return sum(
        weights[j] * np.take(padded, np.arange(j, j + length), axis=axis)
        for j in range(2 * RADIUS + 1)
    )


def two_terms(table):
    high = table.astype(np.float32).astype(jnp.bfloat16)
    low = (table - high.astype(np.float64)).astype(np.float32).astype(jnp.bfloat16)
    return np.stack((high, low))


def phase_np(first, second, length):
    return 2.0 * np.pi * ((first[:, None] * second[None, :]) % length) / length


def x_tables(length):
    half = length // 2
    where = np.arange(length)
    ahead, behind = [], []
    for odd in range(2):
        k = 2 * np.arange(half // 2) + odd
        angle = phase_np(k, where, length)
        ahead.append(np.concatenate((np.cos(angle), -np.sin(angle)), axis=0)[:, :half])
        weight = (np.where(k == 0, 1.0, 2.0) / length)[:, None]
        behind.append(np.concatenate((weight * np.cos(angle), -weight * np.sin(angle)), axis=0))
    sharp = np.stack([table[:, :half] for table in behind])
    soft = smooth_np(np.concatenate(behind, axis=0), 1)
    return two_terms(np.stack(ahead)), two_terms(sharp), two_terms(soft)


def y_tables(length):
    half = length // 2
    where = np.arange(length)
    ahead, sharp, soft = [], [], []
    for odd in range(2):
        k = 2 * np.arange(half) + odd
        angle = phase_np(where, k, length)
        cosine, sine = np.cos(angle), np.sin(angle)
        ahead.append(np.concatenate((cosine[:half], sine[:half]), axis=1))
        cosine, sine = cosine.T / length, sine.T / length
        sharp.append(np.concatenate((cosine[:, :half], sine[:, :half]), axis=1))
        soft.append(np.concatenate((smooth_np(cosine, 1), smooth_np(sine, 1)), axis=1))
    return two_terms(np.stack(ahead)), two_terms(np.stack(sharp)), two_terms(np.concatenate(soft))


def z_tables(length):
    where = np.arange(length)
    angle = phase_np(where, where, length)
    cosine, sine = np.cos(angle), np.sin(angle)
    ahead = np.block([[cosine, sine], [-sine, cosine]])
    cosine, sine = cosine / length, sine / length
    sharp = np.block([[cosine, -sine], [sine, cosine]])
    cosine, sine = smooth_np(cosine, 0), smooth_np(sine, 0)
    soft = np.block([[cosine, -sine], [sine, cosine]])
    return two_terms(ahead), two_terms(sharp), two_terms(soft)


def parity_pick(length):
    order = np.concatenate((np.arange(0, length, 2), np.arange(1, length, 2)))
    return np.eye(length, dtype=np.float32)[:, order].astype(jnp.bfloat16)


def dot(left, right):
    return jnp.dot(left, right, preferred_element_type=jnp.float32)


def split_terms(values):
    high = values.astype(jnp.bfloat16)
    return high, (values - high.astype(jnp.float32)).astype(jnp.bfloat16)


def table_times(high, low, values):
    first, second = split_terms(values)
    return dot(
        jnp.concatenate((high, high, low), axis=1), jnp.concatenate((first, second, first), axis=0)
    )


def times_table(values, high, low):
    first, second = split_terms(values)
    return dot(
        jnp.concatenate((first, second, first), axis=1), jnp.concatenate((high, high, low), axis=0)
    )


def table_times_lines(high, low, values):
    first, second = split_terms(values)
    return lax.dot_general(
        jnp.concatenate((high, high, low), axis=1),
        jnp.concatenate((first, second, first), axis=1),
        (((1,), (1,)), ((), ())),
        preferred_element_type=jnp.float32,
    )


def lines_of(values, high, low):
    return times_table(values.T, high, low)


def swapped(blocks):
    row = lax.broadcasted_iota(jnp.int32, blocks[0].shape, 1)
    blocks = list(blocks)
    for step in (1, 2, 4):
        upper = (row & step) == 0
        for i in range(SUBLANES):
            if i & step == 0:
                a, b = blocks[i], blocks[i + step]
                blocks[i] = jnp.where(upper, a, pltpu.roll(b, step, 1))
                blocks[i + step] = jnp.where(upper, pltpu.roll(a, SUBLANES - step, 1), b)
    return blocks


def load_lines(got_ref, tile):
    half = got_ref.shape[0] * got_ref.shape[1] // 2
    parts = []
    for part in range(2):
        blocks = swapped([got_ref[:, i, part, tile] for i in range(SUBLANES)])
        parts.append(jnp.concatenate([b.reshape(-1, LANES) for b in blocks], axis=1))
    return [
        jnp.concatenate([p[odd * half : (odd + 1) * half] for p in parts], axis=0)
        for odd in range(2)
    ]


def store_lines(send_ref, tile, parities):
    devs = send_ref.shape[0]
    half = devs * send_ref.shape[1] // 2
    for part in range(2):
        values = jnp.concatenate([p[part * half : (part + 1) * half] for p in parities], axis=0)
        blocks = [
            values[:, z * LANES : (z + 1) * LANES].reshape(devs, SUBLANES, LANES)
            for z in range(SUBLANES)
        ]
        for i, block in enumerate(swapped(blocks)):
            send_ref[:, i, part, tile] = block


def lines_back_sharp(got_ref, tile, x_ref):
    even, odd = load_lines(got_ref, tile)
    even = lines_of(even, x_ref[0, 0], x_ref[1, 0])
    odd = lines_of(odd, x_ref[0, 1], x_ref[1, 1])
    return even + odd, even - odd


def lines_back_soft(got_ref, tile, x_ref):
    both = lines_of(jnp.concatenate(load_lines(got_ref, tile), axis=0), x_ref[0], x_ref[1])
    half = both.shape[1] // 2
    return both[:, :half], both[:, half:]


def lines_ahead(left, right, send_ref, tile, x_ref):
    even = table_times_lines(x_ref[0, 0], x_ref[1, 0], left + right)
    odd = table_times_lines(x_ref[0, 1], x_ref[1, 1], left - right)
    store_lines(send_ref, tile, (even, odd))


def halves(volume_ref, tile):
    half = volume_ref.shape[2] // 2
    rows = slice(tile * LANES, (tile + 1) * LANES)
    return (
        volume_ref[:, rows, :half].reshape(-1, half),
        volume_ref[:, rows, half:].reshape(-1, half),
    )


def store_halves(volume_ref, tile, left, right):
    half = volume_ref.shape[2] // 2
    rows = slice(tile * LANES, (tile + 1) * LANES)
    shape = (volume_ref.shape[0], LANES, half)
    volume_ref[:, rows, :half] = left.reshape(shape)
    volume_ref[:, rows, half:] = right.reshape(shape)


def first_kernel(volume_ref, xa_ref, send_ref):
    for tile in range(send_ref.shape[3]):
        left, right = halves(volume_ref, tile)
        lines_ahead(left, right, send_ref, tile, xa_ref)


def ratio_kernel(got_ref, measured_ref, xb_ref, xa_ref, send_ref):
    for tile in range(got_ref.shape[3]):
        left, right = lines_back_sharp(got_ref, tile, xb_ref)
        over_left, over_right = halves(measured_ref, tile)
        left = over_left / jnp.maximum(left, FLOOR)
        right = over_right / jnp.maximum(right, FLOOR)
        lines_ahead(left, right, send_ref, tile, xa_ref)


def correct_kernel(got_ref, estimate_ref, xb_ref, xa_ref, send_ref, out_ref):
    for tile in range(got_ref.shape[3]):
        left, right = lines_back_soft(got_ref, tile, xb_ref)
        old_left, old_right = halves(estimate_ref, tile)
        left, right = old_left * left, old_right * right
        store_halves(out_ref, tile, left, right)
        lines_ahead(left, right, send_ref, tile, xa_ref)


def last_kernel(got_ref, estimate_ref, xb_ref, out_ref):
    for tile in range(got_ref.shape[3]):
        left, right = lines_back_soft(got_ref, tile, xb_ref)
        old_left, old_right = halves(estimate_ref, tile)
        store_halves(out_ref, tile, old_left * left, old_right * right)


def picked(values, pick):
    first, second = split_terms(values)
    rest = values - first.astype(jnp.float32) - second.astype(jnp.float32)
    return dot(first, pick) + dot(second, pick) + dot(rest.astype(jnp.bfloat16), pick)


def arrange_kernel(real_ref, imag_ref, pick_x_ref, pick_y_ref, send_ref):
    z_len, _, kx_len = real_ref.shape
    tiles = send_ref.shape[2]
    flat = send_ref.reshape(kx_len * 2 * tiles * z_len, LANES)
    for part, ref in enumerate((real_ref, imag_ref)):
        for z in range(z_len):
            values = picked(picked(ref[z], pick_x_ref[...]).T, pick_y_ref[...])
            for tile in range(tiles):
                start = (part * tiles + tile) * z_len + z
                flat[pl.ds(start, kx_len, 2 * tiles * z_len), :] = values[
                    :, tile * LANES : (tile + 1) * LANES
                ]


def plane_of(ref, k, part, tiles):
    pieces = [
        ref[:, g, k, part, tile].reshape(-1, LANES) for g in range(ref.shape[1]) for tile in tiles
    ]
    return jnp.concatenate(pieces, axis=1)


def turned_ahead(both):
    rows, half = both.shape[0] // 2, both.shape[1] // 2
    return (
        both[:rows, :half] + both[rows:, half:],
        both[rows:, :half] - both[:rows, half:],
    )


def turned_back(both):
    rows, half = both.shape[0] // 2, both.shape[1] // 2
    return (
        both[:rows, :half] - both[rows:, half:],
        both[rows:, :half] + both[:rows, half:],
    )


def gain_kernel(adjoint, at_once, got_ref, *refs):
    @pl.loop(0, got_ref.shape[2] // at_once)
    def _(step):
        gain_planes(adjoint, at_once, step * at_once, got_ref, *refs)


def gain_planes(
    adjoint, share, base, got_ref, gain_ref, ya_ref, za_ref, zb_ref, yb_ref, send_ref
):
    z_devs, y_devs, _, _, tiles, z_local, _ = got_ref.shape
    rows = 2 * z_devs * z_local
    half = y_devs * tiles * LANES // 2

    def by_kx(values):
        return [values[k * rows : (k + 1) * rows] for k in range(share)]

    values = jnp.concatenate(
        [plane_of(got_ref, base + k, part, range(tiles)) for k in range(share) for part in range(2)],
        axis=0,
    )
    left, right = values[:, :half], values[:, half:]
    evens = by_kx(times_table(left + right, ya_ref[0, 0], ya_ref[1, 0]))
    odds = by_kx(times_table(left - right, ya_ref[0, 1], ya_ref[1, 1]))
    planes = []
    for k in range(share):
        even, odd = turned_ahead(evens[k]), turned_ahead(odds[k])
        values = jnp.concatenate(
            [jnp.concatenate((even[part], odd[part]), axis=1) for part in range(2)], axis=0
        )
        values = table_times(za_ref[0], za_ref[1], values)
        real, imag = values[: rows // 2], values[rows // 2 :]
        gain_real, gain_imag = [
            jnp.concatenate(
                (
                    plane_of(gain_ref, base + k, part, range(tiles // 2)),
                    plane_of(gain_ref, base + k, part, range(tiles // 2, tiles)),
                ),
                axis=1,
            )
            for part in range(2)
        ]
        if adjoint:
            turned = (real * gain_real + imag * gain_imag, imag * gain_real - real * gain_imag)
        else:
            turned = (real * gain_real - imag * gain_imag, real * gain_imag + imag * gain_real)
        planes.append(table_times(zb_ref[0], zb_ref[1], jnp.concatenate(turned, axis=0)))
    values = jnp.concatenate(planes, axis=0)
    if adjoint:
        boths = by_kx(times_table(values, yb_ref[0], yb_ref[1]))
    else:
        evens = by_kx(times_table(values[:, :half], yb_ref[0, 0], yb_ref[1, 0]))
        odds = by_kx(times_table(values[:, half:], yb_ref[0, 1], yb_ref[1, 1]))
    for k in range(share):
        if adjoint:
            parts = turned_back(boths[k])
        else:
            even, odd = turned_back(evens[k]), turned_back(odds[k])
            parts = [jnp.concatenate((a + b, a - b), axis=1) for a, b in zip(even, odd)]
        for part in range(2):
            for g in range(y_devs):
                for tile in range(tiles):
                    low = (g * tiles + tile) * LANES
                    send_ref[:, g, base + k, part, tile] = parts[part][:, low : low + LANES].reshape(
                        z_devs, z_local, LANES
                    )


KX_AT_ONCE = 4
VMEM_BYTES = 32 * 2**20


def call(kernel, arrays, outs, flops, name):
    leaves = (*arrays, *jax.tree.leaves(outs))
    moved = sum(math.prod(a.shape) * a.dtype.itemsize for a in leaves)
    spec = pl.BlockSpec(memory_space=pltpu.VMEM)
    return pl.pallas_call(
        kernel,
        in_specs=[spec] * len(arrays),
        out_specs=jax.tree.map(lambda _: spec, outs),
        out_shape=outs,
        compiler_params=pltpu.CompilerParams(vmem_limit_bytes=VMEM_BYTES),
        cost_estimate=pl.CostEstimate(flops=flops, bytes_accessed=moved, transcendentals=0),
        name=name,
    )(*arrays)


def exchange(values):
    return lax.all_to_all(values, ("gz", "gy"), split_axis=0, concat_axis=0, tiled=True)


def on_device_lines(measured, transfer_real, transfer_imag):
    z_devs, y_devs = lax.axis_size("gz"), lax.axis_size("gy")
    devs = z_devs * y_devs
    z_local, y_local, x_len = measured.shape
    z_len, y_len, kx_len = z_local * z_devs, y_local * y_devs, x_len // 2
    tiles, share = y_local // LANES, kx_len // devs
    xa, xb, xs = (jnp.asarray(t) for t in x_tables(x_len))
    ya, yb, ys = (jnp.asarray(t) for t in y_tables(y_len))
    za, zb, zs = (jnp.asarray(t) for t in z_tables(z_len))
    pick_x, pick_y = (jnp.asarray(parity_pick(n)) for n in (kx_len, y_local))

    spectrum = jax.ShapeDtypeStruct((devs, share, 2, tiles, z_local, LANES), jnp.float32)
    volume = jax.ShapeDtypeStruct(measured.shape, jnp.float32)
    line_flops = 3 * z_local * y_local * x_len * x_len

    def first(values):
        return call(first_kernel, (values, xa), spectrum, line_flops, "first")

    def ratio(got, values):
        return call(ratio_kernel, (got, values, xb, xa), spectrum, 2 * line_flops, "ratio")

    def correct(got, values):
        return call(
            correct_kernel, (got, values, xs, xa), (spectrum, volume), 3 * line_flops, "correct"
        )

    def last(got, values):
        return call(last_kernel, (got, values, xs), volume, 2 * line_flops, "last")

    planes = (z_devs, y_devs, *spectrum.shape[1:])
    at_once = KX_AT_ONCE if share % KX_AT_ONCE == 0 else 1

    def filtered(got, gains, adjoint):
        return call(
            functools.partial(gain_kernel, adjoint, at_once),
            (got.reshape(planes), gains.reshape(planes), ya, za, *((zs, ys) if adjoint else (zb, yb))),
            jax.ShapeDtypeStruct(planes, jnp.float32),
            3 * 8 * share * z_len * y_len * (2 * z_len + y_len),
            "adjoint" if adjoint else "blur",
        ).reshape(spectrum.shape)

    def arranged(transfer_real, transfer_imag):
        return call(
            arrange_kernel, (transfer_real, transfer_imag, pick_x, pick_y),
            jax.ShapeDtypeStruct((kx_len, *spectrum.shape[2:]), jnp.float32),
            3 * 4 * z_local * y_local * kx_len * (y_local + kx_len), "arrange",
        ).reshape(spectrum.shape)

    send = first(measured)
    send, transfer_real, transfer_imag = lax.optimization_barrier(
        (send, transfer_real, transfer_imag)
    )
    send = exchange(send)
    gains = exchange(arranged(transfer_real, transfer_imag))
    estimate = measured
    for iteration in range(ITERS):
        send = ratio(exchange(filtered(send, gains, False)), measured)
        send = exchange(filtered(exchange(send), gains, True))
        if iteration < ITERS - 1:
            send, estimate = correct(send, estimate)
            send = exchange(send)
    return last(send, estimate)


def lines_fit(mesh, shape):
    z_devs, y_devs = mesh.shape["gz"], mesh.shape["gy"]
    z_len, y_len, x_len = shape
    return (
        z_len % LANES == 0
        and z_len // z_devs == SUBLANES
        and y_len % (2 * LANES * y_devs) == 0
        and x_len % (4 * LANES) == 0
        and x_len // 2 == SUBLANES * z_devs * y_devs
    )


def solution(mesh):
    def run(measured, transfer_real, transfer_imag):
        spec = P("gz", "gy", None)
        fits = lines_fit(mesh, measured.shape)
        return jax.shard_map(
            on_device_lines if fits else on_device_rows,
            mesh=mesh,
            in_specs=(spec, spec, spec),
            out_specs=spec,
            check_vma=False,
        )(measured, transfer_real, transfer_imag)

    return run
```

```python
import functools
import math

import jax
import jax.numpy as jnp
import numpy as np
from jax import lax
from jax.experimental import pallas as pl
from jax.experimental.pallas import tpu as pltpu
from jax.sharding import PartitionSpec as P

ITERS = 2
RADIUS = 4


SIGMA = 1.5
FLOOR = 0.1


def product(form, left, right):
    return jnp.einsum(
        form, left, right, precision=lax.Precision.HIGHEST, preferred_element_type=jnp.float32
    )


def gauss_weights():
    offsets = jnp.arange(-RADIUS, RADIUS + 1).astype(jnp.float32)
    weights = jnp.exp(-offsets * offsets / (2.0 * SIGMA * SIGMA))
    return weights / jnp.sum(weights)


def taps_along(padded, axis, length):
    weights = gauss_weights()
    total = weights[0] * lax.slice_in_dim(padded, 0, length, axis=axis)
    for offset in range(1, 2 * RADIUS + 1):
        total = total + weights[offset] * lax.slice_in_dim(
            padded, offset, offset + length, axis=axis
        )
    return total


def blur_local(values, axis):
    length = values.shape[axis]
    widths = [(0, 0)] * values.ndim
    widths[axis] = (RADIUS, RADIUS)
    return taps_along(jnp.pad(values, widths), axis, length)


def angles(length, count):
    position = jnp.arange(length, dtype=jnp.int32)
    frequency = jnp.arange(count, dtype=jnp.int32)
    phase = position[:, None] * frequency[None, :] % length
    return phase.astype(jnp.float32) * (2.0 * math.pi / length)


def square_tables(length):
    angle = angles(length, length)
    cosine = jnp.cos(angle)
    sine = jnp.sin(angle)
    return ((cosine, sine), (cosine / length, sine / length))


def half_tables(length):
    half = length // 2
    angle = angles(length, half)
    cosine = jnp.cos(angle)
    sine = jnp.sin(angle)
    ahead = jnp.stack((cosine, -sine), axis=1)
    weight = jnp.where(jnp.arange(half) == 0, 1.0, 2.0).astype(jnp.float32) / length
    behind = jnp.stack((weight[:, None] * cosine.T, -weight[:, None] * sine.T), axis=0)
    return (ahead, behind)


def shaped(table, shape):
    return (table[0].reshape(shape), table[1].reshape(shape))


def turn(form, values, table, forward):
    first = product(form, values, table[0])
    second = product(form, values, table[1])
    if forward:
        return jnp.stack(
            (first[..., 0, :] + second[..., 1, :], first[..., 1, :] - second[..., 0, :]), axis=-2
        )
    return jnp.stack(
        (first[..., 0, :] - second[..., 1, :], first[..., 1, :] + second[..., 0, :]), axis=-2
    )


def across_z(values):
    return lax.all_to_all(values, "gz", split_axis=0, concat_axis=0, tiled=True)


def across_y(values):
    return lax.all_to_all(values, "gy", split_axis=0, concat_axis=0, tiled=True)


def forward_zfirst(field, ahead, y_fwd, z_fwd):
    z_local, y_local, x_len = field.shape
    z_devs = lax.axis_size("gz")
    y_devs = lax.axis_size("gy")
    x_share = ahead.shape[2] // z_devs
    z_len = z_local * z_devs
    y_len = y_local * y_devs
    z_share = z_len // y_devs
    values = product("zyx,xrgq->gzyrq", field, ahead.reshape(x_len, 2, z_devs, x_share))
    values = across_z(values).reshape(z_len, y_local, 2, x_share)
    values = turn("zyrq,zgk->gykrq", values, shaped(z_fwd, (z_len, y_devs, z_share)), True)
    values = across_y(values).reshape(y_len, z_share, 2, x_share)
    return turn("yjrq,yk->kjrq", values, y_fwd, True)


def inverse_zfirst(spectrum, behind, y_back, z_back, z_local, y_local):
    z_devs = lax.axis_size("gz")
    y_devs = lax.axis_size("gy")
    y_len, z_share, pair, x_share = spectrum.shape
    x_len = behind.shape[2]
    values = turn("kjrq,kgy->gyjrq", spectrum, shaped(y_back, (y_len, y_devs, y_local)), False)
    values = across_y(values)
    values = turn(
        "syjrq,sjgz->gzyrq", values, shaped(z_back, (y_devs, z_share, z_devs, z_local)), False
    )
    values = across_z(values)
    return product("szyrq,rsqx->zyx", values, behind.reshape(2, z_devs, x_share, x_len))


def gains_zfirst(transfer_real, transfer_imag):
    z_local, y_local, half = transfer_real.shape
    z_devs = lax.axis_size("gz")
    y_devs = lax.axis_size("gy")
    x_share = half // z_devs
    z_len = z_local * z_devs
    z_share = z_len // y_devs
    stacked = (
        jnp.stack((transfer_real, transfer_imag), axis=2)
        .reshape(z_local, y_local, 2, z_devs, x_share)
        .transpose(3, 0, 1, 2, 4)
    )
    stacked = (
        across_z(stacked).reshape(y_devs, z_share, y_local, 2, x_share).transpose(0, 2, 1, 3, 4)
    )
    return across_y(stacked).reshape(y_local * y_devs, z_share, 2, x_share)


def apply_gains(spectrum, gains, conjugate):
    spec_real = spectrum[..., 0, :]
    spec_imag = spectrum[..., 1, :]
    gain_real = gains[..., 0, :]
    gain_imag = gains[..., 1, :]
    if conjugate:
        return jnp.stack(
            (
                spec_real * gain_real + spec_imag * gain_imag,
                spec_imag * gain_real - spec_real * gain_imag,
            ),
            axis=-2,
        )
    return jnp.stack(
        (
            spec_real * gain_real - spec_imag * gain_imag,
            spec_real * gain_imag + spec_imag * gain_real,
        ),
        axis=-2,
    )


def on_device_rows(measured, transfer_real, transfer_imag):
    z_local, y_local, x_len = measured.shape
    z_len = z_local * lax.axis_size("gz")
    y_len = y_local * lax.axis_size("gy")
    ahead, behind = half_tables(x_len)
    y_fwd, y_back = square_tables(y_len)
    z_fwd, z_back = square_tables(z_len)
    soft_x = blur_local(behind, 2)
    soft_y = (blur_local(y_back[0], 1), blur_local(y_back[1], 1))
    soft_z = (blur_local(z_back[0], 1), blur_local(z_back[1], 1))
    gains = gains_zfirst(transfer_real, transfer_imag)
    estimate = measured
    for iteration in range(ITERS):
        spectrum = forward_zfirst(estimate, ahead, y_fwd, z_fwd)
        blurred = inverse_zfirst(
            apply_gains(spectrum, gains, False), behind, y_back, z_back, z_local, y_local
        )
        ratio = measured / jnp.maximum(blurred, FLOOR)
        spectrum = forward_zfirst(ratio, ahead, y_fwd, z_fwd)
        correction = inverse_zfirst(
            apply_gains(spectrum, gains, True), soft_x, soft_y, soft_z, z_local, y_local
        )
        estimate = estimate * correction
    return estimate


LANES = 128
SUBLANES = 8


def gauss_weights_np():
    offsets = np.arange(-RADIUS, RADIUS + 1).astype(np.float64)
    weights = np.exp(-offsets * offsets / (2.0 * SIGMA * SIGMA))
    return weights / weights.sum()


def smooth_np(table, axis):
    weights = gauss_weights_np()
    widths = [(0, 0)] * table.ndim
    widths[axis] = (RADIUS, RADIUS)
    padded = np.pad(table, widths)
    length = table.shape[axis]
    return sum(
        weights[j] * np.take(padded, np.arange(j, j + length), axis=axis)
        for j in range(2 * RADIUS + 1)
    )


def two_terms(table):
    high = table.astype(np.float32).astype(jnp.bfloat16)
    low = (table - high.astype(np.float64)).astype(np.float32).astype(jnp.bfloat16)
    return np.stack((high, low))


def phase_np(first, second, length):
    return 2.0 * np.pi * ((first[:, None] * second[None, :]) % length) / length


def x_tables(length):
    half = length // 2
    where = np.arange(length)
    ahead, behind = [], []
    for odd in range(2):
        k = 2 * np.arange(half // 2) + odd
        angle = phase_np(k, where, length)
        ahead.append(np.concatenate((np.cos(angle), -np.sin(angle)), axis=0)[:, :half])
        weight = (np.where(k == 0, 1.0, 2.0) / length)[:, None]
        behind.append(np.concatenate((weight * np.cos(angle), -weight * np.sin(angle)), axis=0))
    sharp = np.stack([table[:, :half] for table in behind])
    soft = smooth_np(np.concatenate(behind, axis=0), 1)
    return two_terms(np.stack(ahead)), two_terms(sharp), two_terms(soft)


def y_order(length, rest):
    quarter = length // 4
    return 4 * ((np.arange(quarter) + (rest % 2) * (quarter // 2)) % quarter) + rest


def y_tables(length):
    quarter = length // 4
    where = np.arange(length)
    ahead, sharp, soft, edges = [], [], [], []
    weights = gauss_weights_np()
    for rest in range(4):
        angle = phase_np(where, y_order(length, rest), length)
        cosine, sine = np.cos(angle), np.sin(angle)
        ahead.append(np.concatenate((cosine[:quarter], sine[:quarter]), axis=1))
        exact, round_trip, edge = [], [], []
        for table in (cosine.T / length, sine.T / length):
            around = sum(
                weights[j] * np.roll(table, RADIUS - j, axis=1) for j in range(2 * RADIUS + 1)
            )
            over = around - smooth_np(table, 1)
            exact.append(table[:, :quarter])
            round_trip.append(around[:, :quarter])
            edge += [over[:, : quarter // 2], over[:, -(quarter // 2) :]]
        sharp.append(np.concatenate(exact, axis=1))
        soft.append(np.concatenate(round_trip, axis=1))
        edges.append(np.concatenate(edge, axis=1))
    return [two_terms(np.stack(t)) for t in (ahead, sharp, soft)] + [
        two_terms(np.concatenate(edges))
    ]


def z_tables(length):
    where = np.arange(length)
    angle = phase_np(where, where, length)
    cosine, sine = np.cos(angle), np.sin(angle)
    ahead = np.block([[cosine, sine], [-sine, cosine]])
    cosine, sine = cosine / length, sine / length
    sharp = np.block([[cosine, -sine], [sine, cosine]])
    cosine, sine = smooth_np(cosine, 0), smooth_np(sine, 0)
    soft = np.block([[cosine, -sine], [sine, cosine]])
    return two_terms(ahead), two_terms(sharp), two_terms(soft)


def pick_of(order):
    return np.eye(len(order), dtype=np.float32)[:, np.asarray(order)].astype(jnp.bfloat16)


def pick_x_table(length):
    return pick_of(np.concatenate((np.arange(0, length, 2), np.arange(1, length, 2))))


def pick_y_tables(length):
    by_rest = [np.arange(rest, length, 4) for rest in range(4)]
    orders = ((0, 1, 2, 3), (1, 0, 3, 2))
    return np.stack([pick_of(np.concatenate([by_rest[r] for r in order])) for order in orders])


def dot(left, right):
    return jnp.dot(left, right, preferred_element_type=jnp.float32)


def split_terms(values):
    high = values.astype(jnp.bfloat16)
    return high, (values - high.astype(jnp.float32)).astype(jnp.bfloat16)


def table_times(high, low, values):
    first, second = split_terms(values)
    return dot(
        jnp.concatenate((high, high, low), axis=1), jnp.concatenate((first, second, first), axis=0)
    )


def times_table(values, high, low):
    first, second = split_terms(values)
    return dot(
        jnp.concatenate((first, second, first), axis=1), jnp.concatenate((high, high, low), axis=0)
    )


def table_times_lines(high, low, values):
    first, second = split_terms(values)
    return lax.dot_general(
        jnp.concatenate((high, high, low), axis=1),
        jnp.concatenate((first, second, first), axis=1),
        (((1,), (1,)), ((), ())),
        preferred_element_type=jnp.float32,
    )


def lines_of(values, high, low):
    return times_table(values.T, high, low)


def swapped(blocks):
    row = lax.broadcasted_iota(jnp.int32, blocks[0].shape, 1)
    blocks = list(blocks)
    for step in (1, 2, 4):
        upper = (row & step) == 0
        for i in range(SUBLANES):
            if i & step == 0:
                a, b = blocks[i], blocks[i + step]
                blocks[i] = jnp.where(upper, a, pltpu.roll(b, step, 1))
                blocks[i + step] = jnp.where(upper, pltpu.roll(a, SUBLANES - step, 1), b)
    return blocks


def load_lines(got_ref, tile):
    half = got_ref.shape[0] * got_ref.shape[1] // 2
    parts = []
    for part in range(2):
        blocks = swapped([got_ref[:, i, part, tile] for i in range(SUBLANES)])
        parts.append(jnp.concatenate([b.reshape(-1, LANES) for b in blocks], axis=1))
    return [
        jnp.concatenate([p[odd * half : (odd + 1) * half] for p in parts], axis=0)
        for odd in range(2)
    ]


def store_lines(send_ref, tile, parities):
    devs = send_ref.shape[0]
    half = devs * send_ref.shape[1] // 2
    for part in range(2):
        values = jnp.concatenate([p[part * half : (part + 1) * half] for p in parities], axis=0)
        blocks = [
            values[:, z * LANES : (z + 1) * LANES].reshape(devs, SUBLANES, LANES)
            for z in range(SUBLANES)
        ]
        for i, block in enumerate(swapped(blocks)):
            send_ref[:, i, part, tile] = block


def lines_back_sharp(got_ref, tile, x_ref):
    even, odd = load_lines(got_ref, tile)
    even = lines_of(even, x_ref[0, 0], x_ref[1, 0])
    odd = lines_of(odd, x_ref[0, 1], x_ref[1, 1])
    return even + odd, even - odd


def lines_back_soft(got_ref, tile, x_ref):
    both = lines_of(jnp.concatenate(load_lines(got_ref, tile), axis=0), x_ref[0], x_ref[1])
    half = both.shape[1] // 2
    return both[:, :half], both[:, half:]


def lines_ahead(left, right, send_ref, tile, x_ref):
    even = table_times_lines(x_ref[0, 0], x_ref[1, 0], left + right)
    odd = table_times_lines(x_ref[0, 1], x_ref[1, 1], left - right)
    store_lines(send_ref, tile, (even, odd))


def halves(volume_ref, tile):
    half = volume_ref.shape[2] // 2
    rows = slice(tile * LANES, (tile + 1) * LANES)
    return (
        volume_ref[:, rows, :half].reshape(-1, half),
        volume_ref[:, rows, half:].reshape(-1, half),
    )


def store_halves(volume_ref, tile, left, right):
    half = volume_ref.shape[2] // 2
    rows = slice(tile * LANES, (tile + 1) * LANES)
    shape = (volume_ref.shape[0], LANES, half)
    volume_ref[:, rows, :half] = left.reshape(shape)
    volume_ref[:, rows, half:] = right.reshape(shape)


def first_kernel(volume_ref, xa_ref, send_ref):
    for tile in range(send_ref.shape[3]):
        left, right = halves(volume_ref, tile)
        lines_ahead(left, right, send_ref, tile, xa_ref)


def ratio_kernel(got_ref, measured_ref, xb_ref, xa_ref, send_ref):
    for tile in range(got_ref.shape[3]):
        left, right = lines_back_sharp(got_ref, tile, xb_ref)
        over_left, over_right = halves(measured_ref, tile)
        left = over_left / jnp.maximum(left, FLOOR)
        right = over_right / jnp.maximum(right, FLOOR)
        lines_ahead(left, right, send_ref, tile, xa_ref)


def correct_kernel(got_ref, estimate_ref, xb_ref, xa_ref, send_ref, out_ref):
    for tile in range(got_ref.shape[3]):
        left, right = lines_back_soft(got_ref, tile, xb_ref)
        old_left, old_right = halves(estimate_ref, tile)
        left, right = old_left * left, old_right * right
        store_halves(out_ref, tile, left, right)
        lines_ahead(left, right, send_ref, tile, xa_ref)


def last_kernel(got_ref, estimate_ref, xb_ref, out_ref):
    for tile in range(got_ref.shape[3]):
        left, right = lines_back_soft(got_ref, tile, xb_ref)
        old_left, old_right = halves(estimate_ref, tile)
        store_halves(out_ref, tile, old_left * left, old_right * right)


def picked(values, pick):
    first, second = split_terms(values)
    rest = values - first.astype(jnp.float32) - second.astype(jnp.float32)
    return dot(first, pick) + dot(second, pick) + dot(rest.astype(jnp.bfloat16), pick)


def arrange_kernel(real_ref, imag_ref, pick_x_ref, pick_y_ref, send_ref):
    z_len, _, kx_len = real_ref.shape
    tiles = send_ref.shape[2]
    flat = send_ref.reshape(kx_len * 2 * tiles * z_len, LANES)
    for part, ref in enumerate((real_ref, imag_ref)):
        for z in range(z_len):
            values = picked(picked(ref[z], pick_x_ref[...]).T, pick_y_ref[...])
            for tile in range(tiles):
                start = (part * tiles + tile) * z_len + z
                flat[pl.ds(start, kx_len, 2 * tiles * z_len), :] = values[
                    :, tile * LANES : (tile + 1) * LANES
                ]


def turned_ahead(both):
    rows, half = both.shape[0] // 2, both.shape[1] // 2
    return (
        both[:rows, :half] + both[rows:, half:],
        both[rows:, :half] - both[:rows, half:],
    )


def turned_back(both):
    rows, half = both.shape[0] // 2, both.shape[1] // 2
    return (
        both[:rows, :half] - both[rows:, half:],
        both[rows:, :half] + both[:rows, half:],
    )


def gain_kernel(adjoint, at_once, got_ref, *refs):
    @pl.loop(0, got_ref.shape[2] // at_once)
    def _(step):
        gain_planes(adjoint, at_once, step * at_once, got_ref, *refs)


def quarters_of(ref, k, part):
    _, y_devs, _, _, tiles, _, _ = ref.shape
    return [ref[:, g, k, part, t].reshape(-1, LANES) for g in range(y_devs) for t in range(tiles)]


def gains_of(ref, k, part):
    first, second, third, fourth = quarters_of(ref, k, part)
    low = lax.broadcasted_iota(jnp.int32, first.shape, 1) < LANES // 2
    pairs = ((first, third), (third, first), (second, fourth), (fourth, second))
    return jnp.concatenate([jnp.where(low, a, b) for a, b in pairs], axis=1)


def gain_planes(
    adjoint, share, base, got_ref, gain_ref, ya_ref, za_ref, zb_ref, yb_ref, *rest_refs
):
    send_ref = rest_refs[-1]
    z_devs, y_devs, _, _, tiles, z_local, _ = got_ref.shape
    z_len = z_devs * z_local
    rows = 2 * z_len

    def by_kx(values):
        return [values[k * rows : (k + 1) * rows] for k in range(share)]

    inputs = [[], [], [], []]
    for k in range(share):
        real, imag = (quarters_of(got_ref, base + k, part) for part in range(2))
        even_real, even_imag = real[0] + real[2], imag[0] + imag[2]
        odd_real, odd_imag = real[1] + real[3], imag[1] + imag[3]
        inputs[0] += [even_real + odd_real, even_imag + odd_imag]
        inputs[2] += [even_real - odd_real, even_imag - odd_imag]
        even_real, even_imag = real[0] - real[2], imag[0] - imag[2]
        odd_real, odd_imag = real[1] - real[3], imag[1] - imag[3]
        inputs[1] += [even_real + odd_imag, even_imag - odd_real]
        inputs[3] += [even_real - odd_imag, even_imag + odd_real]
    turned = [
        by_kx(times_table(jnp.concatenate(inputs[r], axis=0), ya_ref[0, r], ya_ref[1, r]))
        for r in range(4)
    ]
    planes = []
    for k in range(share):
        pairs = [turned_ahead(turned[r][k]) for r in range(4)]
        values = jnp.concatenate(
            [jnp.concatenate([pair[part] for pair in pairs], axis=1) for part in range(2)], axis=0
        )
        values = table_times(za_ref[0], za_ref[1], values)
        real, imag = values[:z_len], values[z_len:]
        gain_real, gain_imag = (gains_of(gain_ref, base + k, part) for part in range(2))
        if adjoint:
            both = (real * gain_real + imag * gain_imag, imag * gain_real - real * gain_imag)
        else:
            both = (real * gain_real - imag * gain_imag, real * gain_imag + imag * gain_real)
        planes.append(table_times(zb_ref[0], zb_ref[1], jnp.concatenate(both, axis=0)))
    values = jnp.concatenate(planes, axis=0)
    turned = [
        by_kx(times_table(values[:, r * LANES : (r + 1) * LANES], yb_ref[0, r], yb_ref[1, r]))
        for r in range(4)
    ]
    if adjoint:
        edge_ref = rest_refs[0]
        edges = by_kx(times_table(values, edge_ref[0], edge_ref[1]))
    for k in range(share):
        pairs = [turned_back(turned[r][k]) for r in range(4)]
        even_real, even_imag = (pairs[0][part] + pairs[2][part] for part in range(2))
        odd_real, odd_imag = (pairs[1][part] + pairs[3][part] for part in range(2))
        outs = [None] * 4
        outs[0] = [even_real + odd_real, even_imag + odd_imag]
        outs[2] = [even_real - odd_real, even_imag - odd_imag]
        even_real, even_imag = (pairs[0][part] - pairs[2][part] for part in range(2))
        odd_real, odd_imag = (pairs[1][part] - pairs[3][part] for part in range(2))
        outs[1] = [even_real - odd_imag, even_imag + odd_real]
        outs[3] = [even_real + odd_imag, even_imag - odd_real]
        if adjoint:
            over = turned_back(edges[k])
            low = lax.broadcasted_iota(jnp.int32, over[0].shape, 1) < LANES // 2
            for part in range(2):
                outs[0][part] = outs[0][part] - jnp.where(low, over[part], 0.0)
                outs[3][part] = outs[3][part] - jnp.where(low, 0.0, over[part])
        for part in range(2):
            for j in range(4):
                send_ref[:, j // tiles, base + k, part, j % tiles] = outs[j][part].reshape(
                    z_devs, z_local, LANES
                )


KX_AT_ONCE = 4
VMEM_BYTES = 32 * 2**20


def call(kernel, arrays, outs, flops, name):
    leaves = (*arrays, *jax.tree.leaves(outs))
    moved = sum(math.prod(a.shape) * a.dtype.itemsize for a in leaves)
    spec = pl.BlockSpec(memory_space=pltpu.VMEM)
    return pl.pallas_call(
        kernel,
        in_specs=[spec] * len(arrays),
        out_specs=jax.tree.map(lambda _: spec, outs),
        out_shape=outs,
        compiler_params=pltpu.CompilerParams(vmem_limit_bytes=VMEM_BYTES),
        cost_estimate=pl.CostEstimate(flops=flops, bytes_accessed=moved, transcendentals=0),
        name=name,
    )(*arrays)


def exchange(values):
    return lax.all_to_all(values, ("gz", "gy"), split_axis=0, concat_axis=0, tiled=True)


def on_device_lines(measured, transfer_real, transfer_imag):
    z_devs, y_devs = lax.axis_size("gz"), lax.axis_size("gy")
    devs = z_devs * y_devs
    z_local, y_local, x_len = measured.shape
    z_len, y_len, kx_len = z_local * z_devs, y_local * y_devs, x_len // 2
    tiles, share = y_local // LANES, kx_len // devs
    xa, xb, xs = (jnp.asarray(t) for t in x_tables(x_len))
    ya, yb, ys, edges = (jnp.asarray(t) for t in y_tables(y_len))
    za, zb, zs = (jnp.asarray(t) for t in z_tables(z_len))
    pick_x = jnp.asarray(pick_x_table(kx_len))
    pick_y = lax.dynamic_index_in_dim(
        jnp.asarray(pick_y_tables(y_local)), lax.axis_index("gy"), 0, keepdims=False
    )

    spectrum = jax.ShapeDtypeStruct((devs, share, 2, tiles, z_local, LANES), jnp.float32)
    volume = jax.ShapeDtypeStruct(measured.shape, jnp.float32)
    line_flops = 3 * z_local * y_local * x_len * x_len

    def first(values):
        return call(first_kernel, (values, xa), spectrum, line_flops, "first")

    def ratio(got, values):
        return call(ratio_kernel, (got, values, xb, xa), spectrum, 2 * line_flops, "ratio")

    def correct(got, values):
        return call(
            correct_kernel, (got, values, xs, xa), (spectrum, volume), 3 * line_flops, "correct"
        )

    def last(got, values):
        return call(last_kernel, (got, values, xs), volume, 2 * line_flops, "last")

    planes = (z_devs, y_devs, *spectrum.shape[1:])
    at_once = KX_AT_ONCE if share % KX_AT_ONCE == 0 else 1

    def filtered(got, gains, adjoint):
        return call(
            functools.partial(gain_kernel, adjoint, at_once),
            (got.reshape(planes), gains.reshape(planes), ya, za, *((zs, ys, edges) if adjoint else (zb, yb))),
            jax.ShapeDtypeStruct(planes, jnp.float32),
            3 * 8 * share * z_len * y_len * (2 * z_len + y_len),
            "adjoint" if adjoint else "blur",
        ).reshape(spectrum.shape)

    def arranged(pick_x):
        return call(
            arrange_kernel, (transfer_real, transfer_imag, pick_x, pick_y),
            jax.ShapeDtypeStruct((kx_len, *spectrum.shape[2:]), jnp.float32),
            3 * 4 * z_local * y_local * kx_len * (y_local + kx_len), "arrange",
        ).reshape(spectrum.shape)

    send = first(measured)
    send, pick_x = lax.optimization_barrier((send, pick_x))
    send = exchange(send)
    gains = exchange(arranged(pick_x))
    estimate = measured
    for iteration in range(ITERS):
        send = ratio(exchange(filtered(send, gains, False)), measured)
        send = exchange(filtered(exchange(send), gains, True))
        if iteration < ITERS - 1:
            send, estimate = correct(send, estimate)
            send = exchange(send)
    return last(send, estimate)


def lines_fit(mesh, shape):
    z_devs, y_devs = mesh.shape["gz"], mesh.shape["gy"]
    z_len, y_len, x_len = shape
    return (
        z_len % LANES == 0
        and z_len // z_devs == SUBLANES
        and y_devs == 2
        and y_len == 4 * LANES
        and x_len % (4 * LANES) == 0
        and x_len // 2 == SUBLANES * z_devs * y_devs
    )


def solution(mesh):
    def run(measured, transfer_real, transfer_imag):
        spec = P("gz", "gy", None)
        fits = lines_fit(mesh, measured.shape)
        return jax.shard_map(
            on_device_lines if fits else on_device_rows,
            mesh=mesh,
            in_specs=(spec, spec, spec),
            out_specs=spec,
            check_vma=False,
        )(measured, transfer_real, transfer_imag)

    return run
```

```python
import functools
import math

import jax
import jax.numpy as jnp
import numpy as np
from jax import lax
from jax.experimental import pallas as pl
from jax.experimental.pallas import tpu as pltpu
from jax.sharding import PartitionSpec as P

ITERS = 2
RADIUS = 4


SIGMA = 1.5
FLOOR = 0.1


def product(form, left, right):
    return jnp.einsum(
        form, left, right, precision=lax.Precision.HIGHEST, preferred_element_type=jnp.float32
    )


def gauss_weights():
    offsets = jnp.arange(-RADIUS, RADIUS + 1).astype(jnp.float32)
    weights = jnp.exp(-offsets * offsets / (2.0 * SIGMA * SIGMA))
    return weights / jnp.sum(weights)


def taps_along(padded, axis, length):
    weights = gauss_weights()
    total = weights[0] * lax.slice_in_dim(padded, 0, length, axis=axis)
    for offset in range(1, 2 * RADIUS + 1):
        total = total + weights[offset] * lax.slice_in_dim(
            padded, offset, offset + length, axis=axis
        )
    return total


def blur_local(values, axis):
    length = values.shape[axis]
    widths = [(0, 0)] * values.ndim
    widths[axis] = (RADIUS, RADIUS)
    return taps_along(jnp.pad(values, widths), axis, length)


def angles(length, count):
    position = jnp.arange(length, dtype=jnp.int32)
    frequency = jnp.arange(count, dtype=jnp.int32)
    phase = position[:, None] * frequency[None, :] % length
    return phase.astype(jnp.float32) * (2.0 * math.pi / length)


def square_tables(length):
    angle = angles(length, length)
    cosine = jnp.cos(angle)
    sine = jnp.sin(angle)
    return ((cosine, sine), (cosine / length, sine / length))


def half_tables(length):
    half = length // 2
    angle = angles(length, half)
    cosine = jnp.cos(angle)
    sine = jnp.sin(angle)
    ahead = jnp.stack((cosine, -sine), axis=1)
    weight = jnp.where(jnp.arange(half) == 0, 1.0, 2.0).astype(jnp.float32) / length
    behind = jnp.stack((weight[:, None] * cosine.T, -weight[:, None] * sine.T), axis=0)
    return (ahead, behind)


def shaped(table, shape):
    return (table[0].reshape(shape), table[1].reshape(shape))


def turn(form, values, table, forward):
    first = product(form, values, table[0])
    second = product(form, values, table[1])
    if forward:
        return jnp.stack(
            (first[..., 0, :] + second[..., 1, :], first[..., 1, :] - second[..., 0, :]), axis=-2
        )
    return jnp.stack(
        (first[..., 0, :] - second[..., 1, :], first[..., 1, :] + second[..., 0, :]), axis=-2
    )


def across_z(values):
    return lax.all_to_all(values, "gz", split_axis=0, concat_axis=0, tiled=True)


def across_y(values):
    return lax.all_to_all(values, "gy", split_axis=0, concat_axis=0, tiled=True)


def forward_zfirst(field, ahead, y_fwd, z_fwd):
    z_local, y_local, x_len = field.shape
    z_devs = lax.axis_size("gz")
    y_devs = lax.axis_size("gy")
    x_share = ahead.shape[2] // z_devs
    z_len = z_local * z_devs
    y_len = y_local * y_devs
    z_share = z_len // y_devs
    values = product("zyx,xrgq->gzyrq", field, ahead.reshape(x_len, 2, z_devs, x_share))
    values = across_z(values).reshape(z_len, y_local, 2, x_share)
    values = turn("zyrq,zgk->gykrq", values, shaped(z_fwd, (z_len, y_devs, z_share)), True)
    values = across_y(values).reshape(y_len, z_share, 2, x_share)
    return turn("yjrq,yk->kjrq", values, y_fwd, True)


def inverse_zfirst(spectrum, behind, y_back, z_back, z_local, y_local):
    z_devs = lax.axis_size("gz")
    y_devs = lax.axis_size("gy")
    y_len, z_share, pair, x_share = spectrum.shape
    x_len = behind.shape[2]
    values = turn("kjrq,kgy->gyjrq", spectrum, shaped(y_back, (y_len, y_devs, y_local)), False)
    values = across_y(values)
    values = turn(
        "syjrq,sjgz->gzyrq", values, shaped(z_back, (y_devs, z_share, z_devs, z_local)), False
    )
    values = across_z(values)
    return product("szyrq,rsqx->zyx", values, behind.reshape(2, z_devs, x_share, x_len))


def gains_zfirst(transfer_real, transfer_imag):
    z_local, y_local, half = transfer_real.shape
    z_devs = lax.axis_size("gz")
    y_devs = lax.axis_size("gy")
    x_share = half // z_devs
    z_len = z_local * z_devs
    z_share = z_len // y_devs
    stacked = (
        jnp.stack((transfer_real, transfer_imag), axis=2)
        .reshape(z_local, y_local, 2, z_devs, x_share)
        .transpose(3, 0, 1, 2, 4)
    )
    stacked = (
        across_z(stacked).reshape(y_devs, z_share, y_local, 2, x_share).transpose(0, 2, 1, 3, 4)
    )
    return across_y(stacked).reshape(y_local * y_devs, z_share, 2, x_share)


def apply_gains(spectrum, gains, conjugate):
    spec_real = spectrum[..., 0, :]
    spec_imag = spectrum[..., 1, :]
    gain_real = gains[..., 0, :]
    gain_imag = gains[..., 1, :]
    if conjugate:
        return jnp.stack(
            (
                spec_real * gain_real + spec_imag * gain_imag,
                spec_imag * gain_real - spec_real * gain_imag,
            ),
            axis=-2,
        )
    return jnp.stack(
        (
            spec_real * gain_real - spec_imag * gain_imag,
            spec_real * gain_imag + spec_imag * gain_real,
        ),
        axis=-2,
    )


def on_device_rows(measured, transfer_real, transfer_imag):
    z_local, y_local, x_len = measured.shape
    z_len = z_local * lax.axis_size("gz")
    y_len = y_local * lax.axis_size("gy")
    ahead, behind = half_tables(x_len)
    y_fwd, y_back = square_tables(y_len)
    z_fwd, z_back = square_tables(z_len)
    soft_x = blur_local(behind, 2)
    soft_y = (blur_local(y_back[0], 1), blur_local(y_back[1], 1))
    soft_z = (blur_local(z_back[0], 1), blur_local(z_back[1], 1))
    gains = gains_zfirst(transfer_real, transfer_imag)
    estimate = measured
    for iteration in range(ITERS):
        spectrum = forward_zfirst(estimate, ahead, y_fwd, z_fwd)
        blurred = inverse_zfirst(
            apply_gains(spectrum, gains, False), behind, y_back, z_back, z_local, y_local
        )
        ratio = measured / jnp.maximum(blurred, FLOOR)
        spectrum = forward_zfirst(ratio, ahead, y_fwd, z_fwd)
        correction = inverse_zfirst(
            apply_gains(spectrum, gains, True), soft_x, soft_y, soft_z, z_local, y_local
        )
        estimate = estimate * correction
    return estimate


LANES = 128
SUBLANES = 8


def gauss_weights_np():
    offsets = np.arange(-RADIUS, RADIUS + 1).astype(np.float64)
    weights = np.exp(-offsets * offsets / (2.0 * SIGMA * SIGMA))
    return weights / weights.sum()


def smooth_np(table, axis):
    weights = gauss_weights_np()
    widths = [(0, 0)] * table.ndim
    widths[axis] = (RADIUS, RADIUS)
    padded = np.pad(table, widths)
    length = table.shape[axis]
    return sum(
        weights[j] * np.take(padded, np.arange(j, j + length), axis=axis)
        for j in range(2 * RADIUS + 1)
    )


def two_terms(table):
    high = table.astype(np.float32).astype(jnp.bfloat16)
    low = (table - high.astype(np.float64)).astype(np.float32).astype(jnp.bfloat16)
    return np.stack((high, low))


def phase_np(first, second, length):
    return 2.0 * np.pi * ((first[:, None] * second[None, :]) % length) / length


def x_tables(length):
    half = length // 2
    where = np.arange(length)
    ahead, behind = [], []
    for odd in range(2):
        k = 2 * np.arange(half // 2) + odd
        angle = phase_np(k, where, length)
        ahead.append(np.concatenate((np.cos(angle), -np.sin(angle)), axis=0)[:, :half])
        weight = (np.where(k == 0, 1.0, 2.0) / length)[:, None]
        behind.append(np.concatenate((weight * np.cos(angle), -weight * np.sin(angle)), axis=0))
    sharp = np.stack([table[:, :half] for table in behind])
    soft = smooth_np(np.concatenate(behind, axis=0), 1)
    return two_terms(np.stack(ahead)), two_terms(sharp), two_terms(soft)


def y_order(length, rest):
    quarter = length // 4
    return 4 * ((np.arange(quarter) + (rest % 2) * (quarter // 2)) % quarter) + rest


def y_tables(length):
    quarter = length // 4
    where = np.arange(length)
    ahead, sharp, soft, edges = [], [], [], []
    weights = gauss_weights_np()
    for rest in range(4):
        angle = phase_np(where, y_order(length, rest), length)
        cosine, sine = np.cos(angle), np.sin(angle)
        ahead.append(np.concatenate((cosine[:quarter], sine[:quarter]), axis=1))
        exact, round_trip, edge = [], [], []
        for table in (cosine.T / length, sine.T / length):
            around = sum(
                weights[j] * np.roll(table, RADIUS - j, axis=1) for j in range(2 * RADIUS + 1)
            )
            over = around - smooth_np(table, 1)
            exact.append(table[:, :quarter])
            round_trip.append(around[:, :quarter])
            edge += [over[:, : quarter // 2], over[:, -(quarter // 2) :]]
        sharp.append(np.concatenate(exact, axis=1))
        soft.append(np.concatenate(round_trip, axis=1))
        edges.append(np.concatenate(edge, axis=1))
    return [two_terms(np.stack(t)) for t in (ahead, sharp, soft)] + [
        two_terms(np.concatenate(edges))
    ]


def z_tables(length):
    where = np.arange(length)
    angle = phase_np(where, where, length)
    cosine, sine = np.cos(angle), np.sin(angle)
    ahead = np.block([[cosine, sine], [-sine, cosine]])
    cosine, sine = cosine / length, sine / length
    sharp = np.block([[cosine, -sine], [sine, cosine]])
    cosine, sine = smooth_np(cosine, 0), smooth_np(sine, 0)
    soft = np.block([[cosine, -sine], [sine, cosine]])
    return two_terms(ahead), two_terms(sharp), two_terms(soft)


def pick_of(order):
    return np.eye(len(order), dtype=np.float32)[:, np.asarray(order)].astype(jnp.bfloat16)


def pick_x_table(length):
    return pick_of(np.concatenate((np.arange(0, length, 2), np.arange(1, length, 2))))


def pick_y_tables(length):
    by_rest = [np.arange(rest, length, 4) for rest in range(4)]
    orders = ((0, 1, 2, 3), (1, 0, 3, 2))
    return np.stack([pick_of(np.concatenate([by_rest[r] for r in order])) for order in orders])


def dot(left, right):
    return jnp.dot(left, right, preferred_element_type=jnp.float32)


def split_terms(values):
    high = values.astype(jnp.bfloat16)
    return high, (values - high.astype(jnp.float32)).astype(jnp.bfloat16)


def table_times(high, low, values):
    first, second = split_terms(values)
    return dot(
        jnp.concatenate((high, high, low), axis=1), jnp.concatenate((first, second, first), axis=0)
    )


def times_table(values, high, low):
    first, second = split_terms(values)
    return dot(
        jnp.concatenate((first, second, first), axis=1), jnp.concatenate((high, high, low), axis=0)
    )


def table_times_lines(high, low, values):
    first, second = split_terms(values)
    return lax.dot_general(
        jnp.concatenate((high, high, low), axis=1),
        jnp.concatenate((first, second, first), axis=1),
        (((1,), (1,)), ((), ())),
        preferred_element_type=jnp.float32,
    )


def lines_of(values, high, low):
    return times_table(values.T, high, low)


def swapped(blocks):
    row = lax.broadcasted_iota(jnp.int32, blocks[0].shape, 1)
    blocks = list(blocks)
    for step in (1, 2, 4):
        upper = (row & step) == 0
        for i in range(SUBLANES):
            if i & step == 0:
                a, b = blocks[i], blocks[i + step]
                blocks[i] = jnp.where(upper, a, pltpu.roll(b, step, 1))
                blocks[i + step] = jnp.where(upper, pltpu.roll(a, SUBLANES - step, 1), b)
    return blocks


def load_lines(got_ref, tile):
    half = got_ref.shape[0] * got_ref.shape[1] // 2
    parts = []
    for part in range(2):
        blocks = swapped([got_ref[:, i, part, tile] for i in range(SUBLANES)])
        parts.append(jnp.concatenate([b.reshape(-1, LANES) for b in blocks], axis=1))
    return [
        jnp.concatenate([p[odd * half : (odd + 1) * half] for p in parts], axis=0)
        for odd in range(2)
    ]


def store_lines(send_ref, tile, parities):
    devs = send_ref.shape[0]
    half = devs * send_ref.shape[1] // 2
    for part in range(2):
        values = jnp.concatenate([p[part * half : (part + 1) * half] for p in parities], axis=0)
        blocks = [
            values[:, z * LANES : (z + 1) * LANES].reshape(devs, SUBLANES, LANES)
            for z in range(SUBLANES)
        ]
        for i, block in enumerate(swapped(blocks)):
            send_ref[:, i, part, tile] = block


def lines_back_sharp(got_ref, tile, x_ref):
    even, odd = load_lines(got_ref, tile)
    even = lines_of(even, x_ref[0, 0], x_ref[1, 0])
    odd = lines_of(odd, x_ref[0, 1], x_ref[1, 1])
    return even + odd, even - odd


def lines_back_soft(got_ref, tile, x_ref):
    both = lines_of(jnp.concatenate(load_lines(got_ref, tile), axis=0), x_ref[0], x_ref[1])
    half = both.shape[1] // 2
    return both[:, :half], both[:, half:]


def lines_ahead(left, right, send_ref, tile, x_ref):
    even = table_times_lines(x_ref[0, 0], x_ref[1, 0], left + right)
    odd = table_times_lines(x_ref[0, 1], x_ref[1, 1], left - right)
    store_lines(send_ref, tile, (even, odd))


def halves(volume_ref, tile):
    half = volume_ref.shape[2] // 2
    rows = pl.ds(pl.multiple_of(tile * LANES, LANES), LANES)
    return (
        volume_ref[:, rows, :half].reshape(-1, half),
        volume_ref[:, rows, half:].reshape(-1, half),
    )


def store_halves(volume_ref, tile, left, right):
    half = volume_ref.shape[2] // 2
    rows = pl.ds(pl.multiple_of(tile * LANES, LANES), LANES)
    shape = (volume_ref.shape[0], LANES, half)
    volume_ref[:, rows, :half] = left.reshape(shape)
    volume_ref[:, rows, half:] = right.reshape(shape)


def first_kernel(volume_ref, xa_ref, send_ref):
    @pl.loop(0, send_ref.shape[3])
    def _(tile):
        left, right = halves(volume_ref, tile)
        lines_ahead(left, right, send_ref, tile, xa_ref)


def ratio_kernel(got_ref, measured_ref, xb_ref, xa_ref, send_ref):
    @pl.loop(0, got_ref.shape[3])
    def _(tile):
        left, right = lines_back_sharp(got_ref, tile, xb_ref)
        over_left, over_right = halves(measured_ref, tile)
        left = over_left / jnp.maximum(left, FLOOR)
        right = over_right / jnp.maximum(right, FLOOR)
        lines_ahead(left, right, send_ref, tile, xa_ref)


def correct_kernel(got_ref, estimate_ref, xb_ref, xa_ref, send_ref, out_ref):
    @pl.loop(0, got_ref.shape[3])
    def _(tile):
        left, right = lines_back_soft(got_ref, tile, xb_ref)
        old_left, old_right = halves(estimate_ref, tile)
        left, right = old_left * left, old_right * right
        store_halves(out_ref, tile, left, right)
        lines_ahead(left, right, send_ref, tile, xa_ref)


def last_kernel(got_ref, estimate_ref, xb_ref, out_ref):
    @pl.loop(0, got_ref.shape[3])
    def _(tile):
        left, right = lines_back_soft(got_ref, tile, xb_ref)
        old_left, old_right = halves(estimate_ref, tile)
        store_halves(out_ref, tile, old_left * left, old_right * right)


def picked(values, pick):
    first, second = split_terms(values)
    rest = values - first.astype(jnp.float32) - second.astype(jnp.float32)
    return dot(first, pick) + dot(second, pick) + dot(rest.astype(jnp.bfloat16), pick)


def arrange_kernel(real_ref, imag_ref, pick_x_ref, pick_y_ref, send_ref):
    z_len, _, kx_len = real_ref.shape
    tiles = send_ref.shape[2]
    flat = send_ref.reshape(kx_len * 2 * tiles * z_len, LANES)

    @pl.loop(0, z_len)
    def _(z):
        for part, ref in enumerate((real_ref, imag_ref)):
            values = picked(picked(ref[z], pick_x_ref[...]).T, pick_y_ref[...])
            for tile in range(tiles):
                start = (part * tiles + tile) * z_len + z
                flat[pl.ds(start, kx_len, 2 * tiles * z_len), :] = values[
                    :, tile * LANES : (tile + 1) * LANES
                ]


def turned_ahead(both):
    rows, half = both.shape[0] // 2, both.shape[1] // 2
    return (
        both[:rows, :half] + both[rows:, half:],
        both[rows:, :half] - both[:rows, half:],
    )


def turned_back(both):
    rows, half = both.shape[0] // 2, both.shape[1] // 2
    return (
        both[:rows, :half] - both[rows:, half:],
        both[rows:, :half] + both[:rows, half:],
    )


def gain_kernel(adjoint, at_once, got_ref, *refs):
    @pl.loop(0, got_ref.shape[2] // at_once)
    def _(step):
        gain_planes(adjoint, at_once, step * at_once, got_ref, *refs)


def quarters_of(ref, k, part):
    _, y_devs, _, _, tiles, _, _ = ref.shape
    return [ref[:, g, k, part, t].reshape(-1, LANES) for g in range(y_devs) for t in range(tiles)]


def gains_of(ref, k, part):
    first, second, third, fourth = quarters_of(ref, k, part)
    low = lax.broadcasted_iota(jnp.int32, first.shape, 1) < LANES // 2
    pairs = ((first, third), (third, first), (second, fourth), (fourth, second))
    return jnp.concatenate([jnp.where(low, a, b) for a, b in pairs], axis=1)


def gain_planes(
    adjoint, share, base, got_ref, gain_ref, ya_ref, za_ref, zb_ref, yb_ref, *rest_refs
):
    send_ref = rest_refs[-1]
    z_devs, y_devs, _, _, tiles, z_local, _ = got_ref.shape
    z_len = z_devs * z_local
    rows = 2 * z_len

    def by_kx(values):
        return [values[k * rows : (k + 1) * rows] for k in range(share)]

    inputs = [[], [], [], []]
    for k in range(share):
        real, imag = (quarters_of(got_ref, base + k, part) for part in range(2))
        even_real, even_imag = real[0] + real[2], imag[0] + imag[2]
        odd_real, odd_imag = real[1] + real[3], imag[1] + imag[3]
        inputs[0] += [even_real + odd_real, even_imag + odd_imag]
        inputs[2] += [even_real - odd_real, even_imag - odd_imag]
        even_real, even_imag = real[0] - real[2], imag[0] - imag[2]
        odd_real, odd_imag = real[1] - real[3], imag[1] - imag[3]
        inputs[1] += [even_real + odd_imag, even_imag - odd_real]
        inputs[3] += [even_real - odd_imag, even_imag + odd_real]
    turned = [
        by_kx(times_table(jnp.concatenate(inputs[r], axis=0), ya_ref[0, r], ya_ref[1, r]))
        for r in range(4)
    ]
    planes = []
    for k in range(share):
        pairs = [turned_ahead(turned[r][k]) for r in range(4)]
        values = jnp.concatenate(
            [jnp.concatenate([pair[part] for pair in pairs], axis=1) for part in range(2)], axis=0
        )
        values = table_times(za_ref[0], za_ref[1], values)
        real, imag = values[:z_len], values[z_len:]
        gain_real, gain_imag = (gains_of(gain_ref, base + k, part) for part in range(2))
        if adjoint:
            both = (real * gain_real + imag * gain_imag, imag * gain_real - real * gain_imag)
        else:
            both = (real * gain_real - imag * gain_imag, real * gain_imag + imag * gain_real)
        planes.append(table_times(zb_ref[0], zb_ref[1], jnp.concatenate(both, axis=0)))
    values = jnp.concatenate(planes, axis=0)
    turned = [
        by_kx(times_table(values[:, r * LANES : (r + 1) * LANES], yb_ref[0, r], yb_ref[1, r]))
        for r in range(4)
    ]
    if adjoint:
        edge_ref = rest_refs[0]
        edges = by_kx(times_table(values, edge_ref[0], edge_ref[1]))
    for k in range(share):
        pairs = [turned_back(turned[r][k]) for r in range(4)]
        even_real, even_imag = (pairs[0][part] + pairs[2][part] for part in range(2))
        odd_real, odd_imag = (pairs[1][part] + pairs[3][part] for part in range(2))
        outs = [None] * 4
        outs[0] = [even_real + odd_real, even_imag + odd_imag]
        outs[2] = [even_real - odd_real, even_imag - odd_imag]
        even_real, even_imag = (pairs[0][part] - pairs[2][part] for part in range(2))
        odd_real, odd_imag = (pairs[1][part] - pairs[3][part] for part in range(2))
        outs[1] = [even_real - odd_imag, even_imag + odd_real]
        outs[3] = [even_real + odd_imag, even_imag - odd_real]
        if adjoint:
            over = turned_back(edges[k])
            low = lax.broadcasted_iota(jnp.int32, over[0].shape, 1) < LANES // 2
            for part in range(2):
                outs[0][part] = outs[0][part] - jnp.where(low, over[part], 0.0)
                outs[3][part] = outs[3][part] - jnp.where(low, 0.0, over[part])
        for part in range(2):
            for j in range(4):
                send_ref[:, j // tiles, base + k, part, j % tiles] = outs[j][part].reshape(
                    z_devs, z_local, LANES
                )


KX_AT_ONCE = 4
VMEM_BYTES = 32 * 2**20


def call(kernel, arrays, outs, flops, name):
    leaves = (*arrays, *jax.tree.leaves(outs))
    moved = sum(math.prod(a.shape) * a.dtype.itemsize for a in leaves)
    spec = pl.BlockSpec(memory_space=pltpu.VMEM)
    return pl.pallas_call(
        kernel,
        in_specs=[spec] * len(arrays),
        out_specs=jax.tree.map(lambda _: spec, outs),
        out_shape=outs,
        compiler_params=pltpu.CompilerParams(vmem_limit_bytes=VMEM_BYTES),
        cost_estimate=pl.CostEstimate(flops=flops, bytes_accessed=moved, transcendentals=0),
        name=name,
    )(*arrays)


def exchange(values):
    return lax.all_to_all(values, ("gz", "gy"), split_axis=0, concat_axis=0, tiled=True)


def on_device_lines(measured, transfer_real, transfer_imag):
    z_devs, y_devs = lax.axis_size("gz"), lax.axis_size("gy")
    devs = z_devs * y_devs
    z_local, y_local, x_len = measured.shape
    z_len, y_len, kx_len = z_local * z_devs, y_local * y_devs, x_len // 2
    tiles, share = y_local // LANES, kx_len // devs
    xa, xb, xs = (jnp.asarray(t) for t in x_tables(x_len))
    ya, yb, ys, edges = (jnp.asarray(t) for t in y_tables(y_len))
    za, zb, zs = (jnp.asarray(t) for t in z_tables(z_len))
    pick_x = jnp.asarray(pick_x_table(kx_len))
    pick_y = lax.dynamic_index_in_dim(
        jnp.asarray(pick_y_tables(y_local)), lax.axis_index("gy"), 0, keepdims=False
    )

    spectrum = jax.ShapeDtypeStruct((devs, share, 2, tiles, z_local, LANES), jnp.float32)
    volume = jax.ShapeDtypeStruct(measured.shape, jnp.float32)
    line_flops = 3 * z_local * y_local * x_len * x_len

    def first(values):
        return call(first_kernel, (values, xa), spectrum, line_flops, "first")

    def ratio(got, values):
        return call(ratio_kernel, (got, values, xb, xa), spectrum, 2 * line_flops, "ratio")

    def correct(got, values):
        return call(
            correct_kernel, (got, values, xs, xa), (spectrum, volume), 3 * line_flops, "correct"
        )

    def last(got, values):
        return call(last_kernel, (got, values, xs), volume, 2 * line_flops, "last")

    planes = (z_devs, y_devs, *spectrum.shape[1:])
    at_once = KX_AT_ONCE if share % KX_AT_ONCE == 0 else 1

    def filtered(got, gains, adjoint):
        return call(
            functools.partial(gain_kernel, adjoint, at_once),
            (got.reshape(planes), gains.reshape(planes), ya, za, *((zs, ys, edges) if adjoint else (zb, yb))),
            jax.ShapeDtypeStruct(planes, jnp.float32),
            3 * 8 * share * z_len * y_len * (2 * z_len + y_len),
            "adjoint" if adjoint else "blur",
        ).reshape(spectrum.shape)

    def arranged(pick_x):
        return call(
            arrange_kernel, (transfer_real, transfer_imag, pick_x, pick_y),
            jax.ShapeDtypeStruct((kx_len, *spectrum.shape[2:]), jnp.float32),
            3 * 4 * z_local * y_local * kx_len * (y_local + kx_len), "arrange",
        ).reshape(spectrum.shape)

    send = first(measured)
    send, pick_x = lax.optimization_barrier((send, pick_x))
    send = exchange(send)
    gains = exchange(arranged(pick_x))
    estimate = measured
    for iteration in range(ITERS):
        send = ratio(exchange(filtered(send, gains, False)), measured)
        send = exchange(filtered(exchange(send), gains, True))
        if iteration < ITERS - 1:
            send, estimate = correct(send, estimate)
            send = exchange(send)
    return last(send, estimate)


def lines_fit(mesh, shape):
    z_devs, y_devs = mesh.shape["gz"], mesh.shape["gy"]
    z_len, y_len, x_len = shape
    return (
        z_len % LANES == 0
        and z_len // z_devs == SUBLANES
        and y_devs == 2
        and y_len == 4 * LANES
        and x_len % (4 * LANES) == 0
        and x_len // 2 == SUBLANES * z_devs * y_devs
    )


def solution(mesh):
    def run(measured, transfer_real, transfer_imag):
        spec = P("gz", "gy", None)
        fits = lines_fit(mesh, measured.shape)
        return jax.shard_map(
            on_device_lines if fits else on_device_rows,
            mesh=mesh,
            in_specs=(spec, spec, spec),
            out_specs=spec,
            check_vma=False,
        )(measured, transfer_real, transfer_imag)

    return run
```

```python
import functools
import math

import jax
import jax.numpy as jnp
import numpy as np
from jax import lax
from jax.experimental import pallas as pl
from jax.experimental.pallas import tpu as pltpu
from jax.sharding import PartitionSpec as P

ITERS = 2
RADIUS = 4


SIGMA = 1.5
FLOOR = 0.1


def product(form, left, right):
    return jnp.einsum(
        form, left, right, precision=lax.Precision.HIGHEST, preferred_element_type=jnp.float32
    )


def gauss_weights():
    offsets = jnp.arange(-RADIUS, RADIUS + 1).astype(jnp.float32)
    weights = jnp.exp(-offsets * offsets / (2.0 * SIGMA * SIGMA))
    return weights / jnp.sum(weights)


def taps_along(padded, axis, length):
    weights = gauss_weights()
    total = weights[0] * lax.slice_in_dim(padded, 0, length, axis=axis)
    for offset in range(1, 2 * RADIUS + 1):
        total = total + weights[offset] * lax.slice_in_dim(
            padded, offset, offset + length, axis=axis
        )
    return total


def blur_local(values, axis):
    length = values.shape[axis]
    widths = [(0, 0)] * values.ndim
    widths[axis] = (RADIUS, RADIUS)
    return taps_along(jnp.pad(values, widths), axis, length)


def angles(length, count):
    position = jnp.arange(length, dtype=jnp.int32)
    frequency = jnp.arange(count, dtype=jnp.int32)
    phase = position[:, None] * frequency[None, :] % length
    return phase.astype(jnp.float32) * (2.0 * math.pi / length)


def square_tables(length):
    angle = angles(length, length)
    cosine = jnp.cos(angle)
    sine = jnp.sin(angle)
    return ((cosine, sine), (cosine / length, sine / length))


def half_tables(length):
    half = length // 2
    angle = angles(length, half)
    cosine = jnp.cos(angle)
    sine = jnp.sin(angle)
    ahead = jnp.stack((cosine, -sine), axis=1)
    weight = jnp.where(jnp.arange(half) == 0, 1.0, 2.0).astype(jnp.float32) / length
    behind = jnp.stack((weight[:, None] * cosine.T, -weight[:, None] * sine.T), axis=0)
    return (ahead, behind)


def shaped(table, shape):
    return (table[0].reshape(shape), table[1].reshape(shape))


def turn(form, values, table, forward):
    first = product(form, values, table[0])
    second = product(form, values, table[1])
    if forward:
        return jnp.stack(
            (first[..., 0, :] + second[..., 1, :], first[..., 1, :] - second[..., 0, :]), axis=-2
        )
    return jnp.stack(
        (first[..., 0, :] - second[..., 1, :], first[..., 1, :] + second[..., 0, :]), axis=-2
    )


def across_z(values):
    return lax.all_to_all(values, "gz", split_axis=0, concat_axis=0, tiled=True)


def across_y(values):
    return lax.all_to_all(values, "gy", split_axis=0, concat_axis=0, tiled=True)


def forward_zfirst(field, ahead, y_fwd, z_fwd):
    z_local, y_local, x_len = field.shape
    z_devs = lax.axis_size("gz")
    y_devs = lax.axis_size("gy")
    x_share = ahead.shape[2] // z_devs
    z_len = z_local * z_devs
    y_len = y_local * y_devs
    z_share = z_len // y_devs
    values = product("zyx,xrgq->gzyrq", field, ahead.reshape(x_len, 2, z_devs, x_share))
    values = across_z(values).reshape(z_len, y_local, 2, x_share)
    values = turn("zyrq,zgk->gykrq", values, shaped(z_fwd, (z_len, y_devs, z_share)), True)
    values = across_y(values).reshape(y_len, z_share, 2, x_share)
    return turn("yjrq,yk->kjrq", values, y_fwd, True)


def inverse_zfirst(spectrum, behind, y_back, z_back, z_local, y_local):
    z_devs = lax.axis_size("gz")
    y_devs = lax.axis_size("gy")
    y_len, z_share, pair, x_share = spectrum.shape
    x_len = behind.shape[2]
    values = turn("kjrq,kgy->gyjrq", spectrum, shaped(y_back, (y_len, y_devs, y_local)), False)
    values = across_y(values)
    values = turn(
        "syjrq,sjgz->gzyrq", values, shaped(z_back, (y_devs, z_share, z_devs, z_local)), False
    )
    values = across_z(values)
    return product("szyrq,rsqx->zyx", values, behind.reshape(2, z_devs, x_share, x_len))


def gains_zfirst(transfer_real, transfer_imag):
    z_local, y_local, half = transfer_real.shape
    z_devs = lax.axis_size("gz")
    y_devs = lax.axis_size("gy")
    x_share = half // z_devs
    z_len = z_local * z_devs
    z_share = z_len // y_devs
    stacked = (
        jnp.stack((transfer_real, transfer_imag), axis=2)
        .reshape(z_local, y_local, 2, z_devs, x_share)
        .transpose(3, 0, 1, 2, 4)
    )
    stacked = (
        across_z(stacked).reshape(y_devs, z_share, y_local, 2, x_share).transpose(0, 2, 1, 3, 4)
    )
    return across_y(stacked).reshape(y_local * y_devs, z_share, 2, x_share)


def apply_gains(spectrum, gains, conjugate):
    spec_real = spectrum[..., 0, :]
    spec_imag = spectrum[..., 1, :]
    gain_real = gains[..., 0, :]
    gain_imag = gains[..., 1, :]
    if conjugate:
        return jnp.stack(
            (
                spec_real * gain_real + spec_imag * gain_imag,
                spec_imag * gain_real - spec_real * gain_imag,
            ),
            axis=-2,
        )
    return jnp.stack(
        (
            spec_real * gain_real - spec_imag * gain_imag,
            spec_real * gain_imag + spec_imag * gain_real,
        ),
        axis=-2,
    )


def on_device_rows(measured, transfer_real, transfer_imag):
    z_local, y_local, x_len = measured.shape
    z_len = z_local * lax.axis_size("gz")
    y_len = y_local * lax.axis_size("gy")
    ahead, behind = half_tables(x_len)
    y_fwd, y_back = square_tables(y_len)
    z_fwd, z_back = square_tables(z_len)
    soft_x = blur_local(behind, 2)
    soft_y = (blur_local(y_back[0], 1), blur_local(y_back[1], 1))
    soft_z = (blur_local(z_back[0], 1), blur_local(z_back[1], 1))
    gains = gains_zfirst(transfer_real, transfer_imag)
    estimate = measured
    for iteration in range(ITERS):
        spectrum = forward_zfirst(estimate, ahead, y_fwd, z_fwd)
        blurred = inverse_zfirst(
            apply_gains(spectrum, gains, False), behind, y_back, z_back, z_local, y_local
        )
        ratio = measured / jnp.maximum(blurred, FLOOR)
        spectrum = forward_zfirst(ratio, ahead, y_fwd, z_fwd)
        correction = inverse_zfirst(
            apply_gains(spectrum, gains, True), soft_x, soft_y, soft_z, z_local, y_local
        )
        estimate = estimate * correction
    return estimate


LANES = 128
SUBLANES = 8


def gauss_weights_np():
    offsets = np.arange(-RADIUS, RADIUS + 1).astype(np.float64)
    weights = np.exp(-offsets * offsets / (2.0 * SIGMA * SIGMA))
    return weights / weights.sum()


def smooth_np(table, axis):
    weights = gauss_weights_np()
    widths = [(0, 0)] * table.ndim
    widths[axis] = (RADIUS, RADIUS)
    padded = np.pad(table, widths)
    length = table.shape[axis]
    return sum(
        weights[j] * np.take(padded, np.arange(j, j + length), axis=axis)
        for j in range(2 * RADIUS + 1)
    )


def two_terms(table):
    high = table.astype(np.float32).astype(jnp.bfloat16)
    low = (table - high.astype(np.float64)).astype(np.float32).astype(jnp.bfloat16)
    return np.stack((high, low))


def phase_np(first, second, length):
    return 2.0 * np.pi * ((first[:, None] * second[None, :]) % length) / length


def x_tables(length):
    half = length // 2
    where = np.arange(length)
    ahead, behind = [], []
    for odd in range(2):
        k = 2 * np.arange(half // 2) + odd
        angle = phase_np(k, where, length)
        ahead.append(np.concatenate((np.cos(angle), -np.sin(angle)), axis=0)[:, :half])
        weight = (np.where(k == 0, 1.0, 2.0) / length)[:, None]
        behind.append(np.concatenate((weight * np.cos(angle), -weight * np.sin(angle)), axis=0))
    sharp = np.stack([table[:, :half] for table in behind])
    soft = smooth_np(np.concatenate(behind, axis=0), 1)
    return two_terms(np.stack(ahead)), two_terms(sharp), two_terms(soft)


def y_order(length, rest):
    quarter = length // 4
    return 4 * ((np.arange(quarter) + (rest % 2) * (quarter // 2)) % quarter) + rest


def y_tables(length):
    quarter = length // 4
    where = np.arange(length)
    ahead, sharp, soft, edges = [], [], [], []
    weights = gauss_weights_np()
    for rest in range(4):
        angle = phase_np(where, y_order(length, rest), length)
        cosine, sine = np.cos(angle), np.sin(angle)
        ahead.append(np.concatenate((cosine[:quarter], sine[:quarter]), axis=1))
        exact, round_trip, edge = [], [], []
        for table in (cosine.T / length, sine.T / length):
            around = sum(
                weights[j] * np.roll(table, RADIUS - j, axis=1) for j in range(2 * RADIUS + 1)
            )
            over = around - smooth_np(table, 1)
            exact.append(table[:, :quarter])
            round_trip.append(around[:, :quarter])
            edge += [over[:, : quarter // 2], over[:, -(quarter // 2) :]]
        sharp.append(np.concatenate(exact, axis=1))
        soft.append(np.concatenate(round_trip, axis=1))
        edges.append(np.concatenate(edge, axis=1))
    return [two_terms(np.stack(t)) for t in (ahead, sharp, soft)] + [
        two_terms(np.concatenate(edges))
    ]


def z_tables(length):
    where = np.arange(length)
    angle = phase_np(where, where, length)
    cosine, sine = np.cos(angle), np.sin(angle)
    ahead = np.block([[cosine, sine], [-sine, cosine]])
    cosine, sine = cosine / length, sine / length
    sharp = np.block([[cosine, -sine], [sine, cosine]])
    cosine, sine = smooth_np(cosine, 0), smooth_np(sine, 0)
    soft = np.block([[cosine, -sine], [sine, cosine]])
    return two_terms(ahead), two_terms(sharp), two_terms(soft)


def pick_of(order):
    return np.eye(len(order), dtype=np.float32)[:, np.asarray(order)].astype(jnp.bfloat16)


def pick_x_table(length):
    return pick_of(np.concatenate((np.arange(0, length, 2), np.arange(1, length, 2))))


def pick_y_tables(length):
    by_rest = [np.arange(rest, length, 4) for rest in range(4)]
    orders = ((0, 1, 2, 3), (1, 0, 3, 2))
    return np.stack([pick_of(np.concatenate([by_rest[r] for r in order])) for order in orders])


def dot(left, right):
    return jnp.dot(left, right, preferred_element_type=jnp.float32)


def split_terms(values):
    high = values.astype(jnp.bfloat16)
    return high, (values - high.astype(jnp.float32)).astype(jnp.bfloat16)


def table_times(high, low, values):
    first, second = split_terms(values)
    return dot(
        jnp.concatenate((high, high, low), axis=1), jnp.concatenate((first, second, first), axis=0)
    )


def times_table(values, high, low):
    first, second = split_terms(values)
    return dot(
        jnp.concatenate((first, second, first), axis=1), jnp.concatenate((high, high, low), axis=0)
    )


def table_times_lines(high, low, values):
    first, second = split_terms(values)
    return lax.dot_general(
        jnp.concatenate((high, high, low), axis=1),
        jnp.concatenate((first, second, first), axis=1),
        (((1,), (1,)), ((), ())),
        preferred_element_type=jnp.float32,
    )


def lines_of(values, high, low):
    return times_table(values.T, high, low)


def swapped(blocks):
    row = lax.broadcasted_iota(jnp.int32, blocks[0].shape, 1)
    blocks = list(blocks)
    for step in (1, 2, 4):
        upper = (row & step) == 0
        for i in range(SUBLANES):
            if i & step == 0:
                a, b = blocks[i], blocks[i + step]
                blocks[i] = jnp.where(upper, a, pltpu.roll(b, step, 1))
                blocks[i + step] = jnp.where(upper, pltpu.roll(a, SUBLANES - step, 1), b)
    return blocks


def load_lines(got_ref, tile):
    half = got_ref.shape[0] * got_ref.shape[1] // 2
    parts = []
    for part in range(2):
        blocks = swapped([got_ref[:, i, part, tile] for i in range(SUBLANES)])
        parts.append(jnp.concatenate([b.reshape(-1, LANES) for b in blocks], axis=1))
    return [
        jnp.concatenate([p[odd * half : (odd + 1) * half] for p in parts], axis=0)
        for odd in range(2)
    ]


def store_lines(send_ref, tile, parities):
    devs = send_ref.shape[0]
    half = devs * send_ref.shape[1] // 2
    for part in range(2):
        values = jnp.concatenate([p[part * half : (part + 1) * half] for p in parities], axis=0)
        blocks = [
            values[:, z * LANES : (z + 1) * LANES].reshape(devs, SUBLANES, LANES)
            for z in range(SUBLANES)
        ]
        for i, block in enumerate(swapped(blocks)):
            send_ref[:, i, part, tile] = block


def lines_back_sharp(got_ref, tile, x_ref):
    even, odd = load_lines(got_ref, tile)
    even = lines_of(even, x_ref[0, 0], x_ref[1, 0])
    odd = lines_of(odd, x_ref[0, 1], x_ref[1, 1])
    return even + odd, even - odd


def lines_back_soft(got_ref, tile, x_ref):
    both = lines_of(jnp.concatenate(load_lines(got_ref, tile), axis=0), x_ref[0], x_ref[1])
    half = both.shape[1] // 2
    return both[:, :half], both[:, half:]


def lines_ahead(left, right, send_ref, tile, x_ref):
    even = table_times_lines(x_ref[0, 0], x_ref[1, 0], left + right)
    odd = table_times_lines(x_ref[0, 1], x_ref[1, 1], left - right)
    store_lines(send_ref, tile, (even, odd))


def halves(volume_ref, tile):
    half = volume_ref.shape[2] // 2
    rows = pl.ds(pl.multiple_of(tile * LANES, LANES), LANES)
    return (
        volume_ref[:, rows, :half].reshape(-1, half),
        volume_ref[:, rows, half:].reshape(-1, half),
    )


def store_halves(volume_ref, tile, left, right):
    half = volume_ref.shape[2] // 2
    rows = pl.ds(pl.multiple_of(tile * LANES, LANES), LANES)
    shape = (volume_ref.shape[0], LANES, half)
    volume_ref[:, rows, :half] = left.reshape(shape)
    volume_ref[:, rows, half:] = right.reshape(shape)


def first_kernel(volume_ref, xa_ref, send_ref, volume_buf, send_buf, in_sems, out_sems):
    tiles = send_ref.shape[3]

    def copy_in(tile):
        rows = pl.ds(pl.multiple_of(tile * LANES, LANES), LANES)
        return pltpu.make_async_copy(volume_ref.at[:, rows], volume_buf.at[tile], in_sems.at[tile])

    def copy_out(tile):
        return pltpu.make_async_copy(
            send_buf.at[tile], send_ref.at[:, :, :, pl.ds(tile, 1)], out_sems.at[tile]
        )

    for tile in range(tiles):
        copy_in(tile).start()

    @pl.loop(0, tiles)
    def _(tile):
        copy_in(tile).wait()
        left, right = halves(volume_buf.at[tile], 0)
        lines_ahead(left, right, send_buf.at[tile], 0, xa_ref)
        copy_out(tile).start()

    for tile in range(tiles):
        copy_out(tile).wait()


def ratio_kernel(got_ref, measured_ref, xb_ref, xa_ref, send_ref):
    @pl.loop(0, got_ref.shape[3])
    def _(tile):
        left, right = lines_back_sharp(got_ref, tile, xb_ref)
        over_left, over_right = halves(measured_ref, tile)
        left = over_left / jnp.maximum(left, FLOOR)
        right = over_right / jnp.maximum(right, FLOOR)
        lines_ahead(left, right, send_ref, tile, xa_ref)


def correct_kernel(got_ref, estimate_ref, xb_ref, xa_ref, send_ref, out_ref):
    @pl.loop(0, got_ref.shape[3])
    def _(tile):
        left, right = lines_back_soft(got_ref, tile, xb_ref)
        old_left, old_right = halves(estimate_ref, tile)
        left, right = old_left * left, old_right * right
        store_halves(out_ref, tile, left, right)
        lines_ahead(left, right, send_ref, tile, xa_ref)


def last_kernel(got_ref, estimate_ref, xb_ref, out_ref, out_buf, out_sems):
    tiles = got_ref.shape[3]

    def copy_out(tile):
        rows = pl.ds(pl.multiple_of(tile * LANES, LANES), LANES)
        return pltpu.make_async_copy(out_buf.at[tile], out_ref.at[:, rows], out_sems.at[tile])

    @pl.loop(0, tiles)
    def _(tile):
        left, right = lines_back_soft(got_ref, tile, xb_ref)
        old_left, old_right = halves(estimate_ref, tile)
        store_halves(out_buf.at[tile], 0, old_left * left, old_right * right)
        copy_out(tile).start()

    for tile in range(tiles):
        copy_out(tile).wait()


def picked(values, pick):
    first, second = split_terms(values)
    return dot(
        jnp.concatenate((first, second), axis=1), jnp.concatenate((pick, pick), axis=0)
    )


def arrange_kernel(real_ref, imag_ref, pick_x_ref, pick_y_ref, send_ref):
    devs, _, _, tiles, z_len, _ = send_ref.shape

    @pl.loop(0, 2)
    def _(part):
        planes = []
        for z in range(z_len):
            values = jnp.where(part == 0, real_ref[z], imag_ref[z])
            planes.append(picked(picked(values, pick_x_ref[...]).T, pick_y_ref[...]))
        for tile in range(tiles):
            blocks = [
                plane[:, tile * LANES : (tile + 1) * LANES].reshape(devs, SUBLANES, LANES)
                for plane in planes
            ]
            for i, block in enumerate(swapped(blocks)):
                send_ref[:, i, part, tile] = block


def turned_ahead(both):
    rows, half = both.shape[0] // 2, both.shape[1] // 2
    return (
        both[:rows, :half] + both[rows:, half:],
        both[rows:, :half] - both[:rows, half:],
    )


def turned_back(both):
    rows, half = both.shape[0] // 2, both.shape[1] // 2
    return (
        both[:rows, :half] - both[rows:, half:],
        both[rows:, :half] + both[:rows, half:],
    )


def gain_kernel(adjoint, at_once, got_ref, *refs):
    @pl.loop(0, got_ref.shape[2] // at_once)
    def _(step):
        gain_planes(adjoint, at_once, step * at_once, got_ref, *refs)


def quarters_of(ref, k, part):
    _, y_devs, _, _, tiles, _, _ = ref.shape
    return [ref[:, g, k, part, t].reshape(-1, LANES) for g in range(y_devs) for t in range(tiles)]


def gains_of(ref, k, part):
    first, second, third, fourth = quarters_of(ref, k, part)
    low = lax.broadcasted_iota(jnp.int32, first.shape, 1) < LANES // 2
    pairs = ((first, third), (third, first), (second, fourth), (fourth, second))
    return jnp.concatenate([jnp.where(low, a, b) for a, b in pairs], axis=1)


def gain_planes(
    adjoint, share, base, got_ref, gain_ref, ya_ref, za_ref, zb_ref, yb_ref, *rest_refs
):
    send_ref = rest_refs[-1]
    z_devs, y_devs, _, _, tiles, z_local, _ = got_ref.shape
    z_len = z_devs * z_local
    rows = 2 * z_len

    def by_kx(values):
        return [values[k * rows : (k + 1) * rows] for k in range(share)]

    inputs = [[], [], [], []]
    for k in range(share):
        real, imag = (quarters_of(got_ref, base + k, part) for part in range(2))
        even_real, even_imag = real[0] + real[2], imag[0] + imag[2]
        odd_real, odd_imag = real[1] + real[3], imag[1] + imag[3]
        inputs[0] += [even_real + odd_real, even_imag + odd_imag]
        inputs[2] += [even_real - odd_real, even_imag - odd_imag]
        even_real, even_imag = real[0] - real[2], imag[0] - imag[2]
        odd_real, odd_imag = real[1] - real[3], imag[1] - imag[3]
        inputs[1] += [even_real + odd_imag, even_imag - odd_real]
        inputs[3] += [even_real - odd_imag, even_imag + odd_real]
    turned = [
        by_kx(times_table(jnp.concatenate(inputs[r], axis=0), ya_ref[0, r], ya_ref[1, r]))
        for r in range(4)
    ]
    planes = []
    for k in range(share):
        pairs = [turned_ahead(turned[r][k]) for r in range(4)]
        values = jnp.concatenate(
            [jnp.concatenate([pair[part] for pair in pairs], axis=1) for part in range(2)], axis=0
        )
        values = table_times(za_ref[0], za_ref[1], values)
        real, imag = values[:z_len], values[z_len:]
        gain_real, gain_imag = (gains_of(gain_ref, base + k, part) for part in range(2))
        if adjoint:
            both = (real * gain_real + imag * gain_imag, imag * gain_real - real * gain_imag)
        else:
            both = (real * gain_real - imag * gain_imag, real * gain_imag + imag * gain_real)
        planes.append(table_times(zb_ref[0], zb_ref[1], jnp.concatenate(both, axis=0)))
    values = jnp.concatenate(planes, axis=0)
    turned = [
        by_kx(times_table(values[:, r * LANES : (r + 1) * LANES], yb_ref[0, r], yb_ref[1, r]))
        for r in range(4)
    ]
    if adjoint:
        edge_ref = rest_refs[0]
        edges = by_kx(times_table(values, edge_ref[0], edge_ref[1]))
    for k in range(share):
        pairs = [turned_back(turned[r][k]) for r in range(4)]
        even_real, even_imag = (pairs[0][part] + pairs[2][part] for part in range(2))
        odd_real, odd_imag = (pairs[1][part] + pairs[3][part] for part in range(2))
        outs = [None] * 4
        outs[0] = [even_real + odd_real, even_imag + odd_imag]
        outs[2] = [even_real - odd_real, even_imag - odd_imag]
        even_real, even_imag = (pairs[0][part] - pairs[2][part] for part in range(2))
        odd_real, odd_imag = (pairs[1][part] - pairs[3][part] for part in range(2))
        outs[1] = [even_real - odd_imag, even_imag + odd_real]
        outs[3] = [even_real + odd_imag, even_imag - odd_real]
        if adjoint:
            over = turned_back(edges[k])
            low = lax.broadcasted_iota(jnp.int32, over[0].shape, 1) < LANES // 2
            for part in range(2):
                outs[0][part] = outs[0][part] - jnp.where(low, over[part], 0.0)
                outs[3][part] = outs[3][part] - jnp.where(low, 0.0, over[part])
        for part in range(2):
            for j in range(4):
                send_ref[:, j // tiles, base + k, part, j % tiles] = outs[j][part].reshape(
                    z_devs, z_local, LANES
                )


KX_AT_ONCE = 4
VMEM_BYTES = 32 * 2**20
ALL_VMEM_BYTES = 59 * 2**20


def call(kernel, arrays, outs, flops, name, specs=(), out_spec=None, scratch=(), vmem=None):
    leaves = (*arrays, *jax.tree.leaves(outs))
    moved = sum(math.prod(a.shape) * a.dtype.itemsize for a in leaves)
    spec = pl.BlockSpec(memory_space=pltpu.VMEM)
    return pl.pallas_call(
        kernel,
        in_specs=[*specs, *[spec] * (len(arrays) - len(specs))],
        out_specs=out_spec or jax.tree.map(lambda _: spec, outs),
        out_shape=outs,
        scratch_shapes=scratch,
        compiler_params=pltpu.CompilerParams(vmem_limit_bytes=vmem or VMEM_BYTES),
        cost_estimate=pl.CostEstimate(flops=flops, bytes_accessed=moved, transcendentals=0),
        name=name,
    )(*arrays)


def exchange(values):
    return lax.all_to_all(values, ("gz", "gy"), split_axis=0, concat_axis=0, tiled=True)


def on_device_lines(measured, transfer_real, transfer_imag):
    z_devs, y_devs = lax.axis_size("gz"), lax.axis_size("gy")
    devs = z_devs * y_devs
    z_local, y_local, x_len = measured.shape
    z_len, y_len, kx_len = z_local * z_devs, y_local * y_devs, x_len // 2
    tiles, share = y_local // LANES, kx_len // devs
    xa, xb, xs = (jnp.asarray(t) for t in x_tables(x_len))
    ya, yb, ys, edges = (jnp.asarray(t) for t in y_tables(y_len))
    za, zb, zs = (jnp.asarray(t) for t in z_tables(z_len))
    pick_x = jnp.asarray(pick_x_table(kx_len))
    pick_y = lax.dynamic_index_in_dim(
        jnp.asarray(pick_y_tables(y_local)), lax.axis_index("gy"), 0, keepdims=False
    )

    spectrum = jax.ShapeDtypeStruct((devs, share, 2, tiles, z_local, LANES), jnp.float32)
    volume = jax.ShapeDtypeStruct(measured.shape, jnp.float32)
    far = pl.BlockSpec(memory_space=pltpu.HBM)
    sems = pltpu.SemaphoreType.DMA((tiles,))
    volume_tiles = pltpu.VMEM((tiles, z_local, LANES, x_len), jnp.float32)
    spectrum_tiles = pltpu.VMEM((tiles, devs, share, 2, 1, z_local, LANES), jnp.float32)
    line_flops = 3 * z_local * y_local * x_len * x_len

    def first(values):
        return call(
            first_kernel, (values, xa), spectrum, line_flops, "first", (far,), far,
            (volume_tiles, spectrum_tiles, sems, sems), ALL_VMEM_BYTES,
        )

    def ratio(got, values):
        return call(ratio_kernel, (got, values, xb, xa), spectrum, 2 * line_flops, "ratio")

    def correct(got, values):
        return call(
            correct_kernel, (got, values, xs, xa), (spectrum, volume), 3 * line_flops, "correct"
        )

    def last(got, values):
        return call(
            last_kernel, (got, values, xs), volume, 2 * line_flops, "last", (), far,
            (volume_tiles, sems),
        )

    planes = (z_devs, y_devs, *spectrum.shape[1:])
    at_once = KX_AT_ONCE if share % KX_AT_ONCE == 0 else 1

    def filtered(got, gains, adjoint):
        return call(
            functools.partial(gain_kernel, adjoint, at_once),
            (got.reshape(planes), gains.reshape(planes), ya, za, *((zs, ys, edges) if adjoint else (zb, yb))),
            jax.ShapeDtypeStruct(planes, jnp.float32),
            3 * 8 * share * z_len * y_len * (2 * z_len + y_len),
            "adjoint" if adjoint else "blur",
        ).reshape(spectrum.shape)

    def arranged(pick_x):
        return call(
            arrange_kernel, (transfer_real, transfer_imag, pick_x, pick_y),
            spectrum,
            3 * 4 * z_local * y_local * kx_len * (y_local + kx_len), "arrange",
        )

    send = first(measured)
    send, pick_x = lax.optimization_barrier((send, pick_x))
    send = exchange(send)
    gains = exchange(arranged(pick_x))
    estimate = measured
    for iteration in range(ITERS):
        send = ratio(exchange(filtered(send, gains, False)), measured)
        send = exchange(filtered(exchange(send), gains, True))
        if iteration < ITERS - 1:
            send, estimate = correct(send, estimate)
            send = exchange(send)
    return last(send, estimate)


def lines_fit(mesh, shape):
    z_devs, y_devs = mesh.shape["gz"], mesh.shape["gy"]
    z_len, y_len, x_len = shape
    return (
        z_len % LANES == 0
        and z_len // z_devs == SUBLANES
        and y_devs == 2
        and y_len == 4 * LANES
        and x_len % (4 * LANES) == 0
        and x_len // 2 == SUBLANES * z_devs * y_devs
    )


def solution(mesh):
    def run(measured, transfer_real, transfer_imag):
        spec = P("gz", "gy", None)
        fits = lines_fit(mesh, measured.shape)
        return jax.shard_map(
            on_device_lines if fits else on_device_rows,
            mesh=mesh,
            in_specs=(spec, spec, spec),
            out_specs=spec,
            check_vma=False,
        )(measured, transfer_real, transfer_imag)

    return run
```

```python
import functools
import math

import jax
import jax.numpy as jnp
import numpy as np
from jax import lax
from jax.experimental import pallas as pl
from jax.experimental.pallas import tpu as pltpu
from jax.sharding import PartitionSpec as P

ITERS = 2
RADIUS = 4


SIGMA = 1.5
FLOOR = 0.1


def product(form, left, right):
    return jnp.einsum(
        form, left, right, precision=lax.Precision.HIGHEST, preferred_element_type=jnp.float32
    )


def gauss_weights():
    offsets = jnp.arange(-RADIUS, RADIUS + 1).astype(jnp.float32)
    weights = jnp.exp(-offsets * offsets / (2.0 * SIGMA * SIGMA))
    return weights / jnp.sum(weights)


def taps_along(padded, axis, length):
    weights = gauss_weights()
    total = weights[0] * lax.slice_in_dim(padded, 0, length, axis=axis)
    for offset in range(1, 2 * RADIUS + 1):
        total = total + weights[offset] * lax.slice_in_dim(
            padded, offset, offset + length, axis=axis
        )
    return total


def blur_local(values, axis):
    length = values.shape[axis]
    widths = [(0, 0)] * values.ndim
    widths[axis] = (RADIUS, RADIUS)
    return taps_along(jnp.pad(values, widths), axis, length)


def angles(length, count):
    position = jnp.arange(length, dtype=jnp.int32)
    frequency = jnp.arange(count, dtype=jnp.int32)
    phase = position[:, None] * frequency[None, :] % length
    return phase.astype(jnp.float32) * (2.0 * math.pi / length)


def square_tables(length):
    angle = angles(length, length)
    cosine = jnp.cos(angle)
    sine = jnp.sin(angle)
    return ((cosine, sine), (cosine / length, sine / length))


def half_tables(length):
    half = length // 2
    angle = angles(length, half)
    cosine = jnp.cos(angle)
    sine = jnp.sin(angle)
    ahead = jnp.stack((cosine, -sine), axis=1)
    weight = jnp.where(jnp.arange(half) == 0, 1.0, 2.0).astype(jnp.float32) / length
    behind = jnp.stack((weight[:, None] * cosine.T, -weight[:, None] * sine.T), axis=0)
    return (ahead, behind)


def shaped(table, shape):
    return (table[0].reshape(shape), table[1].reshape(shape))


def turn(form, values, table, forward):
    first = product(form, values, table[0])
    second = product(form, values, table[1])
    if forward:
        return jnp.stack(
            (first[..., 0, :] + second[..., 1, :], first[..., 1, :] - second[..., 0, :]), axis=-2
        )
    return jnp.stack(
        (first[..., 0, :] - second[..., 1, :], first[..., 1, :] + second[..., 0, :]), axis=-2
    )


def across_z(values):
    return lax.all_to_all(values, "gz", split_axis=0, concat_axis=0, tiled=True)


def across_y(values):
    return lax.all_to_all(values, "gy", split_axis=0, concat_axis=0, tiled=True)


def forward_zfirst(field, ahead, y_fwd, z_fwd):
    z_local, y_local, x_len = field.shape
    z_devs = lax.axis_size("gz")
    y_devs = lax.axis_size("gy")
    x_share = ahead.shape[2] // z_devs
    z_len = z_local * z_devs
    y_len = y_local * y_devs
    z_share = z_len // y_devs
    values = product("zyx,xrgq->gzyrq", field, ahead.reshape(x_len, 2, z_devs, x_share))
    values = across_z(values).reshape(z_len, y_local, 2, x_share)
    values = turn("zyrq,zgk->gykrq", values, shaped(z_fwd, (z_len, y_devs, z_share)), True)
    values = across_y(values).reshape(y_len, z_share, 2, x_share)
    return turn("yjrq,yk->kjrq", values, y_fwd, True)


def inverse_zfirst(spectrum, behind, y_back, z_back, z_local, y_local):
    z_devs = lax.axis_size("gz")
    y_devs = lax.axis_size("gy")
    y_len, z_share, pair, x_share = spectrum.shape
    x_len = behind.shape[2]
    values = turn("kjrq,kgy->gyjrq", spectrum, shaped(y_back, (y_len, y_devs, y_local)), False)
    values = across_y(values)
    values = turn(
        "syjrq,sjgz->gzyrq", values, shaped(z_back, (y_devs, z_share, z_devs, z_local)), False
    )
    values = across_z(values)
    return product("szyrq,rsqx->zyx", values, behind.reshape(2, z_devs, x_share, x_len))


def gains_zfirst(transfer_real, transfer_imag):
    z_local, y_local, half = transfer_real.shape
    z_devs = lax.axis_size("gz")
    y_devs = lax.axis_size("gy")
    x_share = half // z_devs
    z_len = z_local * z_devs
    z_share = z_len // y_devs
    stacked = (
        jnp.stack((transfer_real, transfer_imag), axis=2)
        .reshape(z_local, y_local, 2, z_devs, x_share)
        .transpose(3, 0, 1, 2, 4)
    )
    stacked = (
        across_z(stacked).reshape(y_devs, z_share, y_local, 2, x_share).transpose(0, 2, 1, 3, 4)
    )
    return across_y(stacked).reshape(y_local * y_devs, z_share, 2, x_share)


def apply_gains(spectrum, gains, conjugate):
    spec_real = spectrum[..., 0, :]
    spec_imag = spectrum[..., 1, :]
    gain_real = gains[..., 0, :]
    gain_imag = gains[..., 1, :]
    if conjugate:
        return jnp.stack(
            (
                spec_real * gain_real + spec_imag * gain_imag,
                spec_imag * gain_real - spec_real * gain_imag,
            ),
            axis=-2,
        )
    return jnp.stack(
        (
            spec_real * gain_real - spec_imag * gain_imag,
            spec_real * gain_imag + spec_imag * gain_real,
        ),
        axis=-2,
    )


def on_device_rows(measured, transfer_real, transfer_imag):
    z_local, y_local, x_len = measured.shape
    z_len = z_local * lax.axis_size("gz")
    y_len = y_local * lax.axis_size("gy")
    ahead, behind = half_tables(x_len)
    y_fwd, y_back = square_tables(y_len)
    z_fwd, z_back = square_tables(z_len)
    soft_x = blur_local(behind, 2)
    soft_y = (blur_local(y_back[0], 1), blur_local(y_back[1], 1))
    soft_z = (blur_local(z_back[0], 1), blur_local(z_back[1], 1))
    gains = gains_zfirst(transfer_real, transfer_imag)
    estimate = measured
    for iteration in range(ITERS):
        spectrum = forward_zfirst(estimate, ahead, y_fwd, z_fwd)
        blurred = inverse_zfirst(
            apply_gains(spectrum, gains, False), behind, y_back, z_back, z_local, y_local
        )
        ratio = measured / jnp.maximum(blurred, FLOOR)
        spectrum = forward_zfirst(ratio, ahead, y_fwd, z_fwd)
        correction = inverse_zfirst(
            apply_gains(spectrum, gains, True), soft_x, soft_y, soft_z, z_local, y_local
        )
        estimate = estimate * correction
    return estimate


LANES = 128
SUBLANES = 8


def gauss_weights_np():
    offsets = np.arange(-RADIUS, RADIUS + 1).astype(np.float64)
    weights = np.exp(-offsets * offsets / (2.0 * SIGMA * SIGMA))
    return weights / weights.sum()


def smooth_np(table, axis):
    weights = gauss_weights_np()
    widths = [(0, 0)] * table.ndim
    widths[axis] = (RADIUS, RADIUS)
    padded = np.pad(table, widths)
    length = table.shape[axis]
    return sum(
        weights[j] * np.take(padded, np.arange(j, j + length), axis=axis)
        for j in range(2 * RADIUS + 1)
    )


def two_terms(table):
    high = table.astype(np.float32).astype(jnp.bfloat16)
    low = (table - high.astype(np.float64)).astype(np.float32).astype(jnp.bfloat16)
    return np.stack((high, low))


def phase_np(first, second, length):
    return 2.0 * np.pi * ((first[:, None] * second[None, :]) % length) / length


def x_tables(length):
    half = length // 2
    where = np.arange(length)
    ahead, behind = [], []
    for odd in range(2):
        k = 2 * np.arange(half // 2) + odd
        angle = phase_np(k, where, length)
        ahead.append(np.concatenate((np.cos(angle), -np.sin(angle)), axis=0)[:, :half])
        weight = (np.where(k == 0, 1.0, 2.0) / length)[:, None]
        behind.append(np.concatenate((weight * np.cos(angle), -weight * np.sin(angle)), axis=0))
    sharp = np.stack([table[:, :half] for table in behind])
    soft = smooth_np(np.concatenate(behind, axis=0), 1)
    return two_terms(np.stack(ahead)), two_terms(sharp), two_terms(soft)


def y_order(length, rest):
    quarter = length // 4
    return 4 * ((np.arange(quarter) + (rest % 2) * (quarter // 2)) % quarter) + rest


def y_tables(length):
    quarter = length // 4
    where = np.arange(length)
    ahead, sharp, soft, edges = [], [], [], []
    weights = gauss_weights_np()
    for rest in range(4):
        angle = phase_np(where, y_order(length, rest), length)
        cosine, sine = np.cos(angle), np.sin(angle)
        ahead.append(np.concatenate((cosine[:quarter], sine[:quarter]), axis=1))
        exact, round_trip, edge = [], [], []
        for table in (cosine.T / length, sine.T / length):
            around = sum(
                weights[j] * np.roll(table, RADIUS - j, axis=1) for j in range(2 * RADIUS + 1)
            )
            over = around - smooth_np(table, 1)
            exact.append(table[:, :quarter])
            round_trip.append(around[:, :quarter])
            edge += [over[:, : quarter // 2], over[:, -(quarter // 2) :]]
        sharp.append(np.concatenate(exact, axis=1))
        soft.append(np.concatenate(round_trip, axis=1))
        edges.append(np.concatenate(edge, axis=1))
    return [two_terms(np.stack(t)) for t in (ahead, sharp, soft)] + [
        two_terms(np.concatenate(edges))
    ]


def z_tables(length):
    where = np.arange(length)
    angle = phase_np(where, where, length)
    cosine, sine = np.cos(angle), np.sin(angle)
    ahead = np.block([[cosine, sine], [-sine, cosine]])
    cosine, sine = cosine / length, sine / length
    sharp = np.block([[cosine, -sine], [sine, cosine]])
    cosine, sine = smooth_np(cosine, 0), smooth_np(sine, 0)
    soft = np.block([[cosine, -sine], [sine, cosine]])
    return two_terms(ahead), two_terms(sharp), two_terms(soft)


def pick_of(order):
    return np.eye(len(order), dtype=np.float32)[:, np.asarray(order)].astype(jnp.bfloat16)


def pick_x_table(length):
    return pick_of(np.concatenate((np.arange(0, length, 2), np.arange(1, length, 2))))


def pick_y_tables(length):
    by_rest = [np.arange(rest, length, 4) for rest in range(4)]
    orders = ((0, 1, 2, 3), (1, 0, 3, 2))
    return np.stack([pick_of(np.concatenate([by_rest[r] for r in order])) for order in orders])


def dot(left, right):
    return jnp.dot(left, right, preferred_element_type=jnp.float32)


def split_terms(values):
    high = values.astype(jnp.bfloat16)
    return high, (values - high.astype(jnp.float32)).astype(jnp.bfloat16)


def table_times(high, low, values):
    first, second = split_terms(values)
    return dot(
        jnp.concatenate((high, high, low), axis=1), jnp.concatenate((first, second, first), axis=0)
    )


def times_table(values, high, low):
    first, second = split_terms(values)
    return dot(
        jnp.concatenate((first, second, first), axis=1), jnp.concatenate((high, high, low), axis=0)
    )


def table_times_lines(high, low, values):
    first, second = split_terms(values)
    return lax.dot_general(
        jnp.concatenate((high, high, low), axis=1),
        jnp.concatenate((first, second, first), axis=1),
        (((1,), (1,)), ((), ())),
        preferred_element_type=jnp.float32,
    )


def lines_of(values, high, low):
    return times_table(values.T, high, low)


def swapped(blocks):
    row = lax.broadcasted_iota(jnp.int32, blocks[0].shape, 1)
    blocks = list(blocks)
    for step in (1, 2, 4):
        upper = (row & step) == 0
        for i in range(SUBLANES):
            if i & step == 0:
                a, b = blocks[i], blocks[i + step]
                blocks[i] = jnp.where(upper, a, pltpu.roll(b, step, 1))
                blocks[i + step] = jnp.where(upper, pltpu.roll(a, SUBLANES - step, 1), b)
    return blocks


def load_lines(got_ref, tile):
    half = got_ref.shape[0] * got_ref.shape[1] // 2
    parts = []
    for part in range(2):
        blocks = swapped([got_ref[:, i, part, tile] for i in range(SUBLANES)])
        parts.append(jnp.concatenate([b.reshape(-1, LANES) for b in blocks], axis=1))
    return [
        jnp.concatenate([p[odd * half : (odd + 1) * half] for p in parts], axis=0)
        for odd in range(2)
    ]


def store_lines(send_ref, tile, parities):
    devs = send_ref.shape[0]
    half = devs * send_ref.shape[1] // 2
    for part in range(2):
        values = jnp.concatenate([p[part * half : (part + 1) * half] for p in parities], axis=0)
        blocks = [
            values[:, z * LANES : (z + 1) * LANES].reshape(devs, SUBLANES, LANES)
            for z in range(SUBLANES)
        ]
        for i, block in enumerate(swapped(blocks)):
            send_ref[:, i, part, tile] = block


def lines_back_sharp(got_ref, tile, x_ref):
    even, odd = load_lines(got_ref, tile)
    even = lines_of(even, x_ref[0, 0], x_ref[1, 0])
    odd = lines_of(odd, x_ref[0, 1], x_ref[1, 1])
    return even + odd, even - odd


def lines_back_soft(got_ref, tile, x_ref):
    both = lines_of(jnp.concatenate(load_lines(got_ref, tile), axis=0), x_ref[0], x_ref[1])
    half = both.shape[1] // 2
    return both[:, :half], both[:, half:]


def lines_ahead(left, right, send_ref, tile, x_ref):
    even = table_times_lines(x_ref[0, 0], x_ref[1, 0], left + right)
    odd = table_times_lines(x_ref[0, 1], x_ref[1, 1], left - right)
    store_lines(send_ref, tile, (even, odd))


def halves(volume_ref, tile):
    half = volume_ref.shape[2] // 2
    rows = pl.ds(pl.multiple_of(tile * LANES, LANES), LANES)
    return (
        volume_ref[:, rows, :half].reshape(-1, half),
        volume_ref[:, rows, half:].reshape(-1, half),
    )


def store_halves(volume_ref, tile, left, right):
    half = volume_ref.shape[2] // 2
    rows = pl.ds(pl.multiple_of(tile * LANES, LANES), LANES)
    shape = (volume_ref.shape[0], LANES, half)
    volume_ref[:, rows, :half] = left.reshape(shape)
    volume_ref[:, rows, half:] = right.reshape(shape)


def first_kernel(
    volume_ref, table_ref, send_ref, volume_buf, send_buf, xa_ref, in_sems, out_sems, table_sem
):
    tiles = send_ref.shape[3]
    copy_table = pltpu.make_async_copy(table_ref, xa_ref, table_sem)

    def copy_in(tile):
        rows = pl.ds(pl.multiple_of(tile * LANES, LANES), LANES)
        return pltpu.make_async_copy(volume_ref.at[:, rows], volume_buf.at[tile], in_sems.at[tile])

    def copy_out(tile):
        return pltpu.make_async_copy(
            send_buf.at[tile], send_ref.at[:, :, :, pl.ds(tile, 1)], out_sems.at[tile]
        )

    copy_table.start()
    for tile in range(tiles):
        copy_in(tile).start()
    copy_table.wait()

    @pl.loop(0, tiles)
    def _(tile):
        copy_in(tile).wait()
        left, right = halves(volume_buf.at[tile], 0)
        lines_ahead(left, right, send_buf.at[tile], 0, xa_ref)
        copy_out(tile).start()

    for tile in range(tiles):
        copy_out(tile).wait()


def ratio_kernel(got_ref, measured_ref, xb_ref, xa_ref, send_ref):
    @pl.loop(0, got_ref.shape[3])
    def _(tile):
        left, right = lines_back_sharp(got_ref, tile, xb_ref)
        over_left, over_right = halves(measured_ref, tile)
        left = over_left / jnp.maximum(left, FLOOR)
        right = over_right / jnp.maximum(right, FLOOR)
        lines_ahead(left, right, send_ref, tile, xa_ref)


def correct_kernel(got_ref, estimate_ref, xb_ref, xa_ref, send_ref, out_ref):
    @pl.loop(0, got_ref.shape[3])
    def _(tile):
        left, right = lines_back_soft(got_ref, tile, xb_ref)
        old_left, old_right = halves(estimate_ref, tile)
        left, right = old_left * left, old_right * right
        store_halves(out_ref, tile, left, right)
        lines_ahead(left, right, send_ref, tile, xa_ref)


def last_kernel(got_ref, estimate_ref, xb_ref, out_ref, out_buf, out_sems):
    tiles = got_ref.shape[3]

    def copy_out(tile):
        rows = pl.ds(pl.multiple_of(tile * LANES, LANES), LANES)
        return pltpu.make_async_copy(out_buf.at[tile], out_ref.at[:, rows], out_sems.at[tile])

    @pl.loop(0, tiles)
    def _(tile):
        left, right = lines_back_soft(got_ref, tile, xb_ref)
        old_left, old_right = halves(estimate_ref, tile)
        store_halves(out_buf.at[tile], 0, old_left * left, old_right * right)
        copy_out(tile).start()

    for tile in range(tiles):
        copy_out(tile).wait()


def picked(values, pick):
    first, second = split_terms(values)
    return dot(
        jnp.concatenate((first, second), axis=1), jnp.concatenate((pick, pick), axis=0)
    )


def arrange_kernel(real_ref, imag_ref, pick_x_ref, pick_y_ref, send_ref):
    devs, _, _, tiles, z_len, _ = send_ref.shape

    @pl.loop(0, 2)
    def _(part):
        planes = []
        for z in range(z_len):
            values = jnp.where(part == 0, real_ref[z], imag_ref[z])
            planes.append(picked(picked(values, pick_x_ref[...]).T, pick_y_ref[...]))
        for tile in range(tiles):
            blocks = [
                plane[:, tile * LANES : (tile + 1) * LANES].reshape(devs, SUBLANES, LANES)
                for plane in planes
            ]
            for i, block in enumerate(swapped(blocks)):
                send_ref[:, i, part, tile] = block


def turned_ahead(both):
    rows, half = both.shape[0] // 2, both.shape[1] // 2
    return (
        both[:rows, :half] + both[rows:, half:],
        both[rows:, :half] - both[:rows, half:],
    )


def turned_back(both):
    rows, half = both.shape[0] // 2, both.shape[1] // 2
    return (
        both[:rows, :half] - both[rows:, half:],
        both[rows:, :half] + both[:rows, half:],
    )


def gain_kernel(adjoint, at_once, got_ref, *refs):
    @pl.loop(0, got_ref.shape[2] // at_once)
    def _(step):
        gain_planes(adjoint, at_once, step * at_once, got_ref, *refs)


def quarters_of(ref, k, part):
    _, y_devs, _, _, tiles, _, _ = ref.shape
    return [ref[:, g, k, part, t].reshape(-1, LANES) for g in range(y_devs) for t in range(tiles)]


def gains_of(ref, k, part):
    first, second, third, fourth = quarters_of(ref, k, part)
    low = lax.broadcasted_iota(jnp.int32, first.shape, 1) < LANES // 2
    pairs = ((first, third), (third, first), (second, fourth), (fourth, second))
    return jnp.concatenate([jnp.where(low, a, b) for a, b in pairs], axis=1)


def gain_planes(
    adjoint, share, base, got_ref, gain_ref, ya_ref, za_ref, zb_ref, yb_ref, *rest_refs
):
    send_ref = rest_refs[-1]
    z_devs, y_devs, _, _, tiles, z_local, _ = got_ref.shape
    z_len = z_devs * z_local
    rows = 2 * z_len

    def by_kx(values):
        return [values[k * rows : (k + 1) * rows] for k in range(share)]

    inputs = [[], [], [], []]
    for k in range(share):
        real, imag = (quarters_of(got_ref, base + k, part) for part in range(2))
        even_real, even_imag = real[0] + real[2], imag[0] + imag[2]
        odd_real, odd_imag = real[1] + real[3], imag[1] + imag[3]
        inputs[0] += [even_real + odd_real, even_imag + odd_imag]
        inputs[2] += [even_real - odd_real, even_imag - odd_imag]
        even_real, even_imag = real[0] - real[2], imag[0] - imag[2]
        odd_real, odd_imag = real[1] - real[3], imag[1] - imag[3]
        inputs[1] += [even_real + odd_imag, even_imag - odd_real]
        inputs[3] += [even_real - odd_imag, even_imag + odd_real]
    turned = [
        by_kx(times_table(jnp.concatenate(inputs[r], axis=0), ya_ref[0, r], ya_ref[1, r]))
        for r in range(4)
    ]
    planes = []
    for k in range(share):
        pairs = [turned_ahead(turned[r][k]) for r in range(4)]
        values = jnp.concatenate(
            [jnp.concatenate([pair[part] for pair in pairs], axis=1) for part in range(2)], axis=0
        )
        values = table_times(za_ref[0], za_ref[1], values)
        real, imag = values[:z_len], values[z_len:]
        gain_real, gain_imag = (gains_of(gain_ref, base + k, part) for part in range(2))
        if adjoint:
            both = (real * gain_real + imag * gain_imag, imag * gain_real - real * gain_imag)
        else:
            both = (real * gain_real - imag * gain_imag, real * gain_imag + imag * gain_real)
        planes.append(table_times(zb_ref[0], zb_ref[1], jnp.concatenate(both, axis=0)))
    values = jnp.concatenate(planes, axis=0)
    turned = [
        by_kx(times_table(values[:, r * LANES : (r + 1) * LANES], yb_ref[0, r], yb_ref[1, r]))
        for r in range(4)
    ]
    if adjoint:
        edge_ref = rest_refs[0]
        edges = by_kx(times_table(values, edge_ref[0], edge_ref[1]))
    for k in range(share):
        pairs = [turned_back(turned[r][k]) for r in range(4)]
        even_real, even_imag = (pairs[0][part] + pairs[2][part] for part in range(2))
        odd_real, odd_imag = (pairs[1][part] + pairs[3][part] for part in range(2))
        outs = [None] * 4
        outs[0] = [even_real + odd_real, even_imag + odd_imag]
        outs[2] = [even_real - odd_real, even_imag - odd_imag]
        even_real, even_imag = (pairs[0][part] - pairs[2][part] for part in range(2))
        odd_real, odd_imag = (pairs[1][part] - pairs[3][part] for part in range(2))
        outs[1] = [even_real - odd_imag, even_imag + odd_real]
        outs[3] = [even_real + odd_imag, even_imag - odd_real]
        if adjoint:
            over = turned_back(edges[k])
            low = lax.broadcasted_iota(jnp.int32, over[0].shape, 1) < LANES // 2
            for part in range(2):
                outs[0][part] = outs[0][part] - jnp.where(low, over[part], 0.0)
                outs[3][part] = outs[3][part] - jnp.where(low, 0.0, over[part])
        for part in range(2):
            for j in range(4):
                send_ref[:, j // tiles, base + k, part, j % tiles] = outs[j][part].reshape(
                    z_devs, z_local, LANES
                )


KX_AT_ONCE = 4
VMEM_BYTES = 32 * 2**20
FIRST_VMEM_BYTES = 59 * 2**20


def call(kernel, arrays, outs, flops, name, specs=(), out_spec=None, scratch=(), vmem=None):
    leaves = (*arrays, *jax.tree.leaves(outs))
    moved = sum(math.prod(a.shape) * a.dtype.itemsize for a in leaves)
    spec = pl.BlockSpec(memory_space=pltpu.VMEM)
    return pl.pallas_call(
        kernel,
        in_specs=[*specs, *[spec] * (len(arrays) - len(specs))],
        out_specs=out_spec or jax.tree.map(lambda _: spec, outs),
        out_shape=outs,
        scratch_shapes=scratch,
        compiler_params=pltpu.CompilerParams(vmem_limit_bytes=vmem or VMEM_BYTES),
        cost_estimate=pl.CostEstimate(flops=flops, bytes_accessed=moved, transcendentals=0),
        name=name,
    )(*arrays)


def exchange(values):
    return lax.all_to_all(values, ("gz", "gy"), split_axis=0, concat_axis=0, tiled=True)


def on_device_lines(measured, transfer_real, transfer_imag):
    z_devs, y_devs = lax.axis_size("gz"), lax.axis_size("gy")
    devs = z_devs * y_devs
    z_local, y_local, x_len = measured.shape
    z_len, y_len, kx_len = z_local * z_devs, y_local * y_devs, x_len // 2
    tiles, share = y_local // LANES, kx_len // devs
    xa, xb, xs = (jnp.asarray(t) for t in x_tables(x_len))
    ya, yb, ys, edges = (jnp.asarray(t) for t in y_tables(y_len))
    za, zb, zs = (jnp.asarray(t) for t in z_tables(z_len))
    pick_x = jnp.asarray(pick_x_table(kx_len))
    pick_y = lax.dynamic_index_in_dim(
        jnp.asarray(pick_y_tables(y_local)), lax.axis_index("gy"), 0, keepdims=False
    )

    spectrum = jax.ShapeDtypeStruct((devs, share, 2, tiles, z_local, LANES), jnp.float32)
    volume = jax.ShapeDtypeStruct(measured.shape, jnp.float32)
    far = pl.BlockSpec(memory_space=pltpu.HBM)
    sems = pltpu.SemaphoreType.DMA((tiles,))
    volume_tiles = pltpu.VMEM((tiles, z_local, LANES, x_len), jnp.float32)
    spectrum_tiles = pltpu.VMEM((tiles, devs, share, 2, 1, z_local, LANES), jnp.float32)
    line_flops = 3 * z_local * y_local * x_len * x_len

    def first(values):
        return call(
            first_kernel, (values, xa), spectrum, line_flops, "first", (far, far), far,
            (
                volume_tiles, spectrum_tiles, pltpu.VMEM(xa.shape, xa.dtype), sems, sems,
                pltpu.SemaphoreType.DMA,
            ),
            FIRST_VMEM_BYTES,
        )

    def ratio(got, values):
        return call(ratio_kernel, (got, values, xb, xa), spectrum, 2 * line_flops, "ratio")

    def correct(got, values):
        return call(
            correct_kernel, (got, values, xs, xa), (spectrum, volume), 3 * line_flops, "correct"
        )

    def last(got, values):
        return call(
            last_kernel, (got, values, xs), volume, 2 * line_flops, "last", (), far,
            (volume_tiles, sems),
        )

    planes = (z_devs, y_devs, *spectrum.shape[1:])
    at_once = KX_AT_ONCE if share % KX_AT_ONCE == 0 else 1

    def filtered(got, gains, adjoint):
        return call(
            functools.partial(gain_kernel, adjoint, at_once),
            (got.reshape(planes), gains.reshape(planes), ya, za, *((zs, ys, edges) if adjoint else (zb, yb))),
            jax.ShapeDtypeStruct(planes, jnp.float32),
            3 * 8 * share * z_len * y_len * (2 * z_len + y_len),
            "adjoint" if adjoint else "blur",
        ).reshape(spectrum.shape)

    def arranged(pick_x):
        return call(
            arrange_kernel, (transfer_real, transfer_imag, pick_x, pick_y),
            spectrum,
            3 * 4 * z_local * y_local * kx_len * (y_local + kx_len), "arrange",
        )

    send = first(measured)
    send, pick_x = lax.optimization_barrier((send, pick_x))
    send = exchange(send)
    gains = exchange(arranged(pick_x))
    estimate = measured
    for iteration in range(ITERS):
        send = ratio(exchange(filtered(send, gains, False)), measured)
        send = exchange(filtered(exchange(send), gains, True))
        if iteration < ITERS - 1:
            send, estimate = correct(send, estimate)
            send = exchange(send)
    return last(send, estimate)


def lines_fit(mesh, shape):
    z_devs, y_devs = mesh.shape["gz"], mesh.shape["gy"]
    z_len, y_len, x_len = shape
    return (
        z_len % LANES == 0
        and z_len // z_devs == SUBLANES
        and y_devs == 2
        and y_len == 4 * LANES
        and x_len % (4 * LANES) == 0
        and x_len // 2 == SUBLANES * z_devs * y_devs
    )


def solution(mesh):
    def run(measured, transfer_real, transfer_imag):
        spec = P("gz", "gy", None)
        fits = lines_fit(mesh, measured.shape)
        return jax.shard_map(
            on_device_lines if fits else on_device_rows,
            mesh=mesh,
            in_specs=(spec, spec, spec),
            out_specs=spec,
            check_vma=False,
        )(measured, transfer_real, transfer_imag)

    return run
```
